32 devices in a mesh: grid: 8 (over z, y), sub: 4 (over x, core).
Axes of the slice: x: 2, y: 2, z: 4, core: 2. Of those that a mesh axis runs over, the one named last changes fastest.
Arguments:
- field: float32 [5, 256, 32, 128], P(None, ('grid', 'sub')), may hold values from -6 to 6
- node_jitter: float32 [3, 256, 32, 128], P(None, ('grid', 'sub')), may hold values from -0.15 to 0.15
- time_ratio: float32 [256, 32, 128], P(('grid', 'sub')), may hold values from 0.2 to 5
- donor_cell: int32 [32, 8, 2, 128], P(('grid', 'sub')), may hold values from 0 to 32638, as said below
- receptor_offset: float32 [32, 8, 2, 3, 128], P(('grid', 'sub')), may hold values from 0.1 to 0.9
- receptor_node: int32 [32, 8, 2, 128], P(('grid', 'sub')), may hold values from 4096 to 28671, as said below
- point_count: int32 [32, 8], P(('grid', 'sub')), may hold values from 1 to 256, as said below
Outputs:
- relaxed: float32 [5, 256, 32, 128], P(None, ('grid', 'sub'))
The draws below stay inside these ranges and needn't reach their ends.
Inputs may be any that keep to these rules, and one draw needn't show every extreme that they name: `donor_cell`: a cell i * 32 * 128 + j * 128 + k with i < 8, j < 31, k < 127. `receptor_node`: distinct over all slots of one source block, on local planes 1 to 6. `point_count`: from every block of grid g, owner (g + 1) mod 8 receives exactly 256 points, owner (g + 2) mod 8 receives one point, and every other owner at most 128.
All inputs are finite; a program needn't handle non-finite values.
Results may differ from the reference program's by a relative error of at most 0.0003.
Values sent between devices are 32-bit elements; how exact they have to be, the bound alone decides.
No kernel may reach another device: no remote copies, remote signals or barrier semaphores. Data moves between devices by JAX's collectives and lax.ppermute only.
A program may use at most 128 MiB of HBM per device.

```python
import math
import jax
import jax.numpy as jnp
from jax import lax

NV = 5
PTS = 128
CX = 8
CY = 32
CZ = 128
SLOTS = 2
OWNERS = 8
SUBS = 4
SOURCES = 32
PLANES = 256


def draw_donor_cell(key, part):
    key_plane, key_row, key_col, key_low, key_high = jax.random.split(key, 5)
    shape_all = (SOURCES, OWNERS, SLOTS, PTS)
    plane_id = jax.random.randint(key_plane, shape_all, 0, CX)
    row_id = jax.random.randint(key_row, shape_all, 0, CY - 1)
    col_id = jax.random.randint(key_col, shape_all, 0, CZ - 1)
    cells = (plane_id * CY * CZ + row_id * CZ + col_id).astype(jnp.int32).reshape(-1)
    total = SOURCES * OWNERS * SLOTS * PTS
    half = total // 2
    low_place = jax.random.randint(key_low, (), 0, half)
    high_place = jax.random.randint(key_high, (), half, total)
    top_cell = (CX - 1) * CY * CZ + (CY - 2) * CZ + CZ - 2
    cells = cells.at[low_place].set(0)
    cells = cells.at[high_place].set(top_cell)
    return cells.reshape(shape_all).astype(jnp.int32)


def draw_receptor_node(key, part):
    source_keys = jax.random.split(key, SOURCES)
    interior = (CX - 2) * CY * CZ
    needed = OWNERS * SLOTS * PTS

    def one_source(source_key):
        return jax.random.permutation(source_key, interior)[:needed]
    chosen = jax.vmap(one_source)(source_keys) + CY * CZ
    return chosen.reshape(SOURCES, OWNERS, SLOTS, PTS).astype(jnp.int32)


def draw_point_count(key, part):
    key_level, key_base = jax.random.split(key, 2)
    level = jax.random.randint(key_level, (OWNERS,), 1, 5)
    base = jax.random.randint(key_base, (SOURCES, OWNERS), PTS // 8, PTS // 4 + 1)
    counts = jnp.clip(base * level[None, :], 1, PTS)
    grid_of = jnp.arange(SOURCES, dtype=jnp.int32)[:, None] // SUBS
    owner_ids = jnp.arange(OWNERS, dtype=jnp.int32)[None, :]
    heavy = owner_ids == (grid_of + 1) % OWNERS
    single = owner_ids == (grid_of + 2) % OWNERS
    counts = jnp.where(single, 1, counts)
    counts = jnp.where(heavy, SLOTS * PTS, counts)
    return counts.astype(jnp.int32)


def block_levels(rng, dims, pieces, smallest, top_value):
    level = 1.0
    for dim, parts in pieces:
        heights = jax.random.uniform(jax.random.fold_in(jax.random.fold_in(rng, 6), dim), (parts,), jnp.float32, smallest / len(pieces), top_value / len(pieces))
        level = level * jnp.repeat(jnp.exp(heights), dims[dim] // parts).reshape((-1,) + (1,) * (len(dims) - 1 - dim))
    return level


def centred(rng, dims, scale, bound, cuts=(), kind=jnp.bfloat16):
    values = jax.random.normal(rng, dims, jnp.float32) * scale
    if len(cuts) > 0:
        values = block_levels(rng, dims, cuts, -0.22, 0.18) * values
    return jnp.clip(values, min=-bound, max=bound).astype(kind)


def setup_inputs(seed: int = 0) -> dict:
    key_of = jax.random.split(jax.random.key(seed), 8)
    field = centred(key_of[0], (NV, PLANES, CY, CZ), 1.0, 6.0, ((1, 32),), jnp.float32)
    node_jitter = jnp.clip(jax.random.uniform(key_of[1], (3, PLANES, CY, CZ), jnp.float32, -0.15, 0.15) * block_levels(key_of[1], (3, PLANES, CY, CZ), ((1, 32),), -0.4, 0.0), -0.15, 0.15)
    time_ratio = jnp.clip(jnp.exp(math.log(5.0) - 3.218876 * jax.random.uniform(key_of[2], (PLANES, CY, CZ), jnp.float32) ** block_levels(key_of[2], (PLANES, CY, CZ), ((0, 32),), -0.2, 0.2)), 0.2, 5.0)
    donor_cell = draw_donor_cell(jax.random.fold_in(key_of[7], 71), 0)
    receptor_offset = jnp.clip(0.1 + 0.79999997 * jax.random.uniform(key_of[4], (SOURCES, OWNERS, SLOTS, 3, PTS), jnp.float32) ** block_levels(key_of[4], (SOURCES, OWNERS, SLOTS, 3, PTS), ((0, 32),), -0.2, 0.2), 0.1, 0.9)
    receptor_node = draw_receptor_node(jax.random.fold_in(key_of[7], 71), 0)
    point_count = draw_point_count(jax.random.fold_in(key_of[7], 71), 0)
    return {"field": field, "node_jitter": node_jitter, "time_ratio": time_ratio, "donor_cell": donor_cell, "receptor_offset": receptor_offset, "receptor_node": receptor_node, "point_count": point_count}


def corner_bits(corner):
    return (corner >> 2) & 1, (corner >> 1) & 1, corner & 1


def shape_values(param):
    result = []
    for corner in range(8):
        offset_bits = corner_bits(corner)
        factors = [param[axis_id] if offset_bits[axis_id] else 1.0 - param[axis_id] for axis_id in range(3)]
        derivs = [1.0 if offset_bits[axis_id] else -1.0 for axis_id in range(3)]
        weight = factors[0] * factors[1] * factors[2]
        slopes = [derivs[0] * factors[1] * factors[2], factors[0] * derivs[1] * factors[2], factors[0] * factors[1] * derivs[2]]
        result.append((weight, slopes))
    return result


def determinant(matrix):
    return (matrix[0][0] * (matrix[1][1] * matrix[2][2] - matrix[1][2] * matrix[2][1])
            - matrix[0][1] * (matrix[1][0] * matrix[2][2] - matrix[1][2] * matrix[2][0])
            + matrix[0][2] * (matrix[1][0] * matrix[2][1] - matrix[1][1] * matrix[2][0]))


def solve_point(corners, offsets):
    target = [offsets[..., component, :] for component in range(3)]
    places = [[corners[corner, component] + float(corner_bits(corner)[component]) for component in range(3)] for corner in range(8)]
    param = [jnp.full(target[0].shape, 0.5, target[0].dtype) for component in range(3)]
    for newton_step in range(4):
        shapes = shape_values(param)
        misfit = []
        jacobian = []
        for component in range(3):
            position = shapes[0][0] * places[0][component]
            for corner in range(1, 8):
                position = position + shapes[corner][0] * places[corner][component]
            misfit.append(position - target[component])
            jac_row = []
            for direction in range(3):
                slope_sum = shapes[0][1][direction] * places[0][component]
                for corner in range(1, 8):
                    slope_sum = slope_sum + shapes[corner][1][direction] * places[corner][component]
                jac_row.append(slope_sum)
            jacobian.append(jac_row)
        jac_det = determinant(jacobian)
        updates = []
        for direction in range(3):
            replaced = [[misfit[component] if column == direction else jacobian[component][column] for column in range(3)] for component in range(3)]
            updates.append(determinant(replaced) / jac_det)
        param = [param[direction] - updates[direction] for direction in range(3)]
    shapes = shape_values(param)
    values = []
    for variable in range(corners.shape[1] - 3):
        blended = shapes[0][0] * corners[0, 3 + variable]
        for corner in range(1, 8):
            blended = blended + shapes[corner][0] * corners[corner, 3 + variable]
        values.append(blended)
    return jnp.stack(values, axis=-2)


def fill_fringe(own, values, nodes, counts):
    width = own.shape[0]
    interp = jnp.moveaxis(values, 2, 0).reshape(width, -1)
    slot_count, point_total = nodes.shape[1], nodes.shape[2]
    position = jnp.arange(slot_count, dtype=jnp.int32)[:, None] * point_total + jnp.arange(point_total, dtype=jnp.int32)[None, :]
    live = (position[None] < counts[:, None, None]).reshape(-1)
    flat_nodes = nodes.reshape(-1)
    current = own[:, flat_nodes]
    own = own.at[:, flat_nodes].set(jnp.where(live[None], interp, current))
    flags = jnp.zeros((own.shape[1],), own.dtype).at[flat_nodes].set(live.astype(own.dtype))
    return own, flags


def neighbour_sum(above, below, filled):
    lead = [(0, 0)] * (filled.ndim - 2)
    padded_y = jnp.pad(filled, lead + [(1, 1), (0, 0)])
    padded_z = jnp.pad(filled, lead + [(0, 0), (1, 1)])
    return (above + below + padded_y[..., 2:, :] + padded_y[..., :-2, :]
            + padded_z[..., 2:] + padded_z[..., :-2])


def relax(filled, above, below, ratio, flags):
    smooth = (filled + ratio * neighbour_sum(above, below, filled)) / (1.0 + 6.0 * ratio)
    return jnp.where(flags > 0.5, filled, smooth)


def reference(field, node_jitter, time_ratio, donor_cell, receptor_offset, receptor_node, point_count):
    stacked = jnp.concatenate([node_jitter, field], 0)
    blocks = stacked.reshape(8, OWNERS, SUBS, CX, CY, CZ)
    following = jnp.roll(blocks[:, :, :, :1], -1, axis=2)
    extended = jnp.concatenate([blocks, following], axis=3)
    ext_flat = extended.reshape(8, OWNERS, SUBS, (CX + 1) * CY * CZ)
    own_fields = field.reshape(NV, SOURCES, CX * CY * CZ)
    owner_ids = jnp.arange(OWNERS, dtype=jnp.int32)[:, None, None]

    def one_block(source):
        sub_id = source % SUBS
        donor_data = jnp.take(ext_flat, sub_id, axis=2)
        cells = donor_cell[source]
        picks = []
        for corner in range(8):
            offset_bits = corner_bits(corner)
            shift_amount = offset_bits[0] * CY * CZ + offset_bits[1] * CZ + offset_bits[2]
            picks.append(donor_data[:, owner_ids, cells + shift_amount])
        corners = jnp.stack(picks, 0)
        values = solve_point(corners, receptor_offset[source])
        own = jnp.take(own_fields, source, axis=1)
        return fill_fringe(own, values, receptor_node[source], point_count[source])

    filled, flags = lax.map(one_block, jnp.arange(SOURCES, dtype=jnp.int32))
    filled = jnp.moveaxis(filled, 0, 1).reshape(NV, OWNERS, SUBS * CX, CY, CZ)
    flags = flags.reshape(OWNERS, SUBS * CX, CY, CZ)
    ratio = time_ratio.reshape(OWNERS, SUBS * CX, CY, CZ)
    above = jnp.roll(filled, -1, axis=2)
    below = jnp.roll(filled, 1, axis=2)
    relaxed = relax(filled, above, below, ratio, flags)
    return relaxed.reshape(NV, PLANES, CY, CZ)
```

```python
import functools

import jax
import jax.numpy as jnp
from jax import lax
from jax.experimental import pallas as pl
from jax.experimental.pallas import tpu as pltpu
from jax.sharding import PartitionSpec as P

ROWS = 8
LANES = 128
UNROLL = 8
VMEM = pl.BlockSpec(memory_space=pltpu.VMEM)
SMEM = pl.BlockSpec(memory_space=pltpu.SMEM)
ANY = pl.BlockSpec(memory_space=pl.ANY)
LIMIT = 24 << 20


def passed_along(value, axis, steps):
    count = lax.axis_size(axis)
    pairs = [(source, (source + steps) % count) for source in range(count)]
    return lax.ppermute(value, axis, pairs)


def pack_kernel(count_ref, cell_ref, offset_ref, message_ref):
    owners, points = cell_ref.shape[1], cell_ref.shape[3]

    def one(owner, carry):
        cells = cell_ref[0, owner].astype(jnp.float32)
        count = count_ref[0, owner]
        counts = jnp.full((1, points), count, jnp.int32).astype(jnp.float32)
        message_ref[owner, 0:1, :] = cells[0:1]
        message_ref[owner, 1:4, :] = offset_ref[0, owner, 0]
        message_ref[owner, 4:5, :] = jnp.where(count > points, cells[1:2], counts)
        message_ref[owner, 5:8, :] = offset_ref[0, owner, 1]
        return carry

    lax.fori_loop(0, owners, one, 0, unroll=True)


def coefficients(corner):
    linear = [corner[4] - corner[0], corner[2] - corner[0], corner[1] - corner[0]]
    pair_01 = corner[6] - corner[4] - linear[1]
    pair_02 = corner[5] - corner[4] - linear[2]
    pair_12 = corner[3] - corner[2] - linear[2]
    triple = (corner[7] - corner[6]) - (corner[5] - corner[4]) - pair_12
    return corner[0], linear, pair_01, pair_02, pair_12, triple


def solve(corner, target):
    polys = []
    for component in range(3):
        start, linear, pair_01, pair_02, pair_12, triple = coefficients(
            [corner(q, component) for q in range(8)]
        )
        linear[component] = linear[component] + 1.0
        polys.append((start - target[component], linear, pair_01, pair_02, pair_12, triple))
    s0 = s1 = s2 = jnp.full(target[0].shape, 0.5, jnp.float32)
    for _ in range(4):
        s01, s02, s12 = s0 * s1, s0 * s2, s1 * s2
        misfit, jac = [], []
        for start, (l0, l1, l2), p01, p02, p12, triple in polys:
            d0 = l0 + s1 * p01 + s2 * p02 + s12 * triple
            d1 = l1 + s0 * p01 + s2 * p12 + s02 * triple
            d2 = l2 + s0 * p02 + s1 * p12 + s01 * triple
            misfit.append(start + s0 * d0 + s1 * (l1 + s2 * p12) + s2 * l2)
            jac.append((d0, d1, d2))
        (a0, a1, a2), (b0, b1, b2), (c0, c1, c2) = jac
        m0, m1, m2 = misfit
        bc12 = b1 * c2 - b2 * c1
        bc02 = b0 * c2 - b2 * c0
        bc01 = b0 * c1 - b1 * c0
        det = a0 * bc12 - a1 * bc02 + a2 * bc01
        bm2 = m1 * c2 - b2 * m2
        bm1 = m1 * c1 - b1 * m2
        bm0 = b0 * m2 - m1 * c0
        inverse = 1.0 / det
        u0 = m0 * bc12 - a1 * bm2 + a2 * bm1
        u1 = a0 * bm2 - m0 * bc02 + a2 * bm0
        u2 = a0 * (b1 * m2 - m1 * c1) - a1 * bm0 + m0 * bc01
        s0 = s0 - u0 * inverse
        s1 = s1 - u1 * inverse
        s2 = s2 - u2 * inverse
    values = []
    for variable in range(5):
        u = [corner(q, 3 + variable) for q in range(8)]
        e = [u[q] + s2 * (u[q + 1] - u[q]) for q in (0, 2, 4, 6)]
        f = [e[q] + s1 * (e[q + 1] - e[q]) for q in (0, 2)]
        values.append(f[0] + s0 * (f[1] - f[0]))
    return values


def gather_kernel(
    owners, field_ref, jitter_ref, next_ref, message_ref, message_any, out_ref,
    table, cells, picked, picked_more, sem,
):
    planes, rows_count = field_ref.shape[1], field_ref.shape[2]
    width = 8
    me = lax.axis_index("grid")
    heavy = lax.rem(me + owners - 1, owners)
    copies = [
        pltpu.make_async_copy(message_any.at[:, 4 * slot], cells.at[slot], sem.at[slot])
        for slot in range(2)
    ]
    for copy in copies:
        copy.start()

    blocks = rows_count // ROWS
    for variable in range(width):
        for plane in range(planes + 1):
            for block in range(blocks):
                place = pl.ds(block * ROWS, ROWS)
                if plane == planes:
                    tile = next_ref[variable, 0, place, :]
                elif variable < 3:
                    tile = jitter_ref[variable, plane, place, :]
                else:
                    tile = field_ref[variable - 3, plane, place, :]
                first = (plane * rows_count + block * ROWS) * width + variable
                table[pl.ds(first, ROWS, stride=width), :] = tile
    for copy in copies:
        copy.wait()

    lane = lax.broadcasted_iota(jnp.int32, (ROWS, LANES), 1)
    pair_of = lane >> 1
    even = (lane & 1) == 0
    steps = (0, 1, rows_count, rows_count + 1)

    def pick(slot, source, count):
        def chunk(step, held):
            held = list(held)
            for u in range(UNROLL):
                point = step * UNROLL + u
                cell = cells[slot, source, point].astype(jnp.int32)
                row, column = cell >> 7, cell & 127
                pair = step * (UNROLL // 2) + u // 2
                shift = (2 * pair - column) & 127
                mask = pair_of == pair
                for corner in range(4):
                    first = pl.multiple_of((row + steps[corner]) * width, width)
                    tile = pltpu.roll(table[pl.ds(first, width), :], shift, 1)
                    k = (u & 1) * 4 + corner
                    held[k] = jnp.where(mask, tile, held[k])
            return tuple(held)

        zero = jnp.zeros((width, LANES), jnp.float32)
        return lax.fori_loop(0, (count + UNROLL - 1) // UNROLL, chunk, (zero,) * 8)

    def one_source(source, carry):
        count = cells[1, source, 0].astype(jnp.int32)
        count = jnp.where(source == heavy, LANES, count)
        held = pick(0, source, count)
        for k in range(8):
            picked[pl.ds(k * width * owners + source, width, stride=owners), :] = held[k]
        return carry

    lax.fori_loop(0, owners, one_source, 0)
    held = pick(1, heavy, LANES)
    for k in range(8):
        picked_more[pl.ds(k * width, width), :] = held[k]

    def corner_of(read):
        def corner(q, variable):
            first = read(q >> 1, variable)
            second = read(4 + (q >> 1), variable)
            if q & 1:
                return jnp.where(even, pltpu.roll(first, LANES - 1, 1), second)
            return jnp.where(even, first, pltpu.roll(second, 1, 1))

        return corner

    def one_block(block, carry):
        def read(k, variable):
            first = (k * width + variable) * owners + block * ROWS
            return picked[pl.ds(pl.multiple_of(first, ROWS), ROWS), :]

        first = block * (ROWS * 8)
        target = [message_ref[pl.ds(first + 1 + c, ROWS, stride=8), :] for c in range(3)]
        values = solve(corner_of(read), target)
        for variable in range(5):
            place = pl.ds(block * (ROWS * 16) + variable, ROWS, stride=16)
            out_ref[place, :] = values[variable]
        return carry

    lax.fori_loop(0, owners // ROWS, one_block, 0, unroll=True)

    def read_more(k, variable):
        return jnp.broadcast_to(picked_more[pl.ds(k * width + variable, 1), :], (ROWS, LANES))

    target = [
        jnp.broadcast_to(message_ref[pl.ds(heavy * 8 + 5 + c, 1), :], (ROWS, LANES))
        for c in range(3)
    ]
    values = solve(corner_of(read_more), target)
    for variable in range(5):
        out_ref[pl.ds(heavy * 16 + 8 + variable, 1), :] = values[variable][0:1]


def relax_kernel(
    owners, node_ref, count_ref, field_ref, below_ref, above_ref, ratio_ref, values_ref, out_ref,
    table,
):
    variables, planes, rows_count, _ = field_ref.shape
    width = 8
    blocks = rows_count // ROWS
    plane_rows = rows_count * width

    def put(plane, block, variable, tile):
        first = plane * plane_rows + block * ROWS * width + variable
        table[pl.ds(first, ROWS, stride=width), :] = tile

    zero = jnp.zeros((ROWS, LANES), jnp.float32)
    for block in range(blocks):
        place = pl.ds(block * ROWS, ROWS)
        for variable in range(variables):
            put(0, block, variable, below_ref[variable, 0, place, :])
            put(planes + 1, block, variable, above_ref[3 + variable, 0, place, :])
            for plane in range(planes):
                put(plane + 1, block, variable, field_ref[variable, plane, place, :])
        for plane in range(planes):
            put(plane + 1, block, variables, zero)

    lane = lax.broadcasted_iota(jnp.int32, (ROWS, LANES), 1)
    sublane = lax.broadcasted_iota(jnp.int32, (ROWS, LANES), 0)

    def scatter(owner, slot, count):
        first = pl.multiple_of(owner * 16 + slot * 8, 8)
        tile = jnp.where(sublane == variables, 1.0, values_ref[pl.ds(first, 8), :])

        def one(point):
            node = node_ref[0, owner, slot, point]
            column = node & 127
            shift = (column - point) & 127
            first = pl.multiple_of(((node >> 7) + rows_count) * width, width)
            pltpu.store(
                table.at[pl.ds(first, width), :], pltpu.roll(tile, shift, 1), mask=lane == column
            )

        def chunk(step, carry):
            for u in range(UNROLL):
                one(step * UNROLL + u)
            return carry

        def single(point, carry):
            one(point)
            return carry

        full = count // UNROLL
        lax.fori_loop(0, full, chunk, 0)
        lax.fori_loop(full * UNROLL, count, single, 0)

    def one_owner(owner, carry):
        count = count_ref[0, owner]
        scatter(owner, 0, jnp.minimum(count, LANES))

        @pl.when(count > LANES)
        def _():
            scatter(owner, 1, count - LANES)

        return carry

    lax.fori_loop(0, owners, one_owner, 0)

    def one_plane(plane, carry):
        for block in range(blocks):
            ratio = ratio_ref[plane, pl.ds(block * ROWS, ROWS), :]
            inverse = 1.0 / (1.0 + 6.0 * ratio)
            base = pl.multiple_of((plane + 1) * plane_rows, plane_rows) + block * ROWS * width

            def get(step, variable):
                return table[pl.ds(base + step * width + variable, ROWS, stride=width), :]

            fringe = get(0, variables) > 0.5
            for variable in range(variables):
                here = get(0, variable)
                up, down = get(1, variable), get(-1, variable)
                if block == 0:
                    down = jnp.where(sublane == 0, 0.0, down)
                if block == blocks - 1:
                    up = jnp.where(sublane == ROWS - 1, 0.0, up)
                right = jnp.where(lane == LANES - 1, 0.0, pltpu.roll(here, LANES - 1, 1))
                left = jnp.where(lane == 0, 0.0, pltpu.roll(here, 1, 1))
                total = get(rows_count, variable) + get(-rows_count, variable)
                total = total + up + down + right + left
                smooth = (here + ratio * total) * inverse
                out_ref[variable, plane, pl.ds(block * ROWS, ROWS), :] = jnp.where(
                    fringe, here, smooth
                )
        return carry

    lax.fori_loop(0, planes, one_plane, 0)


def on_device(
    field, node_jitter, time_ratio, donor_cell, receptor_offset, receptor_node, point_count
):
    variables, planes, rows_count, cols_count = field.shape
    owners = donor_cell.shape[1]
    params = pltpu.CompilerParams(vmem_limit_bytes=LIMIT)
    first = jnp.concatenate([node_jitter[:, :1], field[:, :1]], 0)
    following = passed_along(first, "sub", -1)
    below = passed_along(field[:, planes - 1 :], "sub", 1)

    message = pl.pallas_call(
        pack_kernel,
        out_shape=jax.ShapeDtypeStruct((owners, 8, LANES), jnp.float32),
        in_specs=[SMEM, VMEM, VMEM],
        out_specs=VMEM,
        compiler_params=params,
        name="pack",
    )(point_count, donor_cell, receptor_offset)
    message = lax.all_to_all(message, "grid", split_axis=0, concat_axis=0, tiled=True)
    values = pl.pallas_call(
        functools.partial(gather_kernel, owners),
        out_shape=jax.ShapeDtypeStruct((owners * 16, LANES), jnp.float32),
        in_specs=[VMEM, VMEM, VMEM, VMEM, ANY],
        out_specs=VMEM,
        scratch_shapes=[
            pltpu.VMEM(((planes + 1) * rows_count * 8, LANES), jnp.float32),
            pltpu.SMEM((2, owners, LANES), jnp.float32),
            pltpu.VMEM((8 * 8 * owners, LANES), jnp.float32),
            pltpu.VMEM((8 * 8, LANES), jnp.float32),
            pltpu.SemaphoreType.DMA((2,)),
        ],
        compiler_params=params,
        name="gather",
    )(field, node_jitter, following, message.reshape(owners * 8, LANES), message)
    values = values.reshape(owners, 16, LANES)
    values = lax.all_to_all(values, "grid", split_axis=0, concat_axis=0, tiled=True)
    return pl.pallas_call(
        functools.partial(relax_kernel, owners),
        out_shape=jax.ShapeDtypeStruct(field.shape, jnp.float32),
        in_specs=[SMEM, SMEM, VMEM, VMEM, VMEM, VMEM, VMEM],
        out_specs=VMEM,
        scratch_shapes=[
            pltpu.VMEM(((planes + 2) * rows_count * 8, LANES), jnp.float32),
        ],
        compiler_params=params,
        name="relax",
    )(
        receptor_node, point_count, field, below, following, time_ratio,
        values.reshape(owners * 16, LANES),
    )


def solution(mesh):
    placed = (
        P(None, ("grid", "sub"), None, None),
        P(None, ("grid", "sub"), None, None),
        P(("grid", "sub"), None, None),
        P(("grid", "sub"), None, None, None),
        P(("grid", "sub"), None, None, None, None),
        P(("grid", "sub"), None, None, None),
        P(("grid", "sub"), None),
    )
    return jax.shard_map(
        on_device,
        mesh=mesh,
        in_specs=placed,
        out_specs=P(None, ("grid", "sub"), None, None),
        check_vma=False,
    )
```

```python
import functools

import jax
import jax.numpy as jnp
from jax import lax
from jax.experimental import pallas as pl
from jax.experimental.pallas import tpu as pltpu
from jax.sharding import PartitionSpec as P

ROWS = 8
LANES = 128
UNROLL = 64
VMEM = pl.BlockSpec(memory_space=pltpu.VMEM)
SMEM = pl.BlockSpec(memory_space=pltpu.SMEM)
HBM = pl.BlockSpec(memory_space=pltpu.HBM)
LIMIT = 24 << 20


def passed_along(value, axis, steps):
    count = lax.axis_size(axis)
    pairs = [(source, (source + steps) % count) for source in range(count)]
    return lax.ppermute(value, axis, pairs)


def first_kernel(
    count_ref, cell_ref, offset_ref, node_ref, field_ref, jitter_ref,
    message_ref, code_ref, next_ref, last_ref,
    count_smem, cell_vmem, offset_vmem, node_vmem, sem,
):
    owners, points = cell_ref.shape[1], cell_ref.shape[3]
    variables, planes, rows_count, _ = field_ref.shape
    copies = [
        pltpu.make_async_copy(source, target, sem.at[k])
        for k, (source, target) in enumerate(
            (
                (count_ref, count_smem),
                (cell_ref, cell_vmem),
                (offset_ref, offset_vmem),
                (node_ref, node_vmem),
                (jitter_ref.at[:, pl.ds(0, 1)], next_ref.at[pl.ds(0, 3)]),
                (field_ref.at[:, pl.ds(0, 1)], next_ref.at[pl.ds(3, variables)]),
                (field_ref.at[:, pl.ds(planes - 1, 1)], last_ref),
            )
        )
    ]
    for copy in copies:
        copy.start()
    for copy in copies[:4]:
        copy.wait()

    spare = (planes + 1) * rows_count * 8
    lane = lax.broadcasted_iota(jnp.int32, (1, points), 1)

    def one(owner, carry):
        count = count_smem[0, owner]
        more = count > points
        cells = cell_vmem[0, owner].astype(jnp.float32)
        counts = jnp.full((1, points), count, jnp.int32).astype(jnp.float32)
        message_ref[owner, 0:1, :] = cells[0:1]
        message_ref[owner, 4:5, :] = jnp.where(more, cells[1:2], counts)
        for c in range(3):
            message_ref[owner, 1 + c : 2 + c, :] = offset_vmem[0, owner, c, 0:1, :]
            message_ref[owner, 5 + c : 6 + c, :] = offset_vmem[0, owner, c, 1:2, :]
        nodes = node_vmem[0, owner]
        code_ref[0, pl.ds(owner, 1), :] = jnp.where(lane < count, (nodes[0:1] >> 7) * 8, spare)
        code_ref[1, pl.ds(owner, 1), :] = nodes[0:1] & 127

        @pl.when(more)
        def _():
            live = lane + points < count
            code_ref[0, owners : owners + 1, :] = jnp.where(live, (nodes[1:2] >> 7) * 8, spare)
            code_ref[1, owners : owners + 1, :] = nodes[1:2] & 127

        return carry

    lax.fori_loop(0, owners, one, 0, unroll=True)
    for copy in copies[4:]:
        copy.wait()


def coefficients(corner):
    linear = [corner[4] - corner[0], corner[2] - corner[0], corner[1] - corner[0]]
    pair_01 = corner[6] - corner[4] - linear[1]
    pair_02 = corner[5] - corner[4] - linear[2]
    pair_12 = corner[3] - corner[2] - linear[2]
    triple = (corner[7] - corner[6]) - (corner[5] - corner[4]) - pair_12
    return corner[0], linear, pair_01, pair_02, pair_12, triple


def solve(corner, target):
    polys = []
    for component in range(3):
        start, linear, pair_01, pair_02, pair_12, triple = coefficients(
            [corner(q, component) for q in range(8)]
        )
        linear[component] = linear[component] + 1.0
        polys.append((start - target[component], linear, pair_01, pair_02, pair_12, triple))
    s0 = s1 = s2 = jnp.full(target[0].shape, 0.5, jnp.float32)
    for _ in range(4):
        s01, s02, s12 = s0 * s1, s0 * s2, s1 * s2
        misfit, jac = [], []
        for start, (l0, l1, l2), p01, p02, p12, triple in polys:
            d0 = l0 + s1 * p01 + s2 * p02 + s12 * triple
            d1 = l1 + s0 * p01 + s2 * p12 + s02 * triple
            d2 = l2 + s0 * p02 + s1 * p12 + s01 * triple
            misfit.append(start + s0 * d0 + s1 * (l1 + s2 * p12) + s2 * l2)
            jac.append((d0, d1, d2))
        (a0, a1, a2), (b0, b1, b2), (c0, c1, c2) = jac
        m0, m1, m2 = misfit
        bc12 = b1 * c2 - b2 * c1
        bc02 = b0 * c2 - b2 * c0
        bc01 = b0 * c1 - b1 * c0
        det = a0 * bc12 - a1 * bc02 + a2 * bc01
        bm2 = m1 * c2 - b2 * m2
        bm1 = m1 * c1 - b1 * m2
        bm0 = b0 * m2 - m1 * c0
        inverse = 1.0 / det
        u0 = m0 * bc12 - a1 * bm2 + a2 * bm1
        u1 = a0 * bm2 - m0 * bc02 + a2 * bm0
        u2 = a0 * (b1 * m2 - m1 * c1) - a1 * bm0 + m0 * bc01
        s0 = s0 - u0 * inverse
        s1 = s1 - u1 * inverse
        s2 = s2 - u2 * inverse
    values = []
    for variable in range(5):
        u = [corner(q, 3 + variable) for q in range(8)]
        e = [u[q] + s2 * (u[q + 1] - u[q]) for q in (0, 2, 4, 6)]
        f = [e[q] + s1 * (e[q + 1] - e[q]) for q in (0, 2)]
        values.append(f[0] + s0 * (f[1] - f[0]))
    return values


def table_kernel(field_ref, jitter_ref, next_ref, table_ref):
    planes, rows_count, columns = field_ref.shape[1:]

    def one_plane(plane, read):
        for half in range(2):
            tile = jnp.concatenate([read(4 * half + w) for w in range(4)], 0).T
            first = plane * (2 * columns) + half
            table_ref[pl.ds(first, columns, stride=2), :] = tile

    for plane in range(planes):
        one_plane(
            plane, lambda v: jitter_ref[v, plane] if v < 3 else field_ref[v - 3, plane]
        )
    one_plane(planes, lambda v: next_ref[v, 0])


def separated(tiles, lane):
    for bit, distance in ((0, 1), (1, 32), (2, 64)):
        low = (lane & distance) == 0
        result = list(tiles)
        for a in range(8):
            b = a | (1 << bit)
            if a == b:
                continue
            result[a] = jnp.where(low, tiles[a], pltpu.roll(tiles[b], distance, 1))
            result[b] = jnp.where(low, pltpu.roll(tiles[a], LANES - distance, 1), tiles[b])
        tiles = result
    return tiles


def gather_kernel(
    owners, table_ref, message_ref, out_ref, decoded, codes, count_vmem, counts, picked, parts, sem
):
    rows_count = 32
    me = lax.axis_index("grid")
    heavy = lax.rem(me + owners - 1, owners)
    lane = lax.broadcasted_iota(jnp.int32, (ROWS, LANES), 1)
    sublane = lax.broadcasted_iota(jnp.int32, (ROWS, LANES), 0)

    def decode(cells, place):
        cells = cells.astype(jnp.int32)
        decoded[0, place, :] = (cells >> 12) * (2 * LANES) + (cells & 127) * 2
        row = (cells >> 7) & (rows_count - 1)
        decoded[1, place, :] = ((lane & 30) - row) & 127

    for block in range(owners // ROWS):
        place = pl.ds(block * ROWS, ROWS)
        decode(message_ref[pl.ds(block * ROWS * 8, ROWS, stride=8), :], place)
        count_vmem[place, :] = message_ref[
            pl.ds(block * ROWS * 8 + 4, ROWS, stride=8), :
        ].astype(jnp.int32)
    more = jnp.broadcast_to(message_ref[pl.ds(heavy * 8 + 4, 1), :], (ROWS, LANES))
    decode(more, pl.ds(owners, ROWS))
    copies = [
        pltpu.make_async_copy(decoded, codes, sem.at[0]),
        pltpu.make_async_copy(count_vmem, counts, sem.at[1]),
    ]
    for copy in copies:
        copy.start()
    for copy in copies:
        copy.wait()

    low = sublane < 4
    pairs = [(lane & 30) == 2 * k for k in range(16)]

    def pick(source, first):
        for block in range(first // 32, (first + UNROLL) // 32):
            held = [None, None]
            for k in range(32):
                point = block * 32 + k
                row = codes[0, source, point]
                shift = codes[1, source, point]
                tile = jnp.where(
                    low,
                    table_ref[pl.ds(row, ROWS), :],
                    table_ref[pl.ds(row + (2 * LANES - 4), ROWS), :],
                )
                tile = pltpu.roll(tile, shift, 1)
                k2 = k & 1
                held[k2] = tile if held[k2] is None else jnp.where(pairs[k >> 1], tile, held[k2])
            for k in range(2):
                place = ((2 * block + k) * (owners + 1) + source) * 8
                picked[pl.ds(pl.multiple_of(place, 8), ROWS), :] = held[k]

    def one_source(source, carry):
        pick(source, 0)
        count = counts[source, 0]

        @pl.when((count > UNROLL) | (source == heavy) | (source == owners))
        def _():
            pick(source, UNROLL)

        return carry

    lax.fori_loop(0, owners + 1, one_source, 0)

    def solved(read, target):
        def corner(q, variable):
            a0, a1, a2 = q >> 2, (q >> 1) & 1, q & 1
            half, w = variable >> 2, variable & 3
            return read(4 * a0 + 2 * a2 + half, 2 * w + a1)

        return solve(corner, target)

    def one_block(block, carry):
        for s in range(8):
            tiles = [
                picked[pl.ds((g * (owners + 1) + block * ROWS) * 8 + s, ROWS, stride=8), :]
                for g in range(8)
            ]
            for x, tile in enumerate(separated(tiles, lane)):
                parts[s, x] = tile
        first = block * (ROWS * 8)
        target = [message_ref[pl.ds(first + 1 + c, ROWS, stride=8), :] for c in range(3)]
        values = solved(lambda s, x: parts[s, x], target)
        for variable in range(5):
            place = pl.ds(block * (ROWS * 16) + variable, ROWS, stride=16)
            out_ref[place, :] = values[variable]
        return carry

    lax.fori_loop(0, owners // ROWS, one_block, 0, unroll=True)

    tiles = [picked[pl.ds((g * (owners + 1) + owners) * 8, 8), :] for g in range(8)]
    for x, tile in enumerate(separated(tiles, lane)):
        parts[8, x] = tile

    def read_more(s, x):
        return jnp.broadcast_to(parts[8, x, s : s + 1, :], (ROWS, LANES))

    target = [
        jnp.broadcast_to(message_ref[pl.ds(heavy * 8 + 5 + c, 1), :], (ROWS, LANES))
        for c in range(3)
    ]
    values = solved(read_more, target)
    for variable in range(5):
        out_ref[pl.ds(heavy * 16 + 8 + variable, 1), :] = values[variable][0:1]


def relax_kernel(
    owners, count_ref, code_ref, field_ref, below_ref, above_ref, ratio_ref, values_ref, out_ref,
    table, codes, out_vmem, sem, out_sem,
):
    variables, planes, rows_count, _ = field_ref.shape
    width = 8
    blocks = rows_count // ROWS
    plane_rows = rows_count * width

    copy = pltpu.make_async_copy(code_ref, codes, sem)
    copy.start()

    def put(plane, block, variable, tile):
        first = plane * plane_rows + block * ROWS * width + variable
        table[pl.ds(first, ROWS, stride=width), :] = tile

    zero = jnp.zeros((ROWS, LANES), jnp.float32)
    for block in range(blocks):
        place = pl.ds(block * ROWS, ROWS)
        for variable in range(variables):
            put(0, block, variable, below_ref[variable, 0, place, :])
            put(planes + 1, block, variable, above_ref[3 + variable, 0, place, :])
            for plane in range(planes):
                put(plane + 1, block, variable, field_ref[variable, plane, place, :])
        for plane in range(planes):
            put(plane + 1, block, variables, zero)

    copy.wait()
    lane = lax.broadcasted_iota(jnp.int32, (ROWS, LANES), 1)
    sublane = lax.broadcasted_iota(jnp.int32, (ROWS, LANES), 0)

    def scatter(source, tile, first):
        for point in range(first, first + UNROLL):
            row = codes[0, source, point]
            column = codes[1, source, point]
            place = pl.ds(pl.multiple_of(row + plane_rows, width), width)
            tile_here = pltpu.roll(tile, (column - point) & 127, 1)
            pltpu.store(table.at[place, :], tile_here, mask=lane == column)

    def one_source(source, carry):
        owner = jnp.where(source == owners, heavy, source)
        count = jnp.where(source == owners, LANES, count_ref[0, owner])
        first = pl.multiple_of(owner * 16 + jnp.where(source == owners, 8, 0), 8)
        tile = jnp.where(sublane == variables, 1.0, values_ref[pl.ds(first, 8), :])
        scatter(source, tile, 0)

        @pl.when(count > UNROLL)
        def _():
            scatter(source, tile, UNROLL)

        return carry

    heavy = lax.rem(lax.axis_index("grid") + 1, owners)
    lax.fori_loop(0, owners + 1, one_source, 0)

    def out_copy(plane):
        return pltpu.make_async_copy(
            out_vmem.at[:, pl.ds(plane, 1)], out_ref.at[:, pl.ds(plane, 1)], out_sem.at[plane]
        )

    def one_plane(plane, carry):
        for block in range(blocks):
            ratio = ratio_ref[plane, pl.ds(block * ROWS, ROWS), :]
            inverse = 1.0 / (1.0 + 6.0 * ratio)
            base = pl.multiple_of((plane + 1) * plane_rows, plane_rows) + block * ROWS * width

            def get(step, variable):
                return table[pl.ds(base + step * width + variable, ROWS, stride=width), :]

            fringe = get(0, variables) > 0.5
            for variable in range(variables):
                here = get(0, variable)
                up, down = get(1, variable), get(-1, variable)
                if block == 0:
                    down = jnp.where(sublane == 0, 0.0, down)
                if block == blocks - 1:
                    up = jnp.where(sublane == ROWS - 1, 0.0, up)
                right = jnp.where(lane == LANES - 1, 0.0, pltpu.roll(here, LANES - 1, 1))
                left = jnp.where(lane == 0, 0.0, pltpu.roll(here, 1, 1))
                total = get(rows_count, variable) + get(-rows_count, variable)
                total = total + up + down + right + left
                smooth = (here + ratio * total) * inverse
                out_vmem[variable, plane, pl.ds(block * ROWS, ROWS), :] = jnp.where(
                    fringe, here, smooth
                )
        out_copy(plane).start()
        return carry

    lax.fori_loop(0, planes, one_plane, 0)
    for plane in range(planes):
        out_copy(plane).wait()


def on_device(
    field, node_jitter, time_ratio, donor_cell, receptor_offset, receptor_node, point_count
):
    variables, planes, rows_count, cols_count = field.shape
    owners, points = donor_cell.shape[1], donor_cell.shape[3]
    params = pltpu.CompilerParams(vmem_limit_bytes=LIMIT)
    offsets = jnp.swapaxes(receptor_offset, 2, 3)
    f32, i32 = jnp.float32, jnp.int32
    message, codes, first, last = pl.pallas_call(
        first_kernel,
        out_shape=[
            jax.ShapeDtypeStruct((owners, 8, LANES), f32),
            jax.ShapeDtypeStruct((2, owners + 8, LANES), i32),
            jax.ShapeDtypeStruct((3 + variables, 1, rows_count, cols_count), f32),
            jax.ShapeDtypeStruct((variables, 1, rows_count, cols_count), f32),
        ],
        in_specs=[HBM] * 6,
        out_specs=[VMEM] * 4,
        scratch_shapes=[
            pltpu.SMEM(point_count.shape, i32),
            pltpu.VMEM(donor_cell.shape, i32),
            pltpu.VMEM(offsets.shape, f32),
            pltpu.VMEM(receptor_node.shape, i32),
            pltpu.SemaphoreType.DMA((7,)),
        ],
        compiler_params=params,
        name="first",
    )(point_count, donor_cell, offsets, receptor_node, field, node_jitter)
    following = passed_along(first, "sub", -1)
    below = passed_along(last, "sub", 1)
    message = lax.all_to_all(message, "grid", split_axis=0, concat_axis=0, tiled=True)
    table = pl.pallas_call(
        table_kernel,
        out_shape=jax.ShapeDtypeStruct(((planes + 1) * cols_count * 2, LANES), f32),
        in_specs=[VMEM] * 3,
        out_specs=VMEM,
        compiler_params=params,
        cost_estimate=pl.CostEstimate(flops=0, bytes_accessed=8 << 20, transcendentals=0),
        name="table",
    )(field, node_jitter, following)
    values = pl.pallas_call(
        functools.partial(gather_kernel, owners),
        out_shape=jax.ShapeDtypeStruct((owners * 16, LANES), f32),
        in_specs=[VMEM, VMEM],
        out_specs=VMEM,
        scratch_shapes=[
            pltpu.VMEM((2, owners + 8, LANES), i32),
            pltpu.SMEM((2, owners + 8, LANES), i32),
            pltpu.VMEM((owners, LANES), i32),
            pltpu.SMEM((owners, LANES), i32),
            pltpu.VMEM((8 * (owners + 1) * 8, LANES), f32),
            pltpu.VMEM((9, 8, ROWS, LANES), f32),
            pltpu.SemaphoreType.DMA((2,)),
        ],
        compiler_params=params,
        name="gather",
    )(table, message.reshape(owners * 8, LANES))
    values = values.reshape(owners, 16, LANES)
    values = lax.all_to_all(values, "grid", split_axis=0, concat_axis=0, tiled=True)
    return pl.pallas_call(
        functools.partial(relax_kernel, owners),
        out_shape=jax.ShapeDtypeStruct(field.shape, f32),
        in_specs=[SMEM] + [VMEM] * 6,
        out_specs=HBM,
        scratch_shapes=[
            pltpu.VMEM(((planes + 2) * rows_count * 8 + 8, LANES), f32),
            pltpu.SMEM((2, owners + 8, LANES), i32),
            pltpu.VMEM(field.shape, f32),
            pltpu.SemaphoreType.DMA,
            pltpu.SemaphoreType.DMA((planes,)),
        ],
        compiler_params=params,
        name="relax",
    )(
        point_count, codes, field, below, following, time_ratio,
        values.reshape(owners * 16, LANES),
    )


def solution(mesh):
    placed = (
        P(None, ("grid", "sub"), None, None),
        P(None, ("grid", "sub"), None, None),
        P(("grid", "sub"), None, None),
        P(("grid", "sub"), None, None, None),
        P(("grid", "sub"), None, None, None, None),
        P(("grid", "sub"), None, None, None),
        P(("grid", "sub"), None),
    )
    return jax.shard_map(
        on_device,
        mesh=mesh,
        in_specs=placed,
        out_specs=P(None, ("grid", "sub"), None, None),
        check_vma=False,
    )
```

```python
import functools

import jax
import jax.numpy as jnp
from jax import lax
from jax.experimental import pallas as pl
from jax.experimental.pallas import tpu as pltpu
from jax.sharding import PartitionSpec as P

ROWS = 8
LANES = 128
VMEM = pl.BlockSpec(memory_space=pltpu.VMEM)
HBM = pl.BlockSpec(memory_space=pltpu.HBM)
LIMIT = 24 << 20


def passed_along(value, axis, steps):
    count = lax.axis_size(axis)
    pairs = [(source, (source + steps) % count) for source in range(count)]
    return lax.ppermute(value, axis, pairs)


def first_kernel(
    count_ref, cell_ref, offset_ref, node_ref, field_ref, jitter_ref,
    message_ref, code_ref, next_ref, last_ref,
    count_smem, cell_vmem, offset_vmem, node_vmem, sem,
):
    owners, points = cell_ref.shape[1], cell_ref.shape[3]
    variables, planes, rows_count, _ = field_ref.shape
    copies = [
        pltpu.make_async_copy(source, target, sem.at[k])
        for k, (source, target) in enumerate(
            (
                (count_ref, count_smem),
                (cell_ref, cell_vmem),
                (offset_ref, offset_vmem),
                (node_ref, node_vmem),
                (jitter_ref.at[:, pl.ds(0, 1)], next_ref.at[pl.ds(0, 3)]),
                (field_ref.at[:, pl.ds(0, 1)], next_ref.at[pl.ds(3, variables)]),
                (field_ref.at[:, pl.ds(planes - 1, 1)], last_ref),
            )
        )
    ]
    for copy in copies:
        copy.start()
    for copy in copies[:4]:
        copy.wait()

    spare = (planes + 1) * rows_count * 8
    lane = lax.broadcasted_iota(jnp.int32, (1, points), 1)

    def coded(nodes, live):
        row = jnp.where(live, (nodes >> 7) * 8, spare)
        return row * LANES + (((nodes & 127) - lane) & 127)

    def one(owner, carry):
        count = count_smem[0, owner]
        more = count > points
        cells = cell_vmem[0, owner].astype(jnp.float32)
        counts = jnp.full((1, points), count, jnp.int32).astype(jnp.float32)
        message_ref[owner, 0:1, :] = cells[0:1]
        message_ref[owner, 4:5, :] = jnp.where(more, cells[1:2], counts)
        for c in range(3):
            message_ref[owner, 1 + c : 2 + c, :] = offset_vmem[0, owner, c, 0:1, :]
            message_ref[owner, 5 + c : 6 + c, :] = offset_vmem[0, owner, c, 1:2, :]
        nodes = node_vmem[0, owner]
        code_ref[pl.ds(owner, 1), :] = coded(nodes[0:1], lane < count)

        @pl.when(more)
        def _():
            code_ref[owners : owners + 1, :] = coded(nodes[1:2], lane + points < count)

        return carry

    lax.fori_loop(0, owners, one, 0, unroll=True)
    for copy in copies[4:]:
        copy.wait()


def coefficients(corner):
    linear = [corner[4] - corner[0], corner[2] - corner[0], corner[1] - corner[0]]
    pair_01 = corner[6] - corner[4] - linear[1]
    pair_02 = corner[5] - corner[4] - linear[2]
    pair_12 = corner[3] - corner[2] - linear[2]
    triple = (corner[7] - corner[6]) - (corner[5] - corner[4]) - pair_12
    return corner[0], linear, pair_01, pair_02, pair_12, triple


def solve(corner, target):
    polys = []
    for component in range(3):
        start, linear, pair_01, pair_02, pair_12, triple = coefficients(
            [corner(q, component) for q in range(8)]
        )
        linear[component] = linear[component] + 1.0
        polys.append((start - target[component], linear, pair_01, pair_02, pair_12, triple))
    s0 = s1 = s2 = jnp.full(target[0].shape, 0.5, jnp.float32)
    for _ in range(4):
        s01, s02, s12 = s0 * s1, s0 * s2, s1 * s2
        misfit, jac = [], []
        for start, (l0, l1, l2), p01, p02, p12, triple in polys:
            d0 = l0 + s1 * p01 + s2 * p02 + s12 * triple
            d1 = l1 + s0 * p01 + s2 * p12 + s02 * triple
            d2 = l2 + s0 * p02 + s1 * p12 + s01 * triple
            misfit.append(start + s0 * d0 + s1 * (l1 + s2 * p12) + s2 * l2)
            jac.append((d0, d1, d2))
        (a0, a1, a2), (b0, b1, b2), (c0, c1, c2) = jac
        m0, m1, m2 = misfit
        bc12 = b1 * c2 - b2 * c1
        bc02 = b0 * c2 - b2 * c0
        bc01 = b0 * c1 - b1 * c0
        det = a0 * bc12 - a1 * bc02 + a2 * bc01
        bm2 = m1 * c2 - b2 * m2
        bm1 = m1 * c1 - b1 * m2
        bm0 = b0 * m2 - m1 * c0
        inverse = 1.0 / det
        u0 = m0 * bc12 - a1 * bm2 + a2 * bm1
        u1 = a0 * bm2 - m0 * bc02 + a2 * bm0
        u2 = a0 * (b1 * m2 - m1 * c1) - a1 * bm0 + m0 * bc01
        s0 = s0 - u0 * inverse
        s1 = s1 - u1 * inverse
        s2 = s2 - u2 * inverse
    values = []
    for variable in range(5):
        u = [corner(q, 3 + variable) for q in range(8)]
        e = [u[q] + s2 * (u[q + 1] - u[q]) for q in (0, 2, 4, 6)]
        f = [e[q] + s1 * (e[q + 1] - e[q]) for q in (0, 2)]
        values.append(f[0] + s0 * (f[1] - f[0]))
    return values


def table_kernel(field_ref, jitter_ref, next_ref, table_ref):
    planes, rows_count, columns = field_ref.shape[1:]

    def one_plane(plane, read):
        for half in range(2):
            tile = jnp.concatenate([read(4 * half + w) for w in range(4)], 0).T
            first = plane * (2 * columns) + half
            table_ref[pl.ds(first, columns, stride=2), :] = tile

    for plane in range(planes):
        one_plane(
            plane, lambda v: jitter_ref[v, plane] if v < 3 else field_ref[v - 3, plane]
        )
    one_plane(planes, lambda v: next_ref[v, 0])


def separated(tiles, lane):
    for bit, distance in ((0, 1), (1, 32), (2, 64)):
        low = (lane & distance) == 0
        result = list(tiles)
        for a in range(8):
            b = a | (1 << bit)
            if a == b:
                continue
            result[a] = jnp.where(low, tiles[a], pltpu.roll(tiles[b], distance, 1))
            result[b] = jnp.where(low, pltpu.roll(tiles[a], LANES - distance, 1), tiles[b])
        tiles = result
    return tiles


def tile_rows(tile):
    first = tile * ROWS
    return pl.ds(first if isinstance(first, int) else pl.multiple_of(first, ROWS), ROWS)


def each_source(owners, body):
    if owners <= 8:
        for source in range(owners + 1):
            body(source, 0)
    else:
        lax.fori_loop(0, owners + 1, body, 0)


def gather_kernel(owners, table_ref, message_ref, out_ref, decoded, codes, picked, parts, sem):
    rows_count = 32
    me = lax.axis_index("grid")
    heavy = lax.rem(me + owners - 1, owners)
    lane = lax.broadcasted_iota(jnp.int32, (ROWS, LANES), 1)
    sublane = lax.broadcasted_iota(jnp.int32, (ROWS, LANES), 0)

    def decode(cells, place):
        cells = cells.astype(jnp.int32)
        row = (cells >> 12) * (2 * LANES) + (cells & 127) * 2
        shift = ((lane & 30) - ((cells >> 7) & (rows_count - 1))) & 127
        decoded[place, :] = row * LANES + shift

    for block in range(owners // ROWS):
        cells = message_ref[pl.ds(block * ROWS * 8, ROWS, stride=8), :]
        decode(cells, pl.ds(block * ROWS, ROWS))
    more = jnp.broadcast_to(message_ref[pl.ds(heavy * 8 + 4, 1), :], (ROWS, LANES))
    decode(more, pl.ds(owners, ROWS))
    copy = pltpu.make_async_copy(decoded, codes, sem)
    copy.start()
    copy.wait()

    low = sublane < 4
    pairs = [(lane & 30) == 2 * k for k in range(16)]

    def one_source(source, carry):
        for block in range(4):
            held = [None, None]
            for k in range(32):
                code = codes[source, block * 32 + k]
                row = code >> 7
                tile = jnp.where(
                    low,
                    table_ref[pl.ds(row, ROWS), :],
                    table_ref[pl.ds(row + (2 * LANES - 4), ROWS), :],
                )
                tile = pltpu.roll(tile, code & 127, 1)
                k2 = k & 1
                held[k2] = tile if held[k2] is None else jnp.where(pairs[k >> 1], tile, held[k2])
            for k in range(2):
                picked[tile_rows((2 * block + k) * (owners + 1) + source), :] = held[k]
        return carry

    each_source(owners, one_source)

    def one_block(block, last):
        for s in range(8):
            tiles = [
                picked[pl.ds((g * (owners + 1) + block * ROWS) * 8 + s, ROWS, stride=8), :]
                for g in range(8)
            ]
            for x, tile in enumerate(separated(tiles, lane)):
                parts[s, x] = tile
        if last:
            tiles = [picked[pl.ds((g * (owners + 1) + owners) * 8, 8), :] for g in range(8)]
            for x, tile in enumerate(separated(tiles, lane)):
                parts[8, x] = tile

        def corner(q, variable):
            a0, a1, a2 = q >> 2, (q >> 1) & 1, q & 1
            s, x = 4 * a0 + 2 * a2 + (variable >> 2), 2 * (variable & 3) + a1
            tile = parts[s, x]
            if last:
                more = jnp.broadcast_to(parts[8, x, s : s + 1, :], (ROWS, LANES))
                tile = jnp.concatenate([tile, more], 0)
            return tile

        target = []
        for c in range(3):
            tile = message_ref[pl.ds(block * (ROWS * 8) + 1 + c, ROWS, stride=8), :]
            if last:
                more = message_ref[pl.ds(heavy * 8 + 5 + c, 1), :]
                tile = jnp.concatenate([tile, jnp.broadcast_to(more, (ROWS, LANES))], 0)
            target.append(tile)
        values = solve(corner, target)
        for variable in range(5):
            place = pl.ds(block * (ROWS * 16) + variable, ROWS, stride=16)
            out_ref[place, :] = values[variable][:ROWS]
            if last:
                out_ref[pl.ds(heavy * 16 + 8 + variable, 1), :] = values[variable][ROWS : ROWS + 1]

    for block in range(owners // ROWS):
        one_block(block, block == owners // ROWS - 1)


def relax_kernel(
    owners, code_ref, field_ref, below_ref, above_ref, ratio_ref, values_ref, out_ref,
    table, codes, out_vmem, sem, out_sem,
):
    variables, planes, rows_count, _ = field_ref.shape
    width = 8
    blocks = rows_count // ROWS
    plane_rows = rows_count * width

    copy = pltpu.make_async_copy(code_ref, codes, sem)
    copy.start()

    def put(plane, block, variable, tile):
        first = plane * plane_rows + block * ROWS * width + variable
        table[pl.ds(first, ROWS, stride=width), :] = tile

    zero = jnp.zeros((ROWS, LANES), jnp.float32)
    for block in range(blocks):
        place = pl.ds(block * ROWS, ROWS)
        for variable in range(variables):
            put(0, block, variable, below_ref[variable, 0, place, :])
            put(planes + 1, block, variable, above_ref[3 + variable, 0, place, :])
            for plane in range(planes):
                put(plane + 1, block, variable, field_ref[variable, plane, place, :])
        for plane in range(planes):
            put(plane + 1, block, variables, zero)

    copy.wait()
    lane = lax.broadcasted_iota(jnp.int32, (ROWS, LANES), 1)
    sublane = lax.broadcasted_iota(jnp.int32, (ROWS, LANES), 0)

    heavy = lax.rem(lax.axis_index("grid") + 1, owners)

    def one_source(source, carry):
        if isinstance(source, int):
            first = 16 * source if source < owners else heavy * 16 + 8
        else:
            more = source == owners
            first = jnp.where(more, heavy * 16 + 8, source * 16)
        if not isinstance(first, int):
            first = pl.multiple_of(first, 8)
        tile = jnp.where(sublane == variables, 1.0, values_ref[pl.ds(first, 8), :])
        for point in range(LANES):
            code = codes[source, point]
            shift = code & 127
            row = pl.multiple_of((code >> 7) + plane_rows, width)
            pltpu.store(
                table.at[pl.ds(row, width), :],
                pltpu.roll(tile, shift, 1),
                mask=((lane - point) & 127) == shift,
            )
        return carry

    each_source(owners, one_source)

    def out_copy(plane):
        return pltpu.make_async_copy(
            out_vmem.at[:, pl.ds(plane, 1)], out_ref.at[:, pl.ds(plane, 1)], out_sem.at[plane]
        )

    def one_plane(plane):
        for block in range(blocks):
            ratio = ratio_ref[plane, pl.ds(block * ROWS, ROWS), :]
            inverse = 1.0 / (1.0 + 6.0 * ratio)
            base = (plane + 1) * plane_rows + block * ROWS * width

            def get(step, variable):
                return table[pl.ds(base + step * width + variable, ROWS, stride=width), :]

            fringe = get(0, variables) > 0.5
            for variable in range(variables):
                here = get(0, variable)
                up, down = get(1, variable), get(-1, variable)
                if block == 0:
                    down = jnp.where(sublane == 0, 0.0, down)
                if block == blocks - 1:
                    up = jnp.where(sublane == ROWS - 1, 0.0, up)
                right = jnp.where(lane == LANES - 1, 0.0, pltpu.roll(here, LANES - 1, 1))
                left = jnp.where(lane == 0, 0.0, pltpu.roll(here, 1, 1))
                total = get(rows_count, variable) + get(-rows_count, variable)
                total = total + up + down + right + left
                smooth = (here + ratio * total) * inverse
                out_vmem[variable, plane, pl.ds(block * ROWS, ROWS), :] = jnp.where(
                    fringe, here, smooth
                )
        out_copy(plane).start()

    for plane in range(planes):
        one_plane(plane)
    for plane in range(planes):
        out_copy(plane).wait()


def on_device(
    field, node_jitter, time_ratio, donor_cell, receptor_offset, receptor_node, point_count
):
    variables, planes, rows_count, cols_count = field.shape
    owners, points = donor_cell.shape[1], donor_cell.shape[3]
    params = pltpu.CompilerParams(vmem_limit_bytes=LIMIT)
    offsets = jnp.swapaxes(receptor_offset, 2, 3)
    f32, i32 = jnp.float32, jnp.int32
    message, codes, first, last = pl.pallas_call(
        first_kernel,
        out_shape=[
            jax.ShapeDtypeStruct((owners, 8, LANES), f32),
            jax.ShapeDtypeStruct((owners + 8, LANES), i32),
            jax.ShapeDtypeStruct((3 + variables, 1, rows_count, cols_count), f32),
            jax.ShapeDtypeStruct((variables, 1, rows_count, cols_count), f32),
        ],
        in_specs=[HBM] * 6,
        out_specs=[VMEM] * 4,
        scratch_shapes=[
            pltpu.SMEM(point_count.shape, i32),
            pltpu.VMEM(donor_cell.shape, i32),
            pltpu.VMEM(offsets.shape, f32),
            pltpu.VMEM(receptor_node.shape, i32),
            pltpu.SemaphoreType.DMA((7,)),
        ],
        compiler_params=params,
        name="first",
    )(*[
        pltpu.with_memory_space_constraint(x, pltpu.HBM)
        for x in (point_count, donor_cell, offsets, receptor_node, field, node_jitter)
    ])
    following = passed_along(first, "sub", -1)
    below = passed_along(last, "sub", 1)
    message = lax.all_to_all(message, "grid", split_axis=0, concat_axis=0, tiled=True)
    table = pl.pallas_call(
        table_kernel,
        out_shape=jax.ShapeDtypeStruct(((planes + 1) * cols_count * 2, LANES), f32),
        in_specs=[VMEM] * 3,
        out_specs=VMEM,
        compiler_params=params,
        cost_estimate=pl.CostEstimate(flops=0, bytes_accessed=8 << 20, transcendentals=0),
        name="table",
    )(field, node_jitter, following)
    values = pl.pallas_call(
        functools.partial(gather_kernel, owners),
        out_shape=jax.ShapeDtypeStruct((owners * 16, LANES), f32),
        in_specs=[VMEM, VMEM],
        out_specs=VMEM,
        scratch_shapes=[
            pltpu.VMEM((owners + 8, LANES), i32),
            pltpu.SMEM((owners + 8, LANES), i32),
            pltpu.VMEM((8 * (owners + 1) * 8, LANES), f32),
            pltpu.VMEM((9, 8, ROWS, LANES), f32),
            pltpu.SemaphoreType.DMA,
        ],
        compiler_params=params,
        name="gather",
    )(table, message.reshape(owners * 8, LANES))
    values = values.reshape(owners, 16, LANES)
    values = lax.all_to_all(values, "grid", split_axis=0, concat_axis=0, tiled=True)
    return pl.pallas_call(
        functools.partial(relax_kernel, owners),
        out_shape=jax.ShapeDtypeStruct(field.shape, f32),
        in_specs=[VMEM] * 6,
        out_specs=HBM,
        scratch_shapes=[
            pltpu.VMEM(((planes + 2) * rows_count * 8 + 8, LANES), f32),
            pltpu.SMEM((owners + 8, LANES), i32),
            pltpu.VMEM(field.shape, f32),
            pltpu.SemaphoreType.DMA,
            pltpu.SemaphoreType.DMA((planes,)),
        ],
        compiler_params=params,
        name="relax",
    )(
        codes, field, below, following, time_ratio,
        values.reshape(owners * 16, LANES),
    )


def solution(mesh):
    placed = (
        P(None, ("grid", "sub"), None, None),
        P(None, ("grid", "sub"), None, None),
        P(("grid", "sub"), None, None),
        P(("grid", "sub"), None, None, None),
        P(("grid", "sub"), None, None, None, None),
        P(("grid", "sub"), None, None, None),
        P(("grid", "sub"), None),
    )
    return jax.shard_map(
        on_device,
        mesh=mesh,
        in_specs=placed,
        out_specs=P(None, ("grid", "sub"), None, None),
        check_vma=False,
    )
```

```python
import functools

import jax
import jax.numpy as jnp
from jax import lax
from jax.experimental import pallas as pl
from jax.experimental.pallas import tpu as pltpu
from jax.sharding import PartitionSpec as P

ROWS = 8
LANES = 128
VMEM = pl.BlockSpec(memory_space=pltpu.VMEM)
HBM = pl.BlockSpec(memory_space=pltpu.HBM)
LIMIT = 24 << 20


def passed_along(value, axis, steps):
    count = lax.axis_size(axis)
    pairs = [(source, (source + steps) % count) for source in range(count)]
    return lax.ppermute(value, axis, pairs)


def first_kernel(
    count_ref, cell_ref, offset_ref, node_ref, field_ref, jitter_ref,
    message_ref, code_ref, next_ref, last_ref,
    count_smem, cell_vmem, offset_vmem, node_vmem, sem,
):
    owners, points = cell_ref.shape[1], cell_ref.shape[3]
    variables, planes, rows_count, _ = field_ref.shape
    copies = [
        pltpu.make_async_copy(source, target, sem.at[k])
        for k, (source, target) in enumerate(
            (
                (count_ref, count_smem),
                (cell_ref, cell_vmem),
                (offset_ref, offset_vmem),
                (node_ref, node_vmem),
                (jitter_ref.at[:, pl.ds(0, 1)], next_ref.at[pl.ds(0, 3)]),
                (field_ref.at[:, pl.ds(0, 1)], next_ref.at[pl.ds(3, variables)]),
                (field_ref.at[:, pl.ds(planes - 1, 1)], last_ref),
            )
        )
    ]
    for copy in copies:
        copy.start()
    for copy in copies[:4]:
        copy.wait()

    spare = (planes + 1) * rows_count * 8
    lane = lax.broadcasted_iota(jnp.int32, (1, points), 1)

    def code(place, nodes, live):
        code_ref[0, place, :] = jnp.where(live, (nodes >> 7) * 8, spare)
        code_ref[1, place, :] = ((nodes & 127) - lane) & 127

    def one(owner, carry):
        count = count_smem[0, owner]
        more = count > points
        cells = cell_vmem[0, owner].astype(jnp.float32)
        counts = jnp.full((1, points), count, jnp.int32).astype(jnp.float32)
        message_ref[owner, 0:1, :] = cells[0:1]
        message_ref[owner, 4:5, :] = jnp.where(more, cells[1:2], counts)
        for c in range(3):
            message_ref[owner, 1 + c : 2 + c, :] = offset_vmem[0, owner, c, 0:1, :]
            message_ref[owner, 5 + c : 6 + c, :] = offset_vmem[0, owner, c, 1:2, :]
        nodes = node_vmem[0, owner]
        code(pl.ds(owner, 1), nodes[0:1], lane < count)

        @pl.when(more)
        def _():
            code(pl.ds(owners, 1), nodes[1:2], lane + points < count)

        return carry

    lax.fori_loop(0, owners, one, 0, unroll=True)
    for copy in copies[4:]:
        copy.wait()


def coefficients(corner):
    linear = [corner[4] - corner[0], corner[2] - corner[0], corner[1] - corner[0]]
    pair_01 = corner[6] - corner[4] - linear[1]
    pair_02 = corner[5] - corner[4] - linear[2]
    pair_12 = corner[3] - corner[2] - linear[2]
    triple = (corner[7] - corner[6]) - (corner[5] - corner[4]) - pair_12
    return corner[0], linear, pair_01, pair_02, pair_12, triple


def solve(corner, target):
    polys = []
    for component in range(3):
        start, linear, pair_01, pair_02, pair_12, triple = coefficients(
            [corner(q, component) for q in range(8)]
        )
        linear[component] = linear[component] + 1.0
        polys.append((start - target[component], linear, pair_01, pair_02, pair_12, triple))
    s0 = s1 = s2 = jnp.full(target[0].shape, 0.5, jnp.float32)
    for _ in range(4):
        s01, s02, s12 = s0 * s1, s0 * s2, s1 * s2
        misfit, jac = [], []
        for start, (l0, l1, l2), p01, p02, p12, triple in polys:
            d0 = l0 + s1 * p01 + s2 * p02 + s12 * triple
            d1 = l1 + s0 * p01 + s2 * p12 + s02 * triple
            d2 = l2 + s0 * p02 + s1 * p12 + s01 * triple
            misfit.append(start + s0 * d0 + s1 * (l1 + s2 * p12) + s2 * l2)
            jac.append((d0, d1, d2))
        (a0, a1, a2), (b0, b1, b2), (c0, c1, c2) = jac
        m0, m1, m2 = misfit
        bc12 = b1 * c2 - b2 * c1
        bc02 = b0 * c2 - b2 * c0
        bc01 = b0 * c1 - b1 * c0
        det = a0 * bc12 - a1 * bc02 + a2 * bc01
        bm2 = m1 * c2 - b2 * m2
        bm1 = m1 * c1 - b1 * m2
        bm0 = b0 * m2 - m1 * c0
        inverse = 1.0 / det
        u0 = m0 * bc12 - a1 * bm2 + a2 * bm1
        u1 = a0 * bm2 - m0 * bc02 + a2 * bm0
        u2 = a0 * (b1 * m2 - m1 * c1) - a1 * bm0 + m0 * bc01
        s0 = s0 - u0 * inverse
        s1 = s1 - u1 * inverse
        s2 = s2 - u2 * inverse
    values = []
    for variable in range(5):
        u = [corner(q, 3 + variable) for q in range(8)]
        e = [u[q] + s2 * (u[q + 1] - u[q]) for q in (0, 2, 4, 6)]
        f = [e[q] + s1 * (e[q + 1] - e[q]) for q in (0, 2)]
        values.append(f[0] + s0 * (f[1] - f[0]))
    return values


def table_kernel(
    field_ref, jitter_ref, next_ref, below_ref, table_ref, rows_ref, field, jitter, sem
):
    variables, planes, rows_count, columns = field_ref.shape
    copies = [
        pltpu.make_async_copy(field_ref, field, sem.at[0]),
        pltpu.make_async_copy(jitter_ref, jitter, sem.at[1]),
    ]
    for copy in copies:
        copy.start()

    def one_plane(plane, read):
        for half in range(2):
            tile = jnp.concatenate([read(4 * half + w) for w in range(4)], 0).T
            first = plane * (2 * columns) + half
            table_ref[pl.ds(first, columns, stride=2), :] = tile

    def put(plane, variable, tile):
        first = plane * rows_count * 8 + variable
        rows_ref[pl.ds(first, rows_count, stride=8), :] = tile

    one_plane(planes, lambda v: next_ref[v, 0])
    for variable in range(variables):
        put(0, variable, below_ref[variable, 0])
        put(planes + 1, variable, next_ref[3 + variable, 0])
    for plane in range(planes):
        put(plane + 1, variables, jnp.zeros((rows_count, columns), jnp.float32))
    for copy in copies:
        copy.wait()
    for plane in range(planes):
        one_plane(plane, lambda v: jitter[v, plane] if v < 3 else field[v - 3, plane])
        for variable in range(variables):
            put(plane + 1, variable, field[variable, plane])


def separated(tiles, lane):
    for bit, distance in ((0, 1), (1, 32), (2, 64)):
        low = (lane & distance) == 0
        result = list(tiles)
        for a in range(8):
            b = a | (1 << bit)
            if a == b:
                continue
            result[a] = jnp.where(low, tiles[a], pltpu.roll(tiles[b], distance, 1))
            result[b] = jnp.where(low, pltpu.roll(tiles[a], LANES - distance, 1), tiles[b])
        tiles = result
    return tiles


def tile_rows(tile):
    first = tile * ROWS
    return pl.ds(first if isinstance(first, int) else pl.multiple_of(first, ROWS), ROWS)


def each_source(owners, body):
    if owners <= 8:
        for source in range(owners + 1):
            body(source, 0)
    else:
        lax.fori_loop(0, owners + 1, body, 0)


def gather_kernel(owners, table_ref, message_ref, out_ref, decoded, codes, picked, parts, sem):
    rows_count = 32
    me = lax.axis_index("grid")
    heavy = lax.rem(me + owners - 1, owners)
    lane = lax.broadcasted_iota(jnp.int32, (ROWS, LANES), 1)
    sublane = lax.broadcasted_iota(jnp.int32, (ROWS, LANES), 0)

    def decode(cells, place):
        cells = cells.astype(jnp.int32)
        row = (cells >> 12) * (2 * LANES) + (cells & 127) * 2
        shift = ((lane & 30) - ((cells >> 7) & (rows_count - 1))) & 127
        decoded[place, :] = row * LANES + shift

    for block in range(owners // ROWS):
        cells = message_ref[pl.ds(block * ROWS * 8, ROWS, stride=8), :]
        decode(cells, pl.ds(block * ROWS, ROWS))
    more = jnp.broadcast_to(message_ref[pl.ds(heavy * 8 + 4, 1), :], (ROWS, LANES))
    decode(more, pl.ds(owners, ROWS))
    copy = pltpu.make_async_copy(decoded, codes, sem)
    copy.start()
    copy.wait()

    low = sublane < 4
    pairs = [(lane & 30) == 2 * k for k in range(16)]

    def one_source(source, carry):
        for block in range(4):
            held = [None, None]
            for k in range(32):
                code = codes[source, block * 32 + k]
                row = code >> 7
                tile = jnp.where(
                    low,
                    table_ref[pl.ds(row, ROWS), :],
                    table_ref[pl.ds(row + (2 * LANES - 4), ROWS), :],
                )
                tile = pltpu.roll(tile, code & 127, 1)
                k2 = k & 1
                held[k2] = tile if held[k2] is None else jnp.where(pairs[k >> 1], tile, held[k2])
            for k in range(2):
                picked[tile_rows((2 * block + k) * (owners + 1) + source), :] = held[k]
        return carry

    each_source(owners, one_source)

    def one_block(block, last):
        for s in range(8):
            tiles = [
                picked[pl.ds((g * (owners + 1) + block * ROWS) * 8 + s, ROWS, stride=8), :]
                for g in range(8)
            ]
            for x, tile in enumerate(separated(tiles, lane)):
                parts[s, x] = tile
        if last:
            tiles = [picked[pl.ds((g * (owners + 1) + owners) * 8, 8), :] for g in range(8)]
            for x, tile in enumerate(separated(tiles, lane)):
                parts[8, x] = tile

        def corner(q, variable):
            a0, a1, a2 = q >> 2, (q >> 1) & 1, q & 1
            s, x = 4 * a0 + 2 * a2 + (variable >> 2), 2 * (variable & 3) + a1
            tile = parts[s, x]
            if last:
                more = jnp.broadcast_to(parts[8, x, s : s + 1, :], (ROWS, LANES))
                tile = jnp.concatenate([tile, more], 0)
            return tile

        target = []
        for c in range(3):
            tile = message_ref[pl.ds(block * (ROWS * 8) + 1 + c, ROWS, stride=8), :]
            if last:
                more = message_ref[pl.ds(heavy * 8 + 5 + c, 1), :]
                tile = jnp.concatenate([tile, jnp.broadcast_to(more, (ROWS, LANES))], 0)
            target.append(tile)
        values = solve(corner, target)
        for variable in range(5):
            place = pl.ds(block * (ROWS * 16) + variable, ROWS, stride=16)
            out_ref[place, :] = values[variable][:ROWS]
            if last:
                out_ref[pl.ds(heavy * 16 + 8 + variable, 1), :] = values[variable][ROWS : ROWS + 1]

    for block in range(owners // ROWS):
        one_block(block, block == owners // ROWS - 1)


def relax_kernel(
    owners, rows_ref, code_ref, ratio_ref, values_ref, out_ref, table, codes, rolled, out_vmem,
    sem, out_sem,
):
    variables, planes, rows_count, _ = out_ref.shape
    width = 8
    blocks = rows_count // ROWS
    plane_rows = rows_count * width
    copy = pltpu.make_async_copy(code_ref, codes, sem)
    copy.start()
    lane = lax.broadcasted_iota(jnp.int32, (ROWS, LANES), 1)
    sublane = lax.broadcasted_iota(jnp.int32, (ROWS, LANES), 0)
    heavy = lax.rem(lax.axis_index("grid") + 1, owners)
    for plane in range(planes + 2):
        place = pl.ds(plane * plane_rows, plane_rows)
        table[place, :] = rows_ref[place, :]
    copy.wait()

    def rotate(source, half):
        if isinstance(source, int):
            first = 16 * source if source < owners else heavy * 16 + 8
        else:
            first = jnp.where(source == owners, heavy * 16 + 8, source * 16)
        if not isinstance(first, int):
            first = pl.multiple_of(first, 8)
        tile = jnp.where(sublane == variables, 1.0, values_ref[pl.ds(first, 8), :])
        tile = jnp.where(sublane == variables + 1, lane.astype(jnp.float32), tile)
        for point in range(LANES):
            place = (half * LANES + point) * ROWS
            rolled[place : place + ROWS, :] = pltpu.roll(tile, codes[1, source, point], 1)

    def store(source, half):
        for point in range(LANES):
            place = (half * LANES + point) * ROWS
            tag = rolled[place + variables + 1 : place + variables + 2, :]
            row = pl.multiple_of(codes[0, source, point] + plane_rows, width)
            pltpu.store(
                table.at[pl.ds(row, width), :],
                rolled[place : place + ROWS, :],
                mask=jnp.broadcast_to(tag, (ROWS, LANES)) == float(point),
            )

    if owners <= 8:
        rotate(0, 0)
        for source in range(owners + 1):
            if source < owners:
                rotate(source + 1, (source + 1) % 2)
            store(source, source % 2)
    else:

        def one_source(source, carry):
            rotate(source, 0)
            store(source, 0)
            return carry

        lax.fori_loop(0, owners + 1, one_source, 0)

    def out_copy(plane):
        return pltpu.make_async_copy(
            out_vmem.at[:, pl.ds(plane, 1)], out_ref.at[:, pl.ds(plane, 1)], out_sem.at[plane]
        )

    def one_plane(plane):
        for block in range(blocks):
            ratio = ratio_ref[plane, pl.ds(block * ROWS, ROWS), :]
            inverse = 1.0 / (1.0 + 6.0 * ratio)
            base = (plane + 1) * plane_rows + block * ROWS * width

            def get(step, variable):
                return table[pl.ds(base + step * width + variable, ROWS, stride=width), :]

            fringe = get(0, variables) > 0.5
            for variable in range(variables):
                here = get(0, variable)
                up, down = get(1, variable), get(-1, variable)
                if block == 0:
                    down = jnp.where(sublane == 0, 0.0, down)
                if block == blocks - 1:
                    up = jnp.where(sublane == ROWS - 1, 0.0, up)
                right = jnp.where(lane == LANES - 1, 0.0, pltpu.roll(here, LANES - 1, 1))
                left = jnp.where(lane == 0, 0.0, pltpu.roll(here, 1, 1))
                total = get(rows_count, variable) + get(-rows_count, variable)
                total = total + up + down + right + left
                smooth = (here + ratio * total) * inverse
                out_vmem[variable, plane, pl.ds(block * ROWS, ROWS), :] = jnp.where(
                    fringe, here, smooth
                )
        out_copy(plane).start()

    for plane in range(planes):
        one_plane(plane)
    for plane in range(planes):
        out_copy(plane).wait()


def on_device(
    field, node_jitter, time_ratio, donor_cell, receptor_offset, receptor_node, point_count
):
    variables, planes, rows_count, cols_count = field.shape
    owners, points = donor_cell.shape[1], donor_cell.shape[3]
    params = pltpu.CompilerParams(vmem_limit_bytes=LIMIT)
    offsets = jnp.swapaxes(receptor_offset, 2, 3)
    field, node_jitter = (
        pltpu.with_memory_space_constraint(x, pltpu.HBM) for x in (field, node_jitter)
    )
    f32, i32 = jnp.float32, jnp.int32
    message, codes, first, last = pl.pallas_call(
        first_kernel,
        out_shape=[
            jax.ShapeDtypeStruct((owners, 8, LANES), f32),
            jax.ShapeDtypeStruct((2, owners + 8, LANES), i32),
            jax.ShapeDtypeStruct((3 + variables, 1, rows_count, cols_count), f32),
            jax.ShapeDtypeStruct((variables, 1, rows_count, cols_count), f32),
        ],
        in_specs=[HBM] * 6,
        out_specs=[VMEM] * 4,
        scratch_shapes=[
            pltpu.SMEM(point_count.shape, i32),
            pltpu.VMEM(donor_cell.shape, i32),
            pltpu.VMEM(offsets.shape, f32),
            pltpu.VMEM(receptor_node.shape, i32),
            pltpu.SemaphoreType.DMA((7,)),
        ],
        compiler_params=params,
        name="first",
    )(*[
        pltpu.with_memory_space_constraint(x, pltpu.HBM)
        for x in (point_count, donor_cell, offsets, receptor_node)
    ], field, node_jitter)
    following = passed_along(first, "sub", -1)
    below = passed_along(last, "sub", 1)
    message = lax.all_to_all(message, "grid", split_axis=0, concat_axis=0, tiled=True)
    sweep_rows = (planes + 2) * rows_count * 8
    table, rows = pl.pallas_call(
        table_kernel,
        out_shape=[
            jax.ShapeDtypeStruct(((planes + 1) * cols_count * 2, LANES), f32),
            jax.ShapeDtypeStruct((sweep_rows, LANES), f32),
        ],
        in_specs=[HBM, HBM, VMEM, VMEM],
        out_specs=[VMEM, VMEM],
        scratch_shapes=[
            pltpu.VMEM(field.shape, f32),
            pltpu.VMEM(node_jitter.shape, f32),
            pltpu.SemaphoreType.DMA((2,)),
        ],
        compiler_params=params,
        cost_estimate=pl.CostEstimate(flops=0, bytes_accessed=8 << 20, transcendentals=0),
        name="table",
    )(field, node_jitter, following, below)
    values = pl.pallas_call(
        functools.partial(gather_kernel, owners),
        out_shape=jax.ShapeDtypeStruct((owners * 16, LANES), f32),
        in_specs=[VMEM, VMEM],
        out_specs=VMEM,
        scratch_shapes=[
            pltpu.VMEM((owners + 8, LANES), i32),
            pltpu.SMEM((owners + 8, LANES), i32),
            pltpu.VMEM((8 * (owners + 1) * 8, LANES), f32),
            pltpu.VMEM((9, 8, ROWS, LANES), f32),
            pltpu.SemaphoreType.DMA,
        ],
        compiler_params=params,
        name="gather",
    )(table, message.reshape(owners * 8, LANES))
    values = values.reshape(owners, 16, LANES)
    values = lax.all_to_all(values, "grid", split_axis=0, concat_axis=0, tiled=True)
    return pl.pallas_call(
        functools.partial(relax_kernel, owners),
        out_shape=jax.ShapeDtypeStruct(field.shape, f32),
        in_specs=[VMEM] * 4,
        out_specs=HBM,
        scratch_shapes=[
            pltpu.VMEM((sweep_rows + 8, LANES), f32),
            pltpu.SMEM(codes.shape, i32),
            pltpu.VMEM((2 * LANES * ROWS, LANES), f32),
            pltpu.VMEM(field.shape, f32),
            pltpu.SemaphoreType.DMA,
            pltpu.SemaphoreType.DMA((planes,)),
        ],
        compiler_params=params,
        name="relax",
    )(rows, codes, time_ratio, values.reshape(owners * 16, LANES))


def solution(mesh):
    placed = (
        P(None, ("grid", "sub"), None, None),
        P(None, ("grid", "sub"), None, None),
        P(("grid", "sub"), None, None),
        P(("grid", "sub"), None, None, None),
        P(("grid", "sub"), None, None, None, None),
        P(("grid", "sub"), None, None, None),
        P(("grid", "sub"), None),
    )
    return jax.shard_map(
        on_device,
        mesh=mesh,
        in_specs=placed,
        out_specs=P(None, ("grid", "sub"), None, None),
        check_vma=False,
    )
```

```python
import functools

import jax
import jax.numpy as jnp
from jax import lax
from jax.experimental import pallas as pl
from jax.experimental.pallas import tpu as pltpu
from jax.sharding import PartitionSpec as P

ROWS = 8
LANES = 128
VMEM = pl.BlockSpec(memory_space=pltpu.VMEM)
HBM = pl.BlockSpec(memory_space=pltpu.HBM)
LIMIT = 24 << 20


def passed_along(value, axis, steps):
    count = lax.axis_size(axis)
    pairs = [(source, (source + steps) % count) for source in range(count)]
    return lax.ppermute(value, axis, pairs)


def first_kernel(
    count_ref, cell_ref, offset_ref, node_ref, field_ref, jitter_ref,
    message_ref, code_ref, next_ref, last_ref,
    count_smem, cell_vmem, offset_vmem, node_vmem, sem,
):
    owners, points = cell_ref.shape[1], cell_ref.shape[3]
    variables, planes, rows_count, _ = field_ref.shape
    copies = [
        pltpu.make_async_copy(source, target, sem.at[k])
        for k, (source, target) in enumerate(
            (
                (count_ref, count_smem),
                (cell_ref, cell_vmem),
                (offset_ref, offset_vmem),
                (node_ref, node_vmem),
                (jitter_ref.at[:, pl.ds(0, 1)], next_ref.at[pl.ds(0, 3)]),
                (field_ref.at[:, pl.ds(0, 1)], next_ref.at[pl.ds(3, variables)]),
                (field_ref.at[:, pl.ds(planes - 1, 1)], last_ref),
            )
        )
    ]
    for copy in copies:
        copy.start()
    for copy in copies[:4]:
        copy.wait()

    spare = (planes + 1) * rows_count * 8
    lane = lax.broadcasted_iota(jnp.int32, (1, points), 1)

    def code(place, nodes, live):
        code_ref[pl.ds(place, 1), :] = jnp.where(live, (nodes >> 7) * 8, spare)
        code_ref[pl.ds(owners + 1 + place, 1), :] = ((nodes & 127) - lane) & 127

    def one(owner, carry):
        count = count_smem[0, owner]
        more = count > points
        cells = cell_vmem[0, owner].astype(jnp.float32)
        counts = jnp.full((1, points), count, jnp.int32).astype(jnp.float32)
        message_ref[owner, 0:1, :] = cells[0:1]
        message_ref[owner, 4:5, :] = jnp.where(more, cells[1:2], counts)
        for c in range(3):
            message_ref[owner, 1 + c : 2 + c, :] = offset_vmem[0, owner, c, 0:1, :]
            message_ref[owner, 5 + c : 6 + c, :] = offset_vmem[0, owner, c, 1:2, :]
        nodes = node_vmem[0, owner]
        code(owner, nodes[0:1], lane < count)

        @pl.when(more)
        def _():
            code(owners, nodes[1:2], lane + points < count)

        return carry

    lax.fori_loop(0, owners, one, 0, unroll=True)
    for copy in copies[4:]:
        copy.wait()


def coefficients(corner):
    linear = [corner[4] - corner[0], corner[2] - corner[0], corner[1] - corner[0]]
    pair_01 = corner[6] - corner[4] - linear[1]
    pair_02 = corner[5] - corner[4] - linear[2]
    pair_12 = corner[3] - corner[2] - linear[2]
    triple = (corner[7] - corner[6]) - (corner[5] - corner[4]) - pair_12
    return corner[0], linear, pair_01, pair_02, pair_12, triple


def solve(corner, target):
    polys = []
    for component in range(3):
        start, linear, pair_01, pair_02, pair_12, triple = coefficients(
            [corner(q, component) for q in range(8)]
        )
        linear[component] = linear[component] + 1.0
        polys.append((start - target[component], linear, pair_01, pair_02, pair_12, triple))
    s0 = s1 = s2 = jnp.full(target[0].shape, 0.5, jnp.float32)
    for _ in range(4):
        s01, s02, s12 = s0 * s1, s0 * s2, s1 * s2
        misfit, jac = [], []
        for start, (l0, l1, l2), p01, p02, p12, triple in polys:
            d0 = l0 + s1 * p01 + s2 * p02 + s12 * triple
            d1 = l1 + s0 * p01 + s2 * p12 + s02 * triple
            d2 = l2 + s0 * p02 + s1 * p12 + s01 * triple
            misfit.append(start + s0 * d0 + s1 * (l1 + s2 * p12) + s2 * l2)
            jac.append((d0, d1, d2))
        (a0, a1, a2), (b0, b1, b2), (c0, c1, c2) = jac
        m0, m1, m2 = misfit
        bc12 = b1 * c2 - b2 * c1
        bc02 = b0 * c2 - b2 * c0
        bc01 = b0 * c1 - b1 * c0
        det = a0 * bc12 - a1 * bc02 + a2 * bc01
        bm2 = m1 * c2 - b2 * m2
        bm1 = m1 * c1 - b1 * m2
        bm0 = b0 * m2 - m1 * c0
        inverse = 1.0 / det
        u0 = m0 * bc12 - a1 * bm2 + a2 * bm1
        u1 = a0 * bm2 - m0 * bc02 + a2 * bm0
        u2 = a0 * (b1 * m2 - m1 * c1) - a1 * bm0 + m0 * bc01
        s0 = s0 - u0 * inverse
        s1 = s1 - u1 * inverse
        s2 = s2 - u2 * inverse
    values = []
    for variable in range(5):
        u = [corner(q, 3 + variable) for q in range(8)]
        e = [u[q] + s2 * (u[q + 1] - u[q]) for q in (0, 2, 4, 6)]
        f = [e[q] + s1 * (e[q + 1] - e[q]) for q in (0, 2)]
        values.append(f[0] + s0 * (f[1] - f[0]))
    return values


def lay_out(table, field_ref, jitter_ref, next_ref):
    planes, columns = field_ref.shape[1], field_ref.shape[3]

    def read(plane, variable):
        if plane == planes:
            return next_ref[variable, 0]
        return jitter_ref[variable, plane] if variable < 3 else field_ref[variable - 3, plane]

    for plane in range(planes + 1):
        for half in range(2):
            tile = jnp.concatenate([read(plane, 4 * half + w) for w in range(4)], 0).T
            first = plane * (2 * columns) + half
            table[pl.ds(first, columns, stride=2), :] = tile


def separated(tiles, lane):
    for bit, distance in ((0, 1), (1, 32), (2, 64)):
        low = (lane & distance) == 0
        result = list(tiles)
        for a in range(8):
            b = a | (1 << bit)
            if a == b:
                continue
            result[a] = jnp.where(low, tiles[a], pltpu.roll(tiles[b], distance, 1))
            result[b] = jnp.where(low, pltpu.roll(tiles[a], LANES - distance, 1), tiles[b])
        tiles = result
    return tiles


def tile_rows(tile):
    first = tile * ROWS
    return pl.ds(first if isinstance(first, int) else pl.multiple_of(first, ROWS), ROWS)


def each_source(owners, body):
    if owners <= 8:
        for source in range(owners + 1):
            body(source, 0)
    else:
        lax.fori_loop(0, owners + 1, body, 0)


def gather_kernel(
    owners, field_ref, jitter_ref, next_ref, message_ref, out_ref,
    table, decoded, codes, picked, parts, sem,
):
    rows_count = 32
    me = lax.axis_index("grid")
    heavy = lax.rem(me + owners - 1, owners)
    lane = lax.broadcasted_iota(jnp.int32, (ROWS, LANES), 1)
    sublane = lax.broadcasted_iota(jnp.int32, (ROWS, LANES), 0)

    def decode(cells, place):
        cells = cells.astype(jnp.int32)
        row = (cells >> 12) * (2 * LANES) + (cells & 127) * 2
        shift = ((lane & 30) - ((cells >> 7) & (rows_count - 1))) & 127
        decoded[place, :] = row * LANES + shift

    for block in range(owners // ROWS):
        cells = message_ref[pl.ds(block * ROWS * 8, ROWS, stride=8), :]
        decode(cells, pl.ds(block * ROWS, ROWS))
    more = jnp.broadcast_to(message_ref[pl.ds(heavy * 8 + 4, 1), :], (ROWS, LANES))
    decode(more, pl.ds(owners, ROWS))
    copy = pltpu.make_async_copy(decoded, codes, sem)
    copy.start()
    lay_out(table, field_ref, jitter_ref, next_ref)
    copy.wait()

    low = sublane < 4
    pairs = [(lane & 30) == 2 * k for k in range(16)]

    def one_source(source, carry):
        for block in range(4):
            held = [None, None]
            for k in range(32):
                code = codes[source, block * 32 + k]
                row = code >> 7
                tile = jnp.where(
                    low,
                    table[pl.ds(row, ROWS), :],
                    table[pl.ds(row + (2 * LANES - 4), ROWS), :],
                )
                tile = pltpu.roll(tile, code & 127, 1)
                k2 = k & 1
                held[k2] = tile if held[k2] is None else jnp.where(pairs[k >> 1], tile, held[k2])
            for k in range(2):
                picked[tile_rows((2 * block + k) * (owners + 1) + source), :] = held[k]
        return carry

    each_source(owners, one_source)

    def one_block(block, last):
        for s in range(8):
            tiles = [
                picked[pl.ds((g * (owners + 1) + block * ROWS) * 8 + s, ROWS, stride=8), :]
                for g in range(8)
            ]
            for x, tile in enumerate(separated(tiles, lane)):
                parts[s, x] = tile
        if last:
            tiles = [picked[pl.ds((g * (owners + 1) + owners) * 8, 8), :] for g in range(8)]
            for x, tile in enumerate(separated(tiles, lane)):
                parts[8, x] = tile

        def corner(q, variable):
            a0, a1, a2 = q >> 2, (q >> 1) & 1, q & 1
            s, x = 4 * a0 + 2 * a2 + (variable >> 2), 2 * (variable & 3) + a1
            tile = parts[s, x]
            if last:
                more = jnp.broadcast_to(parts[8, x, s : s + 1, :], (ROWS, LANES))
                tile = jnp.concatenate([tile, more], 0)
            return tile

        target = []
        for c in range(3):
            tile = message_ref[pl.ds(block * (ROWS * 8) + 1 + c, ROWS, stride=8), :]
            if last:
                more = message_ref[pl.ds(heavy * 8 + 5 + c, 1), :]
                tile = jnp.concatenate([tile, jnp.broadcast_to(more, (ROWS, LANES))], 0)
            target.append(tile)
        values = solve(corner, target)
        for variable in range(5):
            place = pl.ds(block * (ROWS * 16) + variable, ROWS, stride=16)
            out_ref[place, :] = values[variable][:ROWS]
            if last:
                out_ref[pl.ds(heavy * 16 + 8 + variable, 1), :] = values[variable][ROWS : ROWS + 1]

    for block in range(owners // ROWS):
        one_block(block, block == owners // ROWS - 1)


def relax_kernel(
    owners, code_ref, field_ref, next_ref, below_ref, ratio_ref, values_ref, out_ref,
    table, codes, rolled, out_vmem, sem, out_sem,
):
    variables, planes, rows_count, _ = out_ref.shape
    width = 8
    blocks = rows_count // ROWS
    plane_rows = rows_count * width
    copy = pltpu.make_async_copy(code_ref, codes, sem)
    copy.start()
    lane = lax.broadcasted_iota(jnp.int32, (ROWS, LANES), 1)
    sublane = lax.broadcasted_iota(jnp.int32, (ROWS, LANES), 0)
    heavy = lax.rem(lax.axis_index("grid") + 1, owners)

    def put(plane, variable, tile):
        table[pl.ds(plane * plane_rows + variable, rows_count, stride=width), :] = tile

    for variable in range(variables):
        put(0, variable, below_ref[variable, 0])
        put(planes + 1, variable, next_ref[3 + variable, 0])
        for plane in range(planes):
            put(plane + 1, variable, field_ref[variable, plane])
    for plane in range(planes):
        put(plane + 1, variables, jnp.zeros((rows_count, LANES), jnp.float32))
    copy.wait()

    def rotate(source, half):
        if isinstance(source, int):
            first = 16 * source if source < owners else heavy * 16 + 8
        else:
            first = jnp.where(source == owners, heavy * 16 + 8, source * 16)
        if not isinstance(first, int):
            first = pl.multiple_of(first, 8)
        tile = jnp.where(sublane == variables, 1.0, values_ref[pl.ds(first, 8), :])
        tile = jnp.where(sublane == variables + 1, lane.astype(jnp.float32), tile)
        for point in range(LANES):
            place = (half * LANES + point) * ROWS
            rolled[place : place + ROWS, :] = pltpu.roll(tile, codes[owners + 1 + source, point], 1)

    def store(source, half):
        for point in range(LANES):
            place = (half * LANES + point) * ROWS
            tag = rolled[place + variables + 1 : place + variables + 2, :]
            row = pl.multiple_of(codes[source, point] + plane_rows, width)
            pltpu.store(
                table.at[pl.ds(row, width), :],
                rolled[place : place + ROWS, :],
                mask=jnp.broadcast_to(tag, (ROWS, LANES)) == float(point),
            )

    if owners <= 8:
        rotate(0, 0)
        for source in range(owners + 1):
            if source < owners:
                rotate(source + 1, source + 1)
            store(source, source)
    else:

        def one_source(source, carry):
            rotate(source, 0)
            store(source, 0)
            return carry

        lax.fori_loop(0, owners + 1, one_source, 0)

    def out_copy(plane):
        return pltpu.make_async_copy(
            out_vmem.at[:, pl.ds(plane, 1)], out_ref.at[:, pl.ds(plane, 1)], out_sem.at[plane]
        )

    def one_plane(plane):
        for block in range(blocks):
            ratio = ratio_ref[plane, pl.ds(block * ROWS, ROWS), :]
            inverse = 1.0 / (1.0 + 6.0 * ratio)
            base = (plane + 1) * plane_rows + block * ROWS * width

            def get(step, variable):
                return table[pl.ds(base + step * width + variable, ROWS, stride=width), :]

            fringe = get(0, variables) > 0.5
            for variable in range(variables):
                here = get(0, variable)
                up, down = get(1, variable), get(-1, variable)
                if block == 0:
                    down = jnp.where(sublane == 0, 0.0, down)
                if block == blocks - 1:
                    up = jnp.where(sublane == ROWS - 1, 0.0, up)
                right = jnp.where(lane == LANES - 1, 0.0, pltpu.roll(here, LANES - 1, 1))
                left = jnp.where(lane == 0, 0.0, pltpu.roll(here, 1, 1))
                total = get(rows_count, variable) + get(-rows_count, variable)
                total = total + up + down + right + left
                smooth = (here + ratio * total) * inverse
                out_vmem[variable, plane, pl.ds(block * ROWS, ROWS), :] = jnp.where(
                    fringe, here, smooth
                )
        out_copy(plane).start()

    for plane in range(planes):
        one_plane(plane)
    for plane in range(planes):
        out_copy(plane).wait()


def on_device(
    field, node_jitter, time_ratio, donor_cell, receptor_offset, receptor_node, point_count
):
    variables, planes, rows_count, cols_count = field.shape
    owners, points = donor_cell.shape[1], donor_cell.shape[3]
    params = pltpu.CompilerParams(vmem_limit_bytes=LIMIT)
    offsets = jnp.swapaxes(receptor_offset, 2, 3)
    f32, i32 = jnp.float32, jnp.int32
    message, codes, first, last = pl.pallas_call(
        first_kernel,
        out_shape=[
            jax.ShapeDtypeStruct((owners, 8, LANES), f32),
            jax.ShapeDtypeStruct((2 * owners + 8, LANES), i32),
            jax.ShapeDtypeStruct((3 + variables, 1, rows_count, cols_count), f32),
            jax.ShapeDtypeStruct((variables, 1, rows_count, cols_count), f32),
        ],
        in_specs=[HBM] * 6,
        out_specs=[VMEM] * 4,
        scratch_shapes=[
            pltpu.SMEM(point_count.shape, i32),
            pltpu.VMEM(donor_cell.shape, i32),
            pltpu.VMEM(offsets.shape, f32),
            pltpu.VMEM(receptor_node.shape, i32),
            pltpu.SemaphoreType.DMA((7,)),
        ],
        compiler_params=params,
        name="first",
    )(*[
        pltpu.with_memory_space_constraint(x, pltpu.HBM)
        for x in (point_count, donor_cell, offsets, receptor_node, field, node_jitter)
    ])
    field, node_jitter, time_ratio, message = lax.optimization_barrier(
        (field, node_jitter, time_ratio, message)
    )
    following = passed_along(first, "sub", -1)
    below = passed_along(last, "sub", 1)
    message = lax.all_to_all(message, "grid", split_axis=0, concat_axis=0, tiled=True)
    values = pl.pallas_call(
        functools.partial(gather_kernel, owners),
        out_shape=jax.ShapeDtypeStruct((owners * 16, LANES), f32),
        in_specs=[VMEM] * 4,
        out_specs=VMEM,
        scratch_shapes=[
            pltpu.VMEM(((planes + 1) * cols_count * 2, LANES), f32),
            pltpu.VMEM((owners + 8, LANES), i32),
            pltpu.SMEM((owners + 8, LANES), i32),
            pltpu.VMEM((8 * (owners + 1) * 8, LANES), f32),
            pltpu.VMEM((9, 8, ROWS, LANES), f32),
            pltpu.SemaphoreType.DMA,
        ],
        compiler_params=params,
        name="gather",
    )(field, node_jitter, following, message.reshape(owners * 8, LANES))
    values = values.reshape(owners, 16, LANES)
    values = lax.all_to_all(values, "grid", split_axis=0, concat_axis=0, tiled=True)
    return pl.pallas_call(
        functools.partial(relax_kernel, owners),
        out_shape=jax.ShapeDtypeStruct(field.shape, f32),
        in_specs=[VMEM] * 6,
        out_specs=HBM,
        scratch_shapes=[
            pltpu.VMEM(((planes + 2) * rows_count * 8 + 8, LANES), f32),
            pltpu.SMEM(codes.shape, i32),
            pltpu.VMEM(((owners + 1 if owners <= 8 else 1) * LANES * ROWS, LANES), f32),
            pltpu.VMEM(field.shape, f32),
            pltpu.SemaphoreType.DMA,
            pltpu.SemaphoreType.DMA((planes,)),
        ],
        compiler_params=params,
        name="relax",
    )(codes, field, following, below, time_ratio, values.reshape(owners * 16, LANES))


def solution(mesh):
    placed = (
        P(None, ("grid", "sub"), None, None),
        P(None, ("grid", "sub"), None, None),
        P(("grid", "sub"), None, None),
        P(("grid", "sub"), None, None, None),
        P(("grid", "sub"), None, None, None, None),
        P(("grid", "sub"), None, None, None),
        P(("grid", "sub"), None),
    )
    return jax.shard_map(
        on_device,
        mesh=mesh,
        in_specs=placed,
        out_specs=P(None, ("grid", "sub"), None, None),
        check_vma=False,
    )
```

```python
import functools

import jax
import jax.numpy as jnp
from jax import lax
from jax.experimental import pallas as pl
from jax.experimental.pallas import tpu as pltpu
from jax.sharding import PartitionSpec as P

ROWS = 8
LANES = 128
VMEM = pl.BlockSpec(memory_space=pltpu.VMEM)
HBM = pl.BlockSpec(memory_space=pltpu.HBM)
LIMIT = 24 << 20


def passed_along(value, axis, steps):
    count = lax.axis_size(axis)
    pairs = [(source, (source + steps) % count) for source in range(count)]
    return lax.ppermute(value, axis, pairs)


def first_kernel(
    count_ref, cell_ref, offset_ref, node_ref, field_ref, jitter_ref,
    message_ref, code_ref, next_ref, last_ref,
    count_smem, cell_vmem, offset_vmem, node_vmem, sem,
):
    owners, points = cell_ref.shape[1], cell_ref.shape[3]
    variables, planes, rows_count, _ = field_ref.shape
    copies = [
        pltpu.make_async_copy(source, target, sem.at[k])
        for k, (source, target) in enumerate(
            (
                (count_ref, count_smem),
                (cell_ref, cell_vmem),
                (offset_ref, offset_vmem),
                (node_ref, node_vmem),
                (jitter_ref.at[:, pl.ds(0, 1)], next_ref.at[pl.ds(0, 3)]),
                (field_ref.at[:, pl.ds(0, 1)], next_ref.at[pl.ds(3, variables)]),
                (field_ref.at[:, pl.ds(planes - 1, 1)], last_ref),
            )
        )
    ]
    for copy in copies:
        copy.start()
    for copy in copies[:4]:
        copy.wait()

    spare = (planes + 1) * rows_count * 8
    lane = lax.broadcasted_iota(jnp.int32, (1, points), 1)

    def code(place, nodes, live):
        code_ref[pl.ds(place, 1), :] = jnp.where(live, (nodes >> 7) * 8, spare)
        code_ref[pl.ds(owners + 1 + place, 1), :] = ((nodes & 127) - lane) & 127

    def one(owner, carry):
        count = count_smem[0, owner]
        more = count > points
        cells = cell_vmem[0, owner].astype(jnp.float32)
        counts = jnp.full((1, points), count, jnp.int32).astype(jnp.float32)
        message_ref[owner, 0:1, :] = cells[0:1]
        message_ref[owner, 4:5, :] = jnp.where(more, cells[1:2], counts)
        for c in range(3):
            message_ref[owner, 1 + c : 2 + c, :] = offset_vmem[0, owner, c, 0:1, :]
            message_ref[owner, 5 + c : 6 + c, :] = offset_vmem[0, owner, c, 1:2, :]
        nodes = node_vmem[0, owner]
        code(owner, nodes[0:1], lane < count)

        @pl.when(more)
        def _():
            code(owners, nodes[1:2], lane + points < count)

        return carry

    lax.fori_loop(0, owners, one, 0, unroll=True)
    for copy in copies[4:]:
        copy.wait()


def coefficients(corner):
    linear = [corner[4] - corner[0], corner[2] - corner[0], corner[1] - corner[0]]
    pair_01 = corner[6] - corner[4] - linear[1]
    pair_02 = corner[5] - corner[4] - linear[2]
    pair_12 = corner[3] - corner[2] - linear[2]
    triple = (corner[7] - corner[6]) - (corner[5] - corner[4]) - pair_12
    return corner[0], linear, pair_01, pair_02, pair_12, triple


def solve(corner, target):
    polys = []
    for component in range(3):
        start, linear, pair_01, pair_02, pair_12, triple = coefficients(
            [corner(q, component) for q in range(8)]
        )
        linear[component] = linear[component] + 1.0
        polys.append((start - target[component], linear, pair_01, pair_02, pair_12, triple))
    s0 = s1 = s2 = jnp.full(target[0].shape, 0.5, jnp.float32)
    for _ in range(4):
        s01, s02, s12 = s0 * s1, s0 * s2, s1 * s2
        misfit, jac = [], []
        for start, (l0, l1, l2), p01, p02, p12, triple in polys:
            d0 = l0 + s1 * p01 + s2 * p02 + s12 * triple
            d1 = l1 + s0 * p01 + s2 * p12 + s02 * triple
            d2 = l2 + s0 * p02 + s1 * p12 + s01 * triple
            misfit.append(start + s0 * d0 + s1 * (l1 + s2 * p12) + s2 * l2)
            jac.append((d0, d1, d2))
        (a0, a1, a2), (b0, b1, b2), (c0, c1, c2) = jac
        m0, m1, m2 = misfit
        bc12 = b1 * c2 - b2 * c1
        bc02 = b0 * c2 - b2 * c0
        bc01 = b0 * c1 - b1 * c0
        det = a0 * bc12 - a1 * bc02 + a2 * bc01
        bm2 = m1 * c2 - b2 * m2
        bm1 = m1 * c1 - b1 * m2
        bm0 = b0 * m2 - m1 * c0
        inverse = 1.0 / det
        u0 = m0 * bc12 - a1 * bm2 + a2 * bm1
        u1 = a0 * bm2 - m0 * bc02 + a2 * bm0
        u2 = a0 * (b1 * m2 - m1 * c1) - a1 * bm0 + m0 * bc01
        s0 = s0 - u0 * inverse
        s1 = s1 - u1 * inverse
        s2 = s2 - u2 * inverse
    values = []
    for variable in range(5):
        u = [corner(q, 3 + variable) for q in range(8)]
        e = [u[q] + s2 * (u[q + 1] - u[q]) for q in (0, 2, 4, 6)]
        f = [e[q] + s1 * (e[q + 1] - e[q]) for q in (0, 2)]
        values.append(f[0] + s0 * (f[1] - f[0]))
    return values


def lay_out(table, field_ref, jitter_ref, next_ref):
    planes, columns = field_ref.shape[1], field_ref.shape[3]

    def read(plane, variable):
        if plane == planes:
            return next_ref[variable, 0]
        return jitter_ref[variable, plane] if variable < 3 else field_ref[variable - 3, plane]

    for plane in range(planes + 1):
        for half in range(2):
            tile = jnp.concatenate([read(plane, 4 * half + w) for w in range(4)], 0).T
            first = plane * (2 * columns) + half
            table[pl.ds(first, columns, stride=2), :] = tile


def separated(tiles, lane):
    for bit, distance in ((0, 1), (1, 32), (2, 64)):
        low = (lane & distance) == 0
        result = list(tiles)
        for a in range(8):
            b = a | (1 << bit)
            if a == b:
                continue
            result[a] = jnp.where(low, tiles[a], pltpu.roll(tiles[b], distance, 1))
            result[b] = jnp.where(low, pltpu.roll(tiles[a], LANES - distance, 1), tiles[b])
        tiles = result
    return tiles


def tile_rows(tile):
    first = tile * ROWS
    return pl.ds(first if isinstance(first, int) else pl.multiple_of(first, ROWS), ROWS)


def after(me, body):
    def once(step, carry):
        body()
        return carry

    lax.fori_loop(0, jnp.minimum(me + 1, 1), once, 0)


def each_source(owners, body):
    if owners <= 8:
        for source in range(owners + 1):
            body(source, 0)
    else:
        lax.fori_loop(0, owners + 1, body, 0)


def gather_kernel(
    owners, field_ref, jitter_ref, next_ref, below_ref, message_ref, out_ref,
    table, decoded, codes, picked, parts, sem,
):
    rows_count = 32
    me = lax.axis_index("grid")
    heavy = lax.rem(me + owners - 1, owners)
    lane = lax.broadcasted_iota(jnp.int32, (ROWS, LANES), 1)
    sublane = lax.broadcasted_iota(jnp.int32, (ROWS, LANES), 0)

    def decode(cells, place):
        cells = cells.astype(jnp.int32)
        row = (cells >> 12) * (2 * LANES) + (cells & 127) * 2
        shift = ((lane & 30) - ((cells >> 7) & (rows_count - 1))) & 127
        decoded[place, :] = row * LANES + shift

    for block in range(owners // ROWS):
        cells = message_ref[pl.ds(block * ROWS * 8, ROWS, stride=8), :]
        decode(cells, pl.ds(block * ROWS, ROWS))
    more = jnp.broadcast_to(message_ref[pl.ds(heavy * 8 + 4, 1), :], (ROWS, LANES))
    decode(more, pl.ds(owners, ROWS))
    copy = pltpu.make_async_copy(decoded, codes, sem)
    copy.start()
    after(me, lambda: lay_out(table, field_ref, jitter_ref, next_ref))
    copy.wait()

    low = sublane < 4
    pairs = [(lane & 30) == 2 * k for k in range(16)]

    def one_source(source, carry):
        for block in range(4):
            held = [None, None]
            for k in range(32):
                code = codes[source, block * 32 + k]
                row = code >> 7
                tile = jnp.where(
                    low,
                    table[pl.ds(row, ROWS), :],
                    table[pl.ds(row + (2 * LANES - 4), ROWS), :],
                )
                tile = pltpu.roll(tile, code & 127, 1)
                k2 = k & 1
                held[k2] = tile if held[k2] is None else jnp.where(pairs[k >> 1], tile, held[k2])
            for k in range(2):
                picked[tile_rows((2 * block + k) * (owners + 1) + source), :] = held[k]
        return carry

    each_source(owners, one_source)

    def one_block(block, last):
        for s in range(8):
            tiles = [
                picked[pl.ds((g * (owners + 1) + block * ROWS) * 8 + s, ROWS, stride=8), :]
                for g in range(8)
            ]
            for x, tile in enumerate(separated(tiles, lane)):
                parts[s, x] = tile
        if last:
            tiles = [picked[pl.ds((g * (owners + 1) + owners) * 8, 8), :] for g in range(8)]
            for x, tile in enumerate(separated(tiles, lane)):
                parts[8, x] = tile

        def corner(q, variable):
            a0, a1, a2 = q >> 2, (q >> 1) & 1, q & 1
            s, x = 4 * a0 + 2 * a2 + (variable >> 2), 2 * (variable & 3) + a1
            tile = parts[s, x]
            if last:
                more = jnp.broadcast_to(parts[8, x, s : s + 1, :], (ROWS, LANES))
                tile = jnp.concatenate([tile, more], 0)
            return tile

        target = []
        for c in range(3):
            tile = message_ref[pl.ds(block * (ROWS * 8) + 1 + c, ROWS, stride=8), :]
            if last:
                more = message_ref[pl.ds(heavy * 8 + 5 + c, 1), :]
                tile = jnp.concatenate([tile, jnp.broadcast_to(more, (ROWS, LANES))], 0)
            target.append(tile)
        values = solve(corner, target)
        for variable in range(5):
            place = pl.ds(block * (ROWS * 16) + variable, ROWS, stride=16)
            out_ref[place, :] = values[variable][:ROWS]
            if last:
                out_ref[pl.ds(heavy * 16 + 8 + variable, 1), :] = values[variable][ROWS : ROWS + 1]

    for block in range(owners // ROWS):
        one_block(block, block == owners // ROWS - 1)


def relax_kernel(
    owners, code_ref, field_ref, next_ref, below_ref, ratio_ref, values_ref, out_ref,
    table, codes, rolled, out_vmem, sem, out_sem,
):
    variables, planes, rows_count, _ = out_ref.shape
    width = 8
    blocks = rows_count // ROWS
    plane_rows = rows_count * width
    copy = pltpu.make_async_copy(code_ref, codes, sem)
    copy.start()
    lane = lax.broadcasted_iota(jnp.int32, (ROWS, LANES), 1)
    sublane = lax.broadcasted_iota(jnp.int32, (ROWS, LANES), 0)
    me = lax.axis_index("grid")
    heavy = lax.rem(me + 1, owners)

    def put(plane, variable, tile):
        table[pl.ds(plane * plane_rows + variable, rows_count, stride=width), :] = tile

    def put_all():
        for variable in range(variables):
            put(0, variable, below_ref[variable, 0])
            put(planes + 1, variable, next_ref[3 + variable, 0])
            for plane in range(planes):
                put(plane + 1, variable, field_ref[variable, plane])
        for plane in range(planes):
            put(plane + 1, variables, jnp.zeros((rows_count, LANES), jnp.float32))

    after(me, put_all)
    copy.wait()

    def rotate(source, half):
        if isinstance(source, int):
            first = 16 * source if source < owners else heavy * 16 + 8
        else:
            first = jnp.where(source == owners, heavy * 16 + 8, source * 16)
        if not isinstance(first, int):
            first = pl.multiple_of(first, 8)
        tile = jnp.where(sublane == variables, 1.0, values_ref[pl.ds(first, 8), :])
        tile = jnp.where(sublane == variables + 1, lane.astype(jnp.float32), tile)
        for point in range(LANES):
            place = (half * LANES + point) * ROWS
            rolled[place : place + ROWS, :] = pltpu.roll(tile, codes[owners + 1 + source, point], 1)

    def store(source, half):
        for point in range(LANES):
            place = (half * LANES + point) * ROWS
            tag = rolled[place + variables + 1 : place + variables + 2, :]
            row = pl.multiple_of(codes[source, point] + plane_rows, width)
            pltpu.store(
                table.at[pl.ds(row, width), :],
                rolled[place : place + ROWS, :],
                mask=jnp.broadcast_to(tag, (ROWS, LANES)) == float(point),
            )

    if owners <= 8:
        rotate(0, 0)
        for source in range(owners + 1):
            if source < owners:
                rotate(source + 1, source + 1)
            store(source, source)
    else:

        def one_source(source, carry):
            rotate(source, 0)
            store(source, 0)
            return carry

        lax.fori_loop(0, owners + 1, one_source, 0)

    def out_copy(plane):
        return pltpu.make_async_copy(
            out_vmem.at[:, pl.ds(plane, 1)], out_ref.at[:, pl.ds(plane, 1)], out_sem.at[plane]
        )

    def one_plane(plane):
        for block in range(blocks):
            ratio = ratio_ref[plane, pl.ds(block * ROWS, ROWS), :]
            inverse = 1.0 / (1.0 + 6.0 * ratio)
            base = (plane + 1) * plane_rows + block * ROWS * width

            def get(step, variable):
                return table[pl.ds(base + step * width + variable, ROWS, stride=width), :]

            fringe = get(0, variables) > 0.5
            for variable in range(variables):
                here = get(0, variable)
                up, down = get(1, variable), get(-1, variable)
                if block == 0:
                    down = jnp.where(sublane == 0, 0.0, down)
                if block == blocks - 1:
                    up = jnp.where(sublane == ROWS - 1, 0.0, up)
                right = jnp.where(lane == LANES - 1, 0.0, pltpu.roll(here, LANES - 1, 1))
                left = jnp.where(lane == 0, 0.0, pltpu.roll(here, 1, 1))
                total = get(rows_count, variable) + get(-rows_count, variable)
                total = total + up + down + right + left
                smooth = (here + ratio * total) * inverse
                out_vmem[variable, plane, pl.ds(block * ROWS, ROWS), :] = jnp.where(
                    fringe, here, smooth
                )
        out_copy(plane).start()

    for plane in range(planes):
        one_plane(plane)
    for plane in range(planes):
        out_copy(plane).wait()


def on_device(
    field, node_jitter, time_ratio, donor_cell, receptor_offset, receptor_node, point_count
):
    variables, planes, rows_count, cols_count = field.shape
    owners, points = donor_cell.shape[1], donor_cell.shape[3]
    params = pltpu.CompilerParams(vmem_limit_bytes=LIMIT)
    offsets = jnp.swapaxes(receptor_offset, 2, 3)
    f32, i32 = jnp.float32, jnp.int32
    message, codes, first, last = pl.pallas_call(
        first_kernel,
        out_shape=[
            jax.ShapeDtypeStruct((owners, 8, LANES), f32),
            jax.ShapeDtypeStruct((2 * owners + 8, LANES), i32),
            jax.ShapeDtypeStruct((3 + variables, 1, rows_count, cols_count), f32),
            jax.ShapeDtypeStruct((variables, 1, rows_count, cols_count), f32),
        ],
        in_specs=[HBM] * 6,
        out_specs=[VMEM] * 4,
        scratch_shapes=[
            pltpu.SMEM(point_count.shape, i32),
            pltpu.VMEM(donor_cell.shape, i32),
            pltpu.VMEM(offsets.shape, f32),
            pltpu.VMEM(receptor_node.shape, i32),
            pltpu.SemaphoreType.DMA((7,)),
        ],
        compiler_params=params,
        name="first",
    )(*[
        pltpu.with_memory_space_constraint(x, pltpu.HBM)
        for x in (point_count, donor_cell, offsets, receptor_node, field, node_jitter)
    ])
    following = passed_along(first, "sub", -1)
    below = passed_along(last, "sub", 1)
    message = lax.all_to_all(message, "grid", split_axis=0, concat_axis=0, tiled=True)
    values = pl.pallas_call(
        functools.partial(gather_kernel, owners),
        out_shape=jax.ShapeDtypeStruct((owners * 16, LANES), f32),
        in_specs=[VMEM] * 5,
        out_specs=VMEM,
        scratch_shapes=[
            pltpu.VMEM(((planes + 1) * cols_count * 2, LANES), f32),
            pltpu.VMEM((owners + 8, LANES), i32),
            pltpu.SMEM((owners + 8, LANES), i32),
            pltpu.VMEM((8 * (owners + 1) * 8, LANES), f32),
            pltpu.VMEM((9, 8, ROWS, LANES), f32),
            pltpu.SemaphoreType.DMA,
        ],
        compiler_params=params,
        name="gather",
    )(field, node_jitter, following, below, message.reshape(owners * 8, LANES))
    values = values.reshape(owners, 16, LANES)
    values = lax.all_to_all(values, "grid", split_axis=0, concat_axis=0, tiled=True)
    return pl.pallas_call(
        functools.partial(relax_kernel, owners),
        out_shape=jax.ShapeDtypeStruct(field.shape, f32),
        in_specs=[VMEM] * 6,
        out_specs=HBM,
        scratch_shapes=[
            pltpu.VMEM(((planes + 2) * rows_count * 8 + 8, LANES), f32),
            pltpu.SMEM(codes.shape, i32),
            pltpu.VMEM(((owners + 1 if owners <= 8 else 1) * LANES * ROWS, LANES), f32),
            pltpu.VMEM(field.shape, f32),
            pltpu.SemaphoreType.DMA,
            pltpu.SemaphoreType.DMA((planes,)),
        ],
        compiler_params=params,
        name="relax",
    )(codes, field, following, below, time_ratio, values.reshape(owners * 16, LANES))


def solution(mesh):
    placed = (
        P(None, ("grid", "sub"), None, None),
        P(None, ("grid", "sub"), None, None),
        P(("grid", "sub"), None, None),
        P(("grid", "sub"), None, None, None),
        P(("grid", "sub"), None, None, None, None),
        P(("grid", "sub"), None, None, None),
        P(("grid", "sub"), None),
    )
    return jax.shard_map(
        on_device,
        mesh=mesh,
        in_specs=placed,
        out_specs=P(None, ("grid", "sub"), None, None),
        check_vma=False,
    )
```

```python
import functools

import jax
import jax.numpy as jnp
from jax import lax
from jax.experimental import pallas as pl
from jax.experimental.pallas import tpu as pltpu
from jax.sharding import PartitionSpec as P

ROWS = 8
LANES = 128
VMEM = pl.BlockSpec(memory_space=pltpu.VMEM)
HBM = pl.BlockSpec(memory_space=pltpu.HBM)
LIMIT = 24 << 20


def passed_along(value, axis, steps):
    count = lax.axis_size(axis)
    pairs = [(source, (source + steps) % count) for source in range(count)]
    return lax.ppermute(value, axis, pairs)


def first_kernel(
    count_ref, cell_ref, offset_ref, node_ref, field_ref, jitter_ref,
    message_ref, code_ref, next_ref, last_ref,
    count_smem, cell_vmem, offset_vmem, node_vmem, sem,
):
    owners, points = cell_ref.shape[1], cell_ref.shape[3]
    variables, planes, rows_count, _ = field_ref.shape
    copies = [
        pltpu.make_async_copy(source, target, sem.at[k])
        for k, (source, target) in enumerate(
            (
                (count_ref, count_smem),
                (cell_ref, cell_vmem),
                (offset_ref, offset_vmem),
                (node_ref, node_vmem),
                (jitter_ref.at[:, pl.ds(0, 1)], next_ref.at[pl.ds(0, 3)]),
                (field_ref.at[:, pl.ds(0, 1)], next_ref.at[pl.ds(3, variables)]),
                (field_ref.at[:, pl.ds(planes - 1, 1)], last_ref),
            )
        )
    ]
    for copy in copies:
        copy.start()
    for copy in copies[:4]:
        copy.wait()

    spare = planes * rows_count * 8
    lane = lax.broadcasted_iota(jnp.int32, (1, points), 1)

    me = lax.axis_index("grid")

    def code(place, nodes, live):
        code_ref[pl.ds(place, 1), :] = jnp.where(live, (nodes >> 7) * 8, spare)
        code_ref[pl.ds(owners + 1 + place, 1), :] = ((nodes & 127) - lane) & 127

    def one(distance, carry):
        owner = lax.rem(me + distance, owners)
        count = count_smem[0, owner]
        cells = cell_vmem[0, owner].astype(jnp.float32)
        message_ref[owner, 0:1, :] = cells[0:1]
        message_ref[owner, 4:5, :] = cells[1:2]
        for c in range(3):
            message_ref[owner, 1 + c : 2 + c, :] = offset_vmem[0, owner, c, 0:1, :]
            message_ref[owner, 5 + c : 6 + c, :] = offset_vmem[0, owner, c, 1:2, :]
        code(distance, node_vmem[0, owner, 0:1, :], lane < count)
        return carry

    lax.fori_loop(0, owners, one, 0, unroll=True)
    heavy = lax.rem(me + 1, owners)
    code(owners, node_vmem[0, heavy, 1:2, :], lane + points < count_smem[0, heavy])
    for copy in copies[4:]:
        copy.wait()


def coefficients(corner):
    linear = [corner[4] - corner[0], corner[2] - corner[0], corner[1] - corner[0]]
    pair_01 = corner[6] - corner[4] - linear[1]
    pair_02 = corner[5] - corner[4] - linear[2]
    pair_12 = corner[3] - corner[2] - linear[2]
    triple = (corner[7] - corner[6]) - (corner[5] - corner[4]) - pair_12
    return corner[0], linear, pair_01, pair_02, pair_12, triple


def solve(corner, target):
    polys = []
    for component in range(3):
        start, linear, pair_01, pair_02, pair_12, triple = coefficients(
            [corner(q, component) for q in range(8)]
        )
        linear[component] = linear[component] + 1.0
        polys.append((start - target[component], linear, pair_01, pair_02, pair_12, triple))
    s0 = s1 = s2 = jnp.full(target[0].shape, 0.5, jnp.float32)
    for _ in range(4):
        s01, s02, s12 = s0 * s1, s0 * s2, s1 * s2
        misfit, jac = [], []
        for start, (l0, l1, l2), p01, p02, p12, triple in polys:
            d0 = l0 + s1 * p01 + s2 * p02 + s12 * triple
            d1 = l1 + s0 * p01 + s2 * p12 + s02 * triple
            d2 = l2 + s0 * p02 + s1 * p12 + s01 * triple
            misfit.append(start + s0 * d0 + s1 * (l1 + s2 * p12) + s2 * l2)
            jac.append((d0, d1, d2))
        (a0, a1, a2), (b0, b1, b2), (c0, c1, c2) = jac
        m0, m1, m2 = misfit
        bc12 = b1 * c2 - b2 * c1
        bc02 = b0 * c2 - b2 * c0
        bc01 = b0 * c1 - b1 * c0
        det = a0 * bc12 - a1 * bc02 + a2 * bc01
        bm2 = m1 * c2 - b2 * m2
        bm1 = m1 * c1 - b1 * m2
        bm0 = b0 * m2 - m1 * c0
        inverse = 1.0 / det
        u0 = m0 * bc12 - a1 * bm2 + a2 * bm1
        u1 = a0 * bm2 - m0 * bc02 + a2 * bm0
        u2 = a0 * (b1 * m2 - m1 * c1) - a1 * bm0 + m0 * bc01
        s0 = s0 - u0 * inverse
        s1 = s1 - u1 * inverse
        s2 = s2 - u2 * inverse
    values = []
    for variable in range(5):
        u = [corner(q, 3 + variable) for q in range(8)]
        e = [u[q] + s2 * (u[q + 1] - u[q]) for q in (0, 2, 4, 6)]
        f = [e[q] + s1 * (e[q + 1] - e[q]) for q in (0, 2)]
        values.append(f[0] + s0 * (f[1] - f[0]))
    return values


def lay_out(table, field_ref, jitter_ref, next_ref):
    planes, columns = field_ref.shape[1], field_ref.shape[3]

    def read(plane, variable):
        if plane == planes:
            return next_ref[variable, 0]
        return jitter_ref[variable, plane] if variable < 3 else field_ref[variable - 3, plane]

    for plane in range(planes + 1):
        for half in range(2):
            tile = jnp.concatenate([read(plane, 4 * half + w) for w in range(4)], 0).T
            first = plane * (2 * columns) + half
            table[pl.ds(first, columns, stride=2), :] = tile


def separated(tiles, lane):
    for bit, distance in ((0, 1), (1, 32), (2, 64)):
        low = (lane & distance) == 0
        result = list(tiles)
        for a in range(8):
            b = a | (1 << bit)
            if a == b:
                continue
            result[a] = jnp.where(low, tiles[a], pltpu.roll(tiles[b], distance, 1))
            result[b] = jnp.where(low, pltpu.roll(tiles[a], LANES - distance, 1), tiles[b])
        tiles = result
    return tiles


def tile_rows(tile):
    first = tile * ROWS
    return pl.ds(first if isinstance(first, int) else pl.multiple_of(first, ROWS), ROWS)


def after(me, body):
    def once(step, carry):
        body()
        return carry

    lax.fori_loop(0, jnp.minimum(me + 1, 1), once, 0)


def each_source(owners, body):
    if owners <= 8:
        for distance in range(owners + 1):
            body(distance, 1 if distance == 2 else LANES)
    else:

        def one(distance, carry):
            body(distance, LANES)
            return carry

        lax.fori_loop(0, owners + 1, one, 0)


def gather_kernel(
    owners, field_ref, jitter_ref, next_ref, below_ref, message_ref, out_ref,
    table, message, decoded, codes, picked, parts, answers, sem,
):
    rows_count = 32
    me = lax.axis_index("grid")
    lane = lax.broadcasted_iota(jnp.int32, (ROWS, LANES), 1)
    sublane = lax.broadcasted_iota(jnp.int32, (ROWS, LANES), 0)

    def decode(cells, place):
        cells = cells.astype(jnp.int32)
        row = (cells >> 12) * (2 * LANES) + (cells & 127) * 2
        shift = ((lane & 30) - ((cells >> 7) & (rows_count - 1))) & 127
        decoded[place, :] = row * LANES + shift

    def of_source(distance):
        return lax.rem(me + owners - distance, owners)

    for distance in range(owners):
        message[tile_rows(distance), :] = message_ref[tile_rows(of_source(distance)), :]
    for block in range(owners // ROWS):
        cells = message[pl.ds(block * ROWS * 8, ROWS, stride=8), :]
        decode(cells, pl.ds(block * ROWS, ROWS))
    more = jnp.broadcast_to(message[12:13, :], (ROWS, LANES))
    decode(more, pl.ds(owners, ROWS))
    copy = pltpu.make_async_copy(decoded, codes, sem)
    copy.start()
    after(me, lambda: lay_out(table, field_ref, jitter_ref, next_ref))
    copy.wait()

    low = sublane < 4
    pairs = [(lane & 30) == 2 * k for k in range(16)]

    def one_source(source, points):
        for block in range((points + 31) // 32):
            held = [None, None]
            for k in range(min(32, points)):
                code = codes[source, block * 32 + k]
                row = code >> 7
                tile = jnp.where(
                    low,
                    table[pl.ds(row, ROWS), :],
                    table[pl.ds(row + (2 * LANES - 4), ROWS), :],
                )
                tile = pltpu.roll(tile, code & 127, 1)
                k2 = k & 1
                held[k2] = tile if held[k2] is None else jnp.where(pairs[k >> 1], tile, held[k2])
            for k in range(min(2, points)):
                picked[tile_rows((2 * block + k) * (owners + 1) + source), :] = held[k]

    each_source(owners, one_source)

    def one_block(block, last):
        for s in range(8):
            tiles = [
                picked[pl.ds((g * (owners + 1) + block * ROWS) * 8 + s, ROWS, stride=8), :]
                for g in range(8)
            ]
            for x, tile in enumerate(separated(tiles, lane)):
                parts[s, x] = tile
        if last:
            tiles = [picked[pl.ds((g * (owners + 1) + owners) * 8, 8), :] for g in range(8)]
            for x, tile in enumerate(separated(tiles, lane)):
                parts[8, x] = tile

        def corner(q, variable):
            a0, a1, a2 = q >> 2, (q >> 1) & 1, q & 1
            s, x = 4 * a0 + 2 * a2 + (variable >> 2), 2 * (variable & 3) + a1
            tile = parts[s, x]
            if last:
                more = jnp.broadcast_to(parts[8, x, s : s + 1, :], (ROWS, LANES))
                tile = jnp.concatenate([tile, more], 0)
            return tile

        target = []
        for c in range(3):
            tile = message[pl.ds(block * (ROWS * 8) + 1 + c, ROWS, stride=8), :]
            if last:
                more = message[13 + c : 14 + c, :]
                tile = jnp.concatenate([tile, jnp.broadcast_to(more, (ROWS, LANES))], 0)
            target.append(tile)
        values = solve(corner, target)
        for variable in range(5):
            answers[pl.ds(variable, ROWS, stride=8), :] = values[variable][:ROWS]
            if last:
                place = pl.ds(of_source(1) * 16 + 8 + variable, 1)
                out_ref[place, :] = values[variable][ROWS : ROWS + 1]
        for distance in range(ROWS):
            source = of_source(block * ROWS + distance)
            out_ref[tile_rows(2 * source), :] = answers[tile_rows(distance), :]

    for block in range(owners // ROWS):
        one_block(block, block == owners // ROWS - 1)


def relax_kernel(
    owners, code_ref, field_ref, next_ref, below_ref, ratio_ref, values_ref, out_ref,
    table, codes, rolled, plain, inverse, out_vmem, sem, out_sem,
):
    variables, planes, rows_count, _ = out_ref.shape
    width = 8
    blocks = rows_count // ROWS
    plane_rows = rows_count * width
    copy = pltpu.make_async_copy(code_ref, codes, sem)
    copy.start()
    lane = lax.broadcasted_iota(jnp.int32, (ROWS, LANES), 1)
    sublane = lax.broadcasted_iota(jnp.int32, (ROWS, LANES), 0)
    me = lax.axis_index("grid")

    def lay_out_rows():
        for plane in range(planes):
            for variable in range(variables + 1):
                tile = jnp.zeros((rows_count, LANES), jnp.float32)
                if variable < variables:
                    tile = field_ref[variable, plane]
                first = plane * plane_rows + variable
                table[pl.ds(first, rows_count, stride=width), :] = tile
            inverse[plane] = 1.0 / (1.0 + 6.0 * ratio_ref[plane])

    after(me, lay_out_rows)
    copy.wait()

    def rotate(distance, points, buffer):
        if isinstance(distance, int):
            owner = lax.rem(me + distance % owners + distance // owners, owners)
            first = owner * 16 + 8 * (distance // owners)
        else:
            more = distance == owners
            owner = lax.rem(jnp.where(more, me + 1, me + distance), owners)
            first = owner * 16 + jnp.where(more, 8, 0)
        tile = values_ref[pl.ds(pl.multiple_of(first, 8), 8), :]
        tile = jnp.where(sublane == variables, 1.0, tile)
        tile = jnp.where(sublane == variables + 1, lane.astype(jnp.float32), tile)
        for point in range(points):
            place = tile_rows(buffer * LANES + point)
            rolled[place, :] = pltpu.roll(tile, codes[owners + 1 + distance, point], 1)

    def store(distance, points, buffer):
        for point in range(points):
            place = (buffer * LANES + point) * ROWS
            tag = rolled[place + variables + 1 : place + variables + 2, :]
            row = pl.multiple_of(codes[distance, point], width)
            pltpu.store(
                table.at[pl.ds(row, width), :],
                rolled[place : place + ROWS, :],
                mask=jnp.broadcast_to(tag, (ROWS, LANES)) == float(point),
            )

    if owners <= 8:
        todo = []
        each_source(owners, lambda distance, points: todo.append((distance, points, distance)))
        rotate(*todo[0])
        for now, later in zip(todo, todo[1:] + [None]):
            if later is not None:
                rotate(*later)
            store(*now)
    else:

        def one_source(distance, points):
            rotate(distance, points, 0)
            store(distance, points, 0)

        each_source(owners, one_source)

    def out_copy(plane):
        return pltpu.make_async_copy(
            out_vmem.at[:, pl.ds(plane, 1)], out_ref.at[:, pl.ds(plane, 1)], out_sem.at[plane]
        )

    def place(plane, block, variable, step=0):
        return pl.ds(ROWS + (variable * planes + plane) * rows_count + block * ROWS + step, ROWS)

    def flat(plane):
        for block in range(blocks):
            for variable in range(variables):
                first = plane * plane_rows + block * ROWS * width + variable
                plain[place(plane, block, variable), :] = table[pl.ds(first, ROWS, stride=width), :]

    def one_plane(plane):
        for block in range(blocks):
            rows = pl.ds(block * ROWS, ROWS)
            ratio, divisor = ratio_ref[plane, rows, :], inverse[plane, rows, :]
            first = plane * plane_rows + block * ROWS * width + variables
            fringe = table[pl.ds(first, ROWS, stride=width), :] > 0.5
            for variable in range(variables):
                here = plain[place(plane, block, variable), :]
                up = plain[place(plane, block, variable, 1), :]
                down = plain[place(plane, block, variable, -1), :]
                if block == 0:
                    down = jnp.where(sublane == 0, 0.0, down)
                if block == blocks - 1:
                    up = jnp.where(sublane == ROWS - 1, 0.0, up)
                right = jnp.where(lane == LANES - 1, 0.0, pltpu.roll(here, LANES - 1, 1))
                left = jnp.where(lane == 0, 0.0, pltpu.roll(here, 1, 1))
                if plane == 0:
                    below = below_ref[variable, 0, rows, :]
                else:
                    below = plain[place(plane - 1, block, variable), :]
                if plane == planes - 1:
                    above = next_ref[3 + variable, 0, rows, :]
                else:
                    above = plain[place(plane + 1, block, variable), :]
                total = (above + below) + (up + down) + (right + left)
                smooth = (here + ratio * total) * divisor
                out_vmem[variable, plane, rows, :] = jnp.where(fringe, here, smooth)
        out_copy(plane).start()

    flat(0)
    for plane in range(planes):
        if plane < planes - 1:
            flat(plane + 1)
        one_plane(plane)
    for plane in range(planes):
        out_copy(plane).wait()


def on_device(
    field, node_jitter, time_ratio, donor_cell, receptor_offset, receptor_node, point_count
):
    variables, planes, rows_count, cols_count = field.shape
    owners, points = donor_cell.shape[1], donor_cell.shape[3]
    params = pltpu.CompilerParams(vmem_limit_bytes=LIMIT)
    offsets = jnp.swapaxes(receptor_offset, 2, 3)
    f32, i32 = jnp.float32, jnp.int32
    message, codes, first, last = pl.pallas_call(
        first_kernel,
        out_shape=[
            jax.ShapeDtypeStruct((owners, 8, LANES), f32),
            jax.ShapeDtypeStruct((2 * owners + 8, LANES), i32),
            jax.ShapeDtypeStruct((3 + variables, 1, rows_count, cols_count), f32),
            jax.ShapeDtypeStruct((variables, 1, rows_count, cols_count), f32),
        ],
        in_specs=[HBM] * 6,
        out_specs=[VMEM] * 4,
        scratch_shapes=[
            pltpu.SMEM(point_count.shape, i32),
            pltpu.VMEM(donor_cell.shape, i32),
            pltpu.VMEM(offsets.shape, f32),
            pltpu.VMEM(receptor_node.shape, i32),
            pltpu.SemaphoreType.DMA((7,)),
        ],
        compiler_params=params,
        name="first",
    )(*[
        pltpu.with_memory_space_constraint(x, pltpu.HBM)
        for x in (point_count, donor_cell, offsets, receptor_node, field, node_jitter)
    ])
    following = passed_along(first, "sub", -1)
    below = passed_along(last, "sub", 1)
    message = lax.all_to_all(message, "grid", split_axis=0, concat_axis=0, tiled=True)
    values = pl.pallas_call(
        functools.partial(gather_kernel, owners),
        out_shape=jax.ShapeDtypeStruct((owners * 16, LANES), f32),
        in_specs=[VMEM] * 5,
        out_specs=VMEM,
        scratch_shapes=[
            pltpu.VMEM(((planes + 1) * cols_count * 2, LANES), f32),
            pltpu.VMEM((owners * 8, LANES), f32),
            pltpu.VMEM((owners + 8, LANES), i32),
            pltpu.SMEM((owners + 8, LANES), i32),
            pltpu.VMEM((8 * (owners + 1) * 8, LANES), f32),
            pltpu.VMEM((9, 8, ROWS, LANES), f32),
            pltpu.VMEM((ROWS * 8, LANES), f32),
            pltpu.SemaphoreType.DMA,
        ],
        compiler_params=params,
        name="gather",
    )(field, node_jitter, following, below, message.reshape(owners * 8, LANES))
    values = values.reshape(owners, 16, LANES)
    values = lax.all_to_all(values, "grid", split_axis=0, concat_axis=0, tiled=True)
    return pl.pallas_call(
        functools.partial(relax_kernel, owners),
        out_shape=jax.ShapeDtypeStruct(field.shape, f32),
        in_specs=[VMEM] * 6,
        out_specs=HBM,
        scratch_shapes=[
            pltpu.VMEM((planes * rows_count * 8 + 8, LANES), f32),
            pltpu.SMEM(codes.shape, i32),
            pltpu.VMEM(((owners + 1 if owners <= 8 else 1) * LANES * ROWS, LANES), f32),
            pltpu.VMEM((variables * planes * rows_count + 2 * ROWS, LANES), f32),
            pltpu.VMEM(time_ratio.shape, f32),
            pltpu.VMEM(field.shape, f32),
            pltpu.SemaphoreType.DMA,
            pltpu.SemaphoreType.DMA((planes,)),
        ],
        compiler_params=params,
        name="relax",
    )(codes, field, following, below, time_ratio, values.reshape(owners * 16, LANES))


def solution(mesh):
    placed = (
        P(None, ("grid", "sub"), None, None),
        P(None, ("grid", "sub"), None, None),
        P(("grid", "sub"), None, None),
        P(("grid", "sub"), None, None, None),
        P(("grid", "sub"), None, None, None, None),
        P(("grid", "sub"), None, None, None),
        P(("grid", "sub"), None),
    )
    return jax.shard_map(
        on_device,
        mesh=mesh,
        in_specs=placed,
        out_specs=P(None, ("grid", "sub"), None, None),
        check_vma=False,
    )
```

```python
import functools

import jax
import jax.numpy as jnp
from jax import lax
from jax.experimental import pallas as pl
from jax.experimental.pallas import tpu as pltpu
from jax.sharding import PartitionSpec as P

ROWS = 8
LANES = 128
VMEM = pl.BlockSpec(memory_space=pltpu.VMEM)
HBM = pl.BlockSpec(memory_space=pltpu.HBM)
LIMIT = 24 << 20


def passed_along(value, axis, steps):
    count = lax.axis_size(axis)
    pairs = [(source, (source + steps) % count) for source in range(count)]
    return lax.ppermute(value, axis, pairs)


def first_kernel(
    count_ref, cell_ref, offset_ref, node_ref, field_ref, jitter_ref,
    message_ref, code_ref, next_ref, last_ref,
    count_smem, cell_vmem, offset_vmem, node_vmem, sem,
):
    owners, points = cell_ref.shape[1], cell_ref.shape[3]
    variables, planes, rows_count, _ = field_ref.shape
    copies = [
        pltpu.make_async_copy(source, target, sem.at[k])
        for k, (source, target) in enumerate(
            (
                (count_ref, count_smem),
                (cell_ref, cell_vmem),
                (offset_ref, offset_vmem),
                (node_ref, node_vmem),
                (jitter_ref.at[:, pl.ds(0, 1)], next_ref.at[pl.ds(0, 3)]),
                (field_ref.at[:, pl.ds(0, 1)], next_ref.at[pl.ds(3, variables)]),
                (field_ref.at[:, pl.ds(planes - 1, 1)], last_ref),
            )
        )
    ]
    for copy in copies:
        copy.start()
    for copy in copies[:4]:
        copy.wait()

    spare = planes * rows_count * 8
    lane = lax.broadcasted_iota(jnp.int32, (1, points), 1)

    me = lax.axis_index("grid")

    def code(place, nodes, live):
        code_ref[pl.ds(place, 1), :] = jnp.where(live, (nodes >> 7) * 8, spare)
        code_ref[pl.ds(owners + 1 + place, 1), :] = ((nodes & 127) - lane) & 127

    def one(distance, carry):
        owner = lax.rem(me + distance, owners)
        count = count_smem[0, owner]
        cells = cell_vmem[0, owner].astype(jnp.float32)
        message_ref[owner, 0:1, :] = cells[0:1]
        message_ref[owner, 4:5, :] = cells[1:2]
        for c in range(3):
            message_ref[owner, 1 + c : 2 + c, :] = offset_vmem[0, owner, c, 0:1, :]
            message_ref[owner, 5 + c : 6 + c, :] = offset_vmem[0, owner, c, 1:2, :]
        code(distance, node_vmem[0, owner, 0:1, :], lane < count)
        return carry

    lax.fori_loop(0, owners, one, 0, unroll=True)
    heavy = lax.rem(me + 1, owners)
    code(owners, node_vmem[0, heavy, 1:2, :], lane + points < count_smem[0, heavy])
    for copy in copies[4:]:
        copy.wait()


def coefficients(corner):
    linear = [corner[4] - corner[0], corner[2] - corner[0], corner[1] - corner[0]]
    pair_01 = corner[6] - corner[4] - linear[1]
    pair_02 = corner[5] - corner[4] - linear[2]
    pair_12 = corner[3] - corner[2] - linear[2]
    triple = (corner[7] - corner[6]) - (corner[5] - corner[4]) - pair_12
    return corner[0], linear, pair_01, pair_02, pair_12, triple


def solve(corner, target):
    polys = []
    for component in range(3):
        start, linear, pair_01, pair_02, pair_12, triple = coefficients(
            [corner(q, component) for q in range(8)]
        )
        linear[component] = linear[component] + 1.0
        polys.append((start - target[component], linear, pair_01, pair_02, pair_12, triple))
    s0 = s1 = s2 = jnp.full(target[0].shape, 0.5, jnp.float32)
    for _ in range(4):
        s01, s02, s12 = s0 * s1, s0 * s2, s1 * s2
        misfit, jac = [], []
        for start, (l0, l1, l2), p01, p02, p12, triple in polys:
            d0 = l0 + s1 * p01 + s2 * p02 + s12 * triple
            d1 = l1 + s0 * p01 + s2 * p12 + s02 * triple
            d2 = l2 + s0 * p02 + s1 * p12 + s01 * triple
            misfit.append(start + s0 * d0 + s1 * (l1 + s2 * p12) + s2 * l2)
            jac.append((d0, d1, d2))
        (a0, a1, a2), (b0, b1, b2), (c0, c1, c2) = jac
        m0, m1, m2 = misfit
        bc12 = b1 * c2 - b2 * c1
        bc02 = b0 * c2 - b2 * c0
        bc01 = b0 * c1 - b1 * c0
        det = a0 * bc12 - a1 * bc02 + a2 * bc01
        bm2 = m1 * c2 - b2 * m2
        bm1 = m1 * c1 - b1 * m2
        bm0 = b0 * m2 - m1 * c0
        inverse = 1.0 / det
        u0 = m0 * bc12 - a1 * bm2 + a2 * bm1
        u1 = a0 * bm2 - m0 * bc02 + a2 * bm0
        u2 = a0 * (b1 * m2 - m1 * c1) - a1 * bm0 + m0 * bc01
        s0 = s0 - u0 * inverse
        s1 = s1 - u1 * inverse
        s2 = s2 - u2 * inverse
    values = []
    for variable in range(5):
        u = [corner(q, 3 + variable) for q in range(8)]
        e = [u[q] + s2 * (u[q + 1] - u[q]) for q in (0, 2, 4, 6)]
        f = [e[q] + s1 * (e[q + 1] - e[q]) for q in (0, 2)]
        values.append(f[0] + s0 * (f[1] - f[0]))
    return values


def lay_out(table, field_ref, jitter_ref, next_ref):
    planes, columns = field_ref.shape[1], field_ref.shape[3]

    def read(plane, variable):
        if plane == planes:
            return next_ref[variable, 0]
        return jitter_ref[variable, plane] if variable < 3 else field_ref[variable - 3, plane]

    for plane in range(planes + 1):
        for half in range(2):
            tile = jnp.concatenate([read(plane, 4 * half + w) for w in range(4)], 0).T
            first = plane * (2 * columns) + half
            table[pl.ds(first, columns, stride=2), :] = tile


def separated(tiles, lane):
    even = (lane & 1) == 0
    result = [None] * 8
    for a1 in range(2):
        block = ((lane - a1) & 127) >> 5
        held = [jnp.where(even, tiles[2 * h + a1], tiles[2 * h + 1 - a1]) for h in range(4)]
        masks = [block == h for h in range(4)]
        for w in range(4):
            tile = held[3]
            for h in range(3):
                tile = jnp.where(masks[(h + w) & 3], held[h], tile)
            distance = (LANES - 32 * w - a1) % LANES
            result[2 * w + a1] = pltpu.roll(tile, distance, 1) if distance else tile
    return result


def tile_rows(tile):
    first = tile * ROWS
    return pl.ds(first if isinstance(first, int) else pl.multiple_of(first, ROWS), ROWS)


def after(me, body):
    def once(step, carry):
        body()
        return carry

    lax.fori_loop(0, jnp.minimum(me + 1, 1), once, 0)


def each_source(owners, body):
    if owners <= 8:
        for distance in range(owners + 1):
            body(distance, 1 if distance == 2 else LANES)
    else:

        def one(distance, carry):
            body(distance, LANES)
            return carry

        lax.fori_loop(0, owners + 1, one, 0)


def gather_kernel(
    owners, field_ref, jitter_ref, next_ref, below_ref, message_ref, out_ref,
    table, message, decoded, codes, picked, parts, answers, sem,
):
    rows_count = 32
    me = lax.axis_index("grid")
    lane = lax.broadcasted_iota(jnp.int32, (ROWS, LANES), 1)
    sublane = lax.broadcasted_iota(jnp.int32, (ROWS, LANES), 0)

    def decode(cells, place):
        cells = cells.astype(jnp.int32)
        row = (cells >> 12) * (2 * LANES) + (cells & 127) * 2
        shift = (lane - ((cells >> 7) & (rows_count - 1))) & 127
        decoded[place, :] = row * LANES + shift

    def of_source(distance):
        return lax.rem(me + owners - distance, owners)

    for distance in range(owners):
        message[tile_rows(distance), :] = message_ref[tile_rows(of_source(distance)), :]
    for block in range(owners // ROWS):
        cells = message[pl.ds(block * ROWS * 8, ROWS, stride=8), :]
        decode(cells, pl.ds(block * ROWS, ROWS))
    more = jnp.broadcast_to(message[12:13, :], (ROWS, LANES))
    decode(more, pl.ds(owners, ROWS))
    copy = pltpu.make_async_copy(decoded, codes, sem)
    copy.start()
    after(me, lambda: lay_out(table, field_ref, jitter_ref, next_ref))
    copy.wait()

    low = sublane < 4
    pairs = [((lane - k) & 31) >> 1 for k in range(2)]

    def one_source(source, points, blocks=range(4)):
        for block in blocks:
            if block * 32 >= points:
                continue
            held = [None, None]
            for k in range(min(32, points)):
                code = codes[source, block * 32 + k]
                row = code >> 7
                tile = jnp.where(
                    low,
                    table[pl.ds(row, ROWS), :],
                    table[pl.ds(row + (2 * LANES - 4), ROWS), :],
                )
                tile = pltpu.roll(tile, code & 127, 1)
                k2 = k & 1
                held[k2] = tile if held[k2] is None else jnp.where(pairs[k2] == k >> 1, tile, held[k2])
            for k in range(min(2, points)):
                picked[tile_rows((2 * block + k) * (owners + 1) + source), :] = held[k]

    if owners <= 8:
        for block in range(4):
            each_source(owners, lambda source, points: one_source(source, points, [block]))
    else:
        each_source(owners, one_source)

    def one_block(block, last):
        for s in range(8):
            tiles = [
                picked[pl.ds((g * (owners + 1) + block * ROWS) * 8 + s, ROWS, stride=8), :]
                for g in range(8)
            ]
            for x, tile in enumerate(separated(tiles, lane)):
                parts[s, x] = tile
        if last:
            tiles = [picked[pl.ds((g * (owners + 1) + owners) * 8, 8), :] for g in range(8)]
            for x, tile in enumerate(separated(tiles, lane)):
                parts[8, x] = tile

        def corner(q, variable):
            a0, a1, a2 = q >> 2, (q >> 1) & 1, q & 1
            s, x = 4 * a0 + 2 * a2 + (variable >> 2), 2 * (variable & 3) + a1
            tile = parts[s, x]
            if last:
                more = jnp.broadcast_to(parts[8, x, s : s + 1, :], (ROWS, LANES))
                tile = jnp.concatenate([tile, more], 0)
            return tile

        target = []
        for c in range(3):
            tile = message[pl.ds(block * (ROWS * 8) + 1 + c, ROWS, stride=8), :]
            if last:
                more = message[13 + c : 14 + c, :]
                tile = jnp.concatenate([tile, jnp.broadcast_to(more, (ROWS, LANES))], 0)
            target.append(tile)
        values = solve(corner, target)
        for variable in range(5):
            answers[pl.ds(variable, ROWS, stride=8), :] = values[variable][:ROWS]
            if last:
                place = pl.ds(of_source(1) * 16 + 8 + variable, 1)
                out_ref[place, :] = values[variable][ROWS : ROWS + 1]
        for distance in range(ROWS):
            source = of_source(block * ROWS + distance)
            out_ref[tile_rows(2 * source), :] = answers[tile_rows(distance), :]

    for block in range(owners // ROWS):
        one_block(block, block == owners // ROWS - 1)


def relax_kernel(
    owners, code_ref, field_ref, next_ref, below_ref, ratio_ref, values_ref, out_ref,
    table, codes, rolled, plain, inverse, out_vmem, sem, out_sem,
):
    variables, planes, rows_count, _ = out_ref.shape
    width = 8
    blocks = rows_count // ROWS
    plane_rows = rows_count * width
    copy = pltpu.make_async_copy(code_ref, codes, sem)
    copy.start()
    lane = lax.broadcasted_iota(jnp.int32, (ROWS, LANES), 1)
    sublane = lax.broadcasted_iota(jnp.int32, (ROWS, LANES), 0)
    me = lax.axis_index("grid")

    def lay_out_rows():
        for plane in range(planes):
            for variable in range(variables + 1):
                tile = jnp.zeros((rows_count, LANES), jnp.float32)
                if variable < variables:
                    tile = field_ref[variable, plane]
                first = plane * plane_rows + variable
                table[pl.ds(first, rows_count, stride=width), :] = tile
            inverse[plane] = 1.0 / (1.0 + 6.0 * ratio_ref[plane])

    after(me, lay_out_rows)
    copy.wait()

    def rotate(distance, points, buffer):
        if isinstance(distance, int):
            owner = lax.rem(me + distance % owners + distance // owners, owners)
            first = owner * 16 + 8 * (distance // owners)
        else:
            more = distance == owners
            owner = lax.rem(jnp.where(more, me + 1, me + distance), owners)
            first = owner * 16 + jnp.where(more, 8, 0)
        tile = values_ref[pl.ds(pl.multiple_of(first, 8), 8), :]
        tile = jnp.where(sublane == variables, 1.0, tile)
        tile = jnp.where(sublane == variables + 1, lane.astype(jnp.float32), tile)
        for point in range(points):
            place = tile_rows(buffer * LANES + point)
            rolled[place, :] = pltpu.roll(tile, codes[owners + 1 + distance, point], 1)

    def store(distance, points, buffer):
        for point in range(points):
            place = (buffer * LANES + point) * ROWS
            tag = rolled[place + variables + 1 : place + variables + 2, :]
            row = pl.multiple_of(codes[distance, point], width)
            pltpu.store(
                table.at[pl.ds(row, width), :],
                rolled[place : place + ROWS, :],
                mask=jnp.broadcast_to(tag, (ROWS, LANES)) == float(point),
            )

    if owners <= 8:
        todo = []
        each_source(owners, lambda distance, points: todo.append((distance, points, distance)))
        rotate(*todo[0])
        for now, later in zip(todo, todo[1:] + [None]):
            if later is not None:
                rotate(*later)
            store(*now)
    else:

        def one_source(distance, points):
            rotate(distance, points, 0)
            store(distance, points, 0)

        each_source(owners, one_source)

    def out_copy(plane):
        return pltpu.make_async_copy(
            out_vmem.at[:, pl.ds(plane, 1)], out_ref.at[:, pl.ds(plane, 1)], out_sem.at[plane]
        )

    def place(plane, block, variable, step=0):
        return pl.ds(ROWS + (variable * planes + plane) * rows_count + block * ROWS + step, ROWS)

    def flat(plane):
        for block in range(blocks):
            for variable in range(variables):
                first = plane * plane_rows + block * ROWS * width + variable
                plain[place(plane, block, variable), :] = table[pl.ds(first, ROWS, stride=width), :]

    def one_plane(plane):
        for block in range(blocks):
            rows = pl.ds(block * ROWS, ROWS)
            ratio, divisor = ratio_ref[plane, rows, :], inverse[plane, rows, :]
            first = plane * plane_rows + block * ROWS * width + variables
            fringe = table[pl.ds(first, ROWS, stride=width), :] > 0.5
            for variable in range(variables):
                here = plain[place(plane, block, variable), :]
                up = plain[place(plane, block, variable, 1), :]
                down = plain[place(plane, block, variable, -1), :]
                if block == 0:
                    down = jnp.where(sublane == 0, 0.0, down)
                if block == blocks - 1:
                    up = jnp.where(sublane == ROWS - 1, 0.0, up)
                right = jnp.where(lane == LANES - 1, 0.0, pltpu.roll(here, LANES - 1, 1))
                left = jnp.where(lane == 0, 0.0, pltpu.roll(here, 1, 1))
                if plane == 0:
                    below = below_ref[variable, 0, rows, :]
                else:
                    below = plain[place(plane - 1, block, variable), :]
                if plane == planes - 1:
                    above = next_ref[3 + variable, 0, rows, :]
                else:
                    above = plain[place(plane + 1, block, variable), :]
                total = (above + below) + (up + down) + (right + left)
                smooth = (here + ratio * total) * divisor
                out_vmem[variable, plane, rows, :] = jnp.where(fringe, here, smooth)
        out_copy(plane).start()

    flat(0)
    for plane in range(planes):
        if plane < planes - 1:
            flat(plane + 1)
        one_plane(plane)
    for plane in range(planes):
        out_copy(plane).wait()


def on_device(
    field, node_jitter, time_ratio, donor_cell, receptor_offset, receptor_node, point_count
):
    variables, planes, rows_count, cols_count = field.shape
    owners, points = donor_cell.shape[1], donor_cell.shape[3]
    params = pltpu.CompilerParams(vmem_limit_bytes=LIMIT)
    offsets = jnp.swapaxes(receptor_offset, 2, 3)
    f32, i32 = jnp.float32, jnp.int32
    message, codes, first, last = pl.pallas_call(
        first_kernel,
        out_shape=[
            jax.ShapeDtypeStruct((owners, 8, LANES), f32),
            jax.ShapeDtypeStruct((2 * owners + 8, LANES), i32),
            jax.ShapeDtypeStruct((3 + variables, 1, rows_count, cols_count), f32),
            jax.ShapeDtypeStruct((variables, 1, rows_count, cols_count), f32),
        ],
        in_specs=[HBM] * 6,
        out_specs=[VMEM] * 4,
        scratch_shapes=[
            pltpu.SMEM(point_count.shape, i32),
            pltpu.VMEM(donor_cell.shape, i32),
            pltpu.VMEM(offsets.shape, f32),
            pltpu.VMEM(receptor_node.shape, i32),
            pltpu.SemaphoreType.DMA((7,)),
        ],
        compiler_params=params,
        name="first",
    )(*[
        pltpu.with_memory_space_constraint(x, pltpu.HBM)
        for x in (point_count, donor_cell, offsets, receptor_node, field, node_jitter)
    ])
    following = passed_along(first, "sub", -1)
    below = passed_along(last, "sub", 1)
    message = lax.all_to_all(message, "grid", split_axis=0, concat_axis=0, tiled=True)
    values = pl.pallas_call(
        functools.partial(gather_kernel, owners),
        out_shape=jax.ShapeDtypeStruct((owners * 16, LANES), f32),
        in_specs=[VMEM] * 5,
        out_specs=VMEM,
        scratch_shapes=[
            pltpu.VMEM(((planes + 1) * cols_count * 2, LANES), f32),
            pltpu.VMEM((owners * 8, LANES), f32),
            pltpu.VMEM((owners + 8, LANES), i32),
            pltpu.SMEM((owners + 8, LANES), i32),
            pltpu.VMEM((8 * (owners + 1) * 8, LANES), f32),
            pltpu.VMEM((9, 8, ROWS, LANES), f32),
            pltpu.VMEM((ROWS * 8, LANES), f32),
            pltpu.SemaphoreType.DMA,
        ],
        compiler_params=params,
        name="gather",
    )(field, node_jitter, following, below, message.reshape(owners * 8, LANES))
    values = values.reshape(owners, 16, LANES)
    values = lax.all_to_all(values, "grid", split_axis=0, concat_axis=0, tiled=True)
    return pl.pallas_call(
        functools.partial(relax_kernel, owners),
        out_shape=jax.ShapeDtypeStruct(field.shape, f32),
        in_specs=[VMEM] * 6,
        out_specs=HBM,
        scratch_shapes=[
            pltpu.VMEM((planes * rows_count * 8 + 8, LANES), f32),
            pltpu.SMEM(codes.shape, i32),
            pltpu.VMEM(((owners + 1 if owners <= 8 else 1) * LANES * ROWS, LANES), f32),
            pltpu.VMEM((variables * planes * rows_count + 2 * ROWS, LANES), f32),
            pltpu.VMEM(time_ratio.shape, f32),
            pltpu.VMEM(field.shape, f32),
            pltpu.SemaphoreType.DMA,
            pltpu.SemaphoreType.DMA((planes,)),
        ],
        compiler_params=params,
        name="relax",
    )(codes, field, following, below, time_ratio, values.reshape(owners * 16, LANES))


def solution(mesh):
    placed = (
        P(None, ("grid", "sub"), None, None),
        P(None, ("grid", "sub"), None, None),
        P(("grid", "sub"), None, None),
        P(("grid", "sub"), None, None, None),
        P(("grid", "sub"), None, None, None, None),
        P(("grid", "sub"), None, None, None),
        P(("grid", "sub"), None),
    )
    return jax.shard_map(
        on_device,
        mesh=mesh,
        in_specs=placed,
        out_specs=P(None, ("grid", "sub"), None, None),
        check_vma=False,
    )
```

```python
import functools

import jax
import jax.numpy as jnp
from jax import lax
from jax.experimental import pallas as pl
from jax.experimental.pallas import tpu as pltpu
from jax.sharding import PartitionSpec as P

ROWS = 8
LANES = 128
VMEM = pl.BlockSpec(memory_space=pltpu.VMEM)
HBM = pl.BlockSpec(memory_space=pltpu.HBM)
LIMIT = 24 << 20
EARLY = (0, 1, )


def passed_along(value, axis, steps):
    count = lax.axis_size(axis)
    pairs = [(source, (source + steps) % count) for source in range(count)]
    return lax.ppermute(value, axis, pairs)


def first_kernel(
    count_ref, cell_ref, offset_ref, node_ref, field_ref, jitter_ref,
    message_ref, code_ref, next_ref, last_ref,
    count_smem, cell_vmem, offset_vmem, node_vmem, sem,
):
    owners, points = cell_ref.shape[1], cell_ref.shape[3]
    variables, planes, rows_count, _ = field_ref.shape
    copies = [
        pltpu.make_async_copy(source, target, sem.at[k])
        for k, (source, target) in enumerate(
            (
                (count_ref, count_smem),
                (cell_ref, cell_vmem),
                (offset_ref, offset_vmem),
                (node_ref, node_vmem),
                (jitter_ref.at[:, pl.ds(0, 1)], next_ref.at[pl.ds(0, 3)]),
                (field_ref.at[:, pl.ds(0, 1)], next_ref.at[pl.ds(3, variables)]),
                (field_ref.at[:, pl.ds(planes - 1, 1)], last_ref),
            )
        )
    ]
    for copy in copies:
        copy.start()
    for copy in copies[:4]:
        copy.wait()

    spare = planes * rows_count * 8
    lane = lax.broadcasted_iota(jnp.int32, (1, points), 1)

    me = lax.axis_index("grid")

    def code(place, nodes, live):
        code_ref[pl.ds(place, 1), :] = jnp.where(live, (nodes >> 7) * 8, spare)
        code_ref[pl.ds(owners + 1 + place, 1), :] = ((nodes & 127) - lane) & 127

    def one(distance, carry):
        owner = lax.rem(me + distance, owners)
        count = count_smem[0, owner]
        cells = cell_vmem[0, owner].astype(jnp.float32)
        message_ref[owner, 0:1, :] = cells[0:1]
        message_ref[owner, 4:5, :] = cells[1:2]
        for c in range(3):
            message_ref[owner, 1 + c : 2 + c, :] = offset_vmem[0, owner, c, 0:1, :]
            message_ref[owner, 5 + c : 6 + c, :] = offset_vmem[0, owner, c, 1:2, :]
        code(distance, node_vmem[0, owner, 0:1, :], lane < count)
        return carry

    lax.fori_loop(0, owners, one, 0, unroll=True)
    heavy = lax.rem(me + 1, owners)
    code(owners, node_vmem[0, heavy, 1:2, :], lane + points < count_smem[0, heavy])
    for copy in copies[4:]:
        copy.wait()


def coefficients(corner):
    linear = [corner[4] - corner[0], corner[2] - corner[0], corner[1] - corner[0]]
    pair_01 = corner[6] - corner[4] - linear[1]
    pair_02 = corner[5] - corner[4] - linear[2]
    pair_12 = corner[3] - corner[2] - linear[2]
    triple = (corner[7] - corner[6]) - (corner[5] - corner[4]) - pair_12
    return corner[0], linear, pair_01, pair_02, pair_12, triple


def solve(corner, target):
    polys = []
    for component in range(3):
        start, linear, pair_01, pair_02, pair_12, triple = coefficients(
            [corner(q, component) for q in range(8)]
        )
        linear[component] = linear[component] + 1.0
        polys.append((start - target[component], linear, pair_01, pair_02, pair_12, triple))
    s0 = s1 = s2 = jnp.full(target[0].shape, 0.5, jnp.float32)
    for _ in range(4):
        s01, s02, s12 = s0 * s1, s0 * s2, s1 * s2
        misfit, jac = [], []
        for start, (l0, l1, l2), p01, p02, p12, triple in polys:
            d0 = l0 + s1 * p01 + s2 * p02 + s12 * triple
            d1 = l1 + s0 * p01 + s2 * p12 + s02 * triple
            d2 = l2 + s0 * p02 + s1 * p12 + s01 * triple
            misfit.append(start + s0 * d0 + s1 * (l1 + s2 * p12) + s2 * l2)
            jac.append((d0, d1, d2))
        (a0, a1, a2), (b0, b1, b2), (c0, c1, c2) = jac
        m0, m1, m2 = misfit
        bc12 = b1 * c2 - b2 * c1
        bc02 = b0 * c2 - b2 * c0
        bc01 = b0 * c1 - b1 * c0
        det = a0 * bc12 - a1 * bc02 + a2 * bc01
        bm2 = m1 * c2 - b2 * m2
        bm1 = m1 * c1 - b1 * m2
        bm0 = b0 * m2 - m1 * c0
        inverse = 1.0 / det
        u0 = m0 * bc12 - a1 * bm2 + a2 * bm1
        u1 = a0 * bm2 - m0 * bc02 + a2 * bm0
        u2 = a0 * (b1 * m2 - m1 * c1) - a1 * bm0 + m0 * bc01
        s0 = s0 - u0 * inverse
        s1 = s1 - u1 * inverse
        s2 = s2 - u2 * inverse
    values = []
    for variable in range(5):
        u = [corner(q, 3 + variable) for q in range(8)]
        e = [u[q] + s2 * (u[q + 1] - u[q]) for q in (0, 2, 4, 6)]
        f = [e[q] + s1 * (e[q + 1] - e[q]) for q in (0, 2)]
        values.append(f[0] + s0 * (f[1] - f[0]))
    return values


def lay_out(table, field_ref, jitter_ref, next_ref):
    planes, columns = field_ref.shape[1], field_ref.shape[3]

    def read(plane, variable):
        if plane == planes:
            return next_ref[variable, 0]
        return jitter_ref[variable, plane] if variable < 3 else field_ref[variable - 3, plane]

    for plane in range(planes + 1):
        for half in range(2):
            tile = jnp.concatenate([read(plane, 4 * half + w) for w in range(4)], 0).T
            first = plane * (2 * columns) + half
            table[pl.ds(first, columns, stride=2), :] = tile


def separated(tiles, lane):
    even = (lane & 1) == 0
    result = [None] * 8
    for a1 in range(2):
        block = ((lane - a1) & 127) >> 5
        held = [jnp.where(even, tiles[2 * h + a1], tiles[2 * h + 1 - a1]) for h in range(4)]
        masks = [block == h for h in range(4)]
        for w in range(4):
            tile = held[3]
            for h in range(3):
                tile = jnp.where(masks[(h + w) & 3], held[h], tile)
            distance = (LANES - 32 * w - a1) % LANES
            result[2 * w + a1] = pltpu.roll(tile, distance, 1) if distance else tile
    return result


def tile_rows(tile):
    first = tile * ROWS
    return pl.ds(first if isinstance(first, int) else pl.multiple_of(first, ROWS), ROWS)


def after(me, body):
    def once(step, carry):
        body()
        return carry

    lax.fori_loop(0, jnp.minimum(me + 1, 1), once, 0)


def each_source(owners, body):
    if owners <= 8:
        for distance in range(owners + 1):
            body(distance, 1 if distance == 2 else LANES)
    else:

        def one(distance, carry):
            body(distance, LANES)
            return carry

        lax.fori_loop(0, owners + 1, one, 0)


def gather_kernel(
    owners, field_ref, jitter_ref, next_ref, below_ref, message_ref, out_ref,
    table, message, decoded, codes, picked, parts, answers, sem,
):
    rows_count = 32
    me = lax.axis_index("grid")
    lane = lax.broadcasted_iota(jnp.int32, (ROWS, LANES), 1)
    sublane = lax.broadcasted_iota(jnp.int32, (ROWS, LANES), 0)

    def decode(cells, place):
        cells = cells.astype(jnp.int32)
        row = (cells >> 12) * (2 * LANES) + (cells & 127) * 2
        shift = (lane - ((cells >> 7) & (rows_count - 1))) & 127
        decoded[place, :] = row * LANES + shift

    def of_source(distance):
        return lax.rem(me + owners - distance, owners)

    for distance in range(owners):
        message[tile_rows(distance), :] = message_ref[tile_rows(of_source(distance)), :]
    for block in range(owners // ROWS):
        cells = message[pl.ds(block * ROWS * 8, ROWS, stride=8), :]
        decode(cells, pl.ds(block * ROWS, ROWS))
    more = jnp.broadcast_to(message[12:13, :], (ROWS, LANES))
    decode(more, pl.ds(owners, ROWS))
    copy = pltpu.make_async_copy(decoded, codes, sem)
    copy.start()
    after(me, lambda: lay_out(table, field_ref, jitter_ref, next_ref))
    copy.wait()

    low = sublane < 4
    pairs = [((lane - k) & 31) >> 1 for k in range(2)]

    def one_source(source, points, blocks=range(4)):
        for block in blocks:
            if block * 32 >= points:
                continue
            held = [None, None]
            for k in range(min(32, points)):
                code = codes[source, block * 32 + k]
                row = code >> 7
                tile = jnp.where(
                    low,
                    table[pl.ds(row, ROWS), :],
                    table[pl.ds(row + (2 * LANES - 4), ROWS), :],
                )
                tile = pltpu.roll(tile, code & 127, 1)
                k2 = k & 1
                held[k2] = tile if held[k2] is None else jnp.where(pairs[k2] == k >> 1, tile, held[k2])
            for k in range(min(2, points)):
                picked[tile_rows((2 * block + k) * (owners + 1) + source), :] = held[k]

    if owners <= 8:
        for block in range(4):
            each_source(owners, lambda source, points: one_source(source, points, [block]))
    else:
        each_source(owners, one_source)

    def one_block(block, last):
        for s in range(8):
            tiles = [
                picked[pl.ds((g * (owners + 1) + block * ROWS) * 8 + s, ROWS, stride=8), :]
                for g in range(8)
            ]
            for x, tile in enumerate(separated(tiles, lane)):
                parts[s, x] = tile
        if last:
            tiles = [picked[pl.ds((g * (owners + 1) + owners) * 8, 8), :] for g in range(8)]
            for x, tile in enumerate(separated(tiles, lane)):
                parts[8, x] = tile

        def corner(q, variable):
            a0, a1, a2 = q >> 2, (q >> 1) & 1, q & 1
            s, x = 4 * a0 + 2 * a2 + (variable >> 2), 2 * (variable & 3) + a1
            tile = parts[s, x]
            if last:
                more = jnp.broadcast_to(parts[8, x, s : s + 1, :], (ROWS, LANES))
                tile = jnp.concatenate([tile, more], 0)
            return tile

        target = []
        for c in range(3):
            tile = message[pl.ds(block * (ROWS * 8) + 1 + c, ROWS, stride=8), :]
            if last:
                more = message[13 + c : 14 + c, :]
                tile = jnp.concatenate([tile, jnp.broadcast_to(more, (ROWS, LANES))], 0)
            target.append(tile)
        values = solve(corner, target)
        for variable in range(5):
            answers[pl.ds(variable, ROWS, stride=8), :] = values[variable][:ROWS]
            if last:
                place = pl.ds(of_source(1) * 16 + 8 + variable, 1)
                out_ref[place, :] = values[variable][ROWS : ROWS + 1]
        for distance in range(ROWS):
            source = of_source(block * ROWS + distance)
            out_ref[tile_rows(2 * source), :] = answers[tile_rows(distance), :]

    for block in range(owners // ROWS):
        one_block(block, block == owners // ROWS - 1)


def relax_kernel(
    owners, code_ref, field_ref, next_ref, below_ref, ratio_ref, values_ref, out_ref,
    table, codes, rolled, plain, inverse, out_vmem, sem, out_sem,
):
    variables, planes, rows_count, _ = out_ref.shape
    width = 8
    blocks = rows_count // ROWS
    plane_rows = rows_count * width
    copy = pltpu.make_async_copy(code_ref, codes, sem)
    copy.start()
    lane = lax.broadcasted_iota(jnp.int32, (ROWS, LANES), 1)
    sublane = lax.broadcasted_iota(jnp.int32, (ROWS, LANES), 0)
    me = lax.axis_index("grid")

    def lay_out_rows():
        for plane in range(planes):
            for variable in range(variables + 1):
                tile = jnp.zeros((rows_count, LANES), jnp.float32)
                if variable < variables:
                    tile = field_ref[variable, plane]
                first = plane * plane_rows + variable
                table[pl.ds(first, rows_count, stride=width), :] = tile
            inverse[plane] = 1.0 / (1.0 + 6.0 * ratio_ref[plane])

    lane_id = lane.astype(jnp.float32)

    def values_of(distance):
        if isinstance(distance, int):
            owner = lax.rem(me + distance % owners + distance // owners, owners)
            first = owner * 16 + 8 * (distance // owners)
        else:
            more = distance == owners
            owner = lax.rem(jnp.where(more, me + 1, me + distance), owners)
            first = owner * 16 + jnp.where(more, 8, 0)
        tile = values_ref[pl.ds(pl.multiple_of(first, 8), 8), :]
        return jnp.where(sublane == variables, 1.0, tile)

    def spread(distance, points, buffer):
        column = (code_ref[pl.ds(owners + 1 + distance, 1), :] + lane[:1]) & (LANES - 1)
        tile = jnp.where(
            sublane == variables + 1, column.astype(jnp.float32), values_of(distance)
        )
        for point in range(points):
            rolled[tile_rows(buffer * LANES + point), :] = jnp.broadcast_to(
                tile[:, point : point + 1], (ROWS, LANES)
            )

    def rotate(distance, points, buffer):
        tile = values_of(distance)
        tile = jnp.where(sublane == variables + 1, lane.astype(jnp.float32), tile)
        for point in range(points):
            place = tile_rows(buffer * LANES + point)
            rolled[place, :] = pltpu.roll(tile, codes[owners + 1 + distance, point], 1)

    def store(distance, points, buffer):
        for point in range(points):
            place = (buffer * LANES + point) * ROWS
            tag = rolled[place + variables + 1 : place + variables + 2, :]
            row = pl.multiple_of(codes[distance, point], width)
            tag = jnp.broadcast_to(tag, (ROWS, LANES))
            early = isinstance(distance, int) and distance in EARLY
            pltpu.store(
                table.at[pl.ds(row, width), :],
                rolled[place : place + ROWS, :],
                mask=tag == (lane_id if early else float(point)),
            )

    if owners <= 8:
        todo = []
        each_source(owners, lambda distance, points: todo.append((distance, points, distance)))

        def meanwhile():
            lay_out_rows()
            for distance in EARLY:
                spread(distance, LANES, distance)

        after(me, meanwhile)
        copy.wait()
        late = [item for item in todo if item[0] not in EARLY]
        rotate(*late[0])
        for distance in EARLY:
            store(distance, LANES, distance)
        for now, later in zip(late, late[1:] + [None]):
            if later is not None:
                rotate(*later)
            store(*now)
    else:

        after(me, lay_out_rows)
        copy.wait()

        def one_source(distance, points):
            rotate(distance, points, 0)
            store(distance, points, 0)

        each_source(owners, one_source)

    def out_copy(plane):
        return pltpu.make_async_copy(
            out_vmem.at[:, pl.ds(plane, 1)], out_ref.at[:, pl.ds(plane, 1)], out_sem.at[plane]
        )

    def place(plane, block, variable, step=0):
        return pl.ds(ROWS + (variable * planes + plane) * rows_count + block * ROWS + step, ROWS)

    def flat(plane):
        for block in range(blocks):
            for variable in range(variables):
                first = plane * plane_rows + block * ROWS * width + variable
                plain[place(plane, block, variable), :] = table[pl.ds(first, ROWS, stride=width), :]

    def one_plane(plane):
        for block in range(blocks):
            rows = pl.ds(block * ROWS, ROWS)
            ratio, divisor = ratio_ref[plane, rows, :], inverse[plane, rows, :]
            first = plane * plane_rows + block * ROWS * width + variables
            fringe = table[pl.ds(first, ROWS, stride=width), :] > 0.5
            for variable in range(variables):
                here = plain[place(plane, block, variable), :]
                up = plain[place(plane, block, variable, 1), :]
                down = plain[place(plane, block, variable, -1), :]
                if block == 0:
                    down = jnp.where(sublane == 0, 0.0, down)
                if block == blocks - 1:
                    up = jnp.where(sublane == ROWS - 1, 0.0, up)
                right = jnp.where(lane == LANES - 1, 0.0, pltpu.roll(here, LANES - 1, 1))
                left = jnp.where(lane == 0, 0.0, pltpu.roll(here, 1, 1))
                if plane == 0:
                    below = below_ref[variable, 0, rows, :]
                else:
                    below = plain[place(plane - 1, block, variable), :]
                if plane == planes - 1:
                    above = next_ref[3 + variable, 0, rows, :]
                else:
                    above = plain[place(plane + 1, block, variable), :]
                total = (above + below) + (up + down) + (right + left)
                smooth = (here + ratio * total) * divisor
                out_vmem[variable, plane, rows, :] = jnp.where(fringe, here, smooth)
        out_copy(plane).start()

    flat(0)
    for plane in range(planes):
        if plane < planes - 1:
            flat(plane + 1)
        one_plane(plane)
    for plane in range(planes):
        out_copy(plane).wait()


def on_device(
    field, node_jitter, time_ratio, donor_cell, receptor_offset, receptor_node, point_count
):
    variables, planes, rows_count, cols_count = field.shape
    owners, points = donor_cell.shape[1], donor_cell.shape[3]
    params = pltpu.CompilerParams(vmem_limit_bytes=LIMIT)
    offsets = jnp.swapaxes(receptor_offset, 2, 3)
    f32, i32 = jnp.float32, jnp.int32
    message, codes, first, last = pl.pallas_call(
        first_kernel,
        out_shape=[
            jax.ShapeDtypeStruct((owners, 8, LANES), f32),
            jax.ShapeDtypeStruct((2 * owners + 8, LANES), i32),
            jax.ShapeDtypeStruct((3 + variables, 1, rows_count, cols_count), f32),
            jax.ShapeDtypeStruct((variables, 1, rows_count, cols_count), f32),
        ],
        in_specs=[HBM] * 6,
        out_specs=[VMEM] * 4,
        scratch_shapes=[
            pltpu.SMEM(point_count.shape, i32),
            pltpu.VMEM(donor_cell.shape, i32),
            pltpu.VMEM(offsets.shape, f32),
            pltpu.VMEM(receptor_node.shape, i32),
            pltpu.SemaphoreType.DMA((7,)),
        ],
        compiler_params=params,
        name="first",
    )(*[
        pltpu.with_memory_space_constraint(x, pltpu.HBM)
        for x in (point_count, donor_cell, offsets, receptor_node, field, node_jitter)
    ])
    following = passed_along(first, "sub", -1)
    below = passed_along(last, "sub", 1)
    message = lax.all_to_all(message, "grid", split_axis=0, concat_axis=0, tiled=True)
    values = pl.pallas_call(
        functools.partial(gather_kernel, owners),
        out_shape=jax.ShapeDtypeStruct((owners * 16, LANES), f32),
        in_specs=[VMEM] * 5,
        out_specs=VMEM,
        scratch_shapes=[
            pltpu.VMEM(((planes + 1) * cols_count * 2, LANES), f32),
            pltpu.VMEM((owners * 8, LANES), f32),
            pltpu.VMEM((owners + 8, LANES), i32),
            pltpu.SMEM((owners + 8, LANES), i32),
            pltpu.VMEM((8 * (owners + 1) * 8, LANES), f32),
            pltpu.VMEM((9, 8, ROWS, LANES), f32),
            pltpu.VMEM((ROWS * 8, LANES), f32),
            pltpu.SemaphoreType.DMA,
        ],
        compiler_params=params,
        name="gather",
    )(field, node_jitter, following, below, message.reshape(owners * 8, LANES))
    values = values.reshape(owners, 16, LANES)
    values = lax.all_to_all(values, "grid", split_axis=0, concat_axis=0, tiled=True)
    return pl.pallas_call(
        functools.partial(relax_kernel, owners),
        out_shape=jax.ShapeDtypeStruct(field.shape, f32),
        in_specs=[VMEM] * 6,
        out_specs=HBM,
        scratch_shapes=[
            pltpu.VMEM((planes * rows_count * 8 + 8, LANES), f32),
            pltpu.SMEM(codes.shape, i32),
            pltpu.VMEM(((owners + 1 if owners <= 8 else 1) * LANES * ROWS, LANES), f32),
            pltpu.VMEM((variables * planes * rows_count + 2 * ROWS, LANES), f32),
            pltpu.VMEM(time_ratio.shape, f32),
            pltpu.VMEM(field.shape, f32),
            pltpu.SemaphoreType.DMA,
            pltpu.SemaphoreType.DMA((planes,)),
        ],
        compiler_params=params,
        name="relax",
    )(codes, field, following, below, time_ratio, values.reshape(owners * 16, LANES))


def solution(mesh):
    placed = (
        P(None, ("grid", "sub"), None, None),
        P(None, ("grid", "sub"), None, None),
        P(("grid", "sub"), None, None),
        P(("grid", "sub"), None, None, None),
        P(("grid", "sub"), None, None, None, None),
        P(("grid", "sub"), None, None, None),
        P(("grid", "sub"), None),
    )
    return jax.shard_map(
        on_device,
        mesh=mesh,
        in_specs=placed,
        out_specs=P(None, ("grid", "sub"), None, None),
        check_vma=False,
    )
```

```python
import functools

import jax
import jax.numpy as jnp
from jax import lax
from jax.experimental import pallas as pl
from jax.experimental.pallas import tpu as pltpu
from jax.sharding import PartitionSpec as P

ROWS = 8
LANES = 128
VMEM = pl.BlockSpec(memory_space=pltpu.VMEM)
HBM = pl.BlockSpec(memory_space=pltpu.HBM)
LIMIT = 24 << 20
EARLY = (0, 1, 3,)


def passed_along(value, axis, steps):
    count = lax.axis_size(axis)
    pairs = [(source, (source + steps) % count) for source in range(count)]
    return lax.ppermute(value, axis, pairs)


def first_kernel(
    count_ref, cell_ref, offset_ref, node_ref, field_ref, jitter_ref,
    message_ref, code_ref, next_ref, last_ref,
    count_smem, cell_vmem, offset_vmem, node_vmem, sem,
):
    owners, points = cell_ref.shape[1], cell_ref.shape[3]
    variables, planes, rows_count, _ = field_ref.shape
    copies = [
        pltpu.make_async_copy(source, target, sem.at[k])
        for k, (source, target) in enumerate(
            (
                (jitter_ref.at[:, pl.ds(0, 1)], next_ref.at[pl.ds(0, 3)]),
                (field_ref.at[:, pl.ds(0, 1)], next_ref.at[pl.ds(3, variables)]),
                (field_ref.at[:, pl.ds(planes - 1, 1)], last_ref),
                (count_ref, count_smem),
                (cell_ref, cell_vmem),
                (offset_ref, offset_vmem),
                (node_ref, node_vmem),
            )
        )
    ]
    for copy in copies:
        copy.start()
    for copy in copies[3:]:
        copy.wait()

    spare = planes * rows_count * 8
    lane = lax.broadcasted_iota(jnp.int32, (1, points), 1)

    me = lax.axis_index("grid")

    def code(place, nodes, live):
        code_ref[pl.ds(place, 1), :] = jnp.where(live, (nodes >> 7) * 8, spare)
        code_ref[pl.ds(owners + 1 + place, 1), :] = ((nodes & 127) - lane) & 127

    def one(distance, carry):
        owner = lax.rem(me + distance, owners)
        count = count_smem[0, owner]
        cells = cell_vmem[0, owner].astype(jnp.float32)
        message_ref[owner, 0:1, :] = cells[0:1]
        message_ref[owner, 4:5, :] = cells[1:2]
        for c in range(3):
            message_ref[owner, 1 + c : 2 + c, :] = offset_vmem[0, owner, c, 0:1, :]
            message_ref[owner, 5 + c : 6 + c, :] = offset_vmem[0, owner, c, 1:2, :]
        code(distance, node_vmem[0, owner, 0:1, :], lane < count)
        return carry

    lax.fori_loop(0, owners, one, 0, unroll=True)
    heavy = lax.rem(me + 1, owners)
    code(owners, node_vmem[0, heavy, 1:2, :], lane + points < count_smem[0, heavy])
    for copy in copies[:3]:
        copy.wait()


def coefficients(corner):
    linear = [corner[4] - corner[0], corner[2] - corner[0], corner[1] - corner[0]]
    pair_01 = corner[6] - corner[4] - linear[1]
    pair_02 = corner[5] - corner[4] - linear[2]
    pair_12 = corner[3] - corner[2] - linear[2]
    triple = (corner[7] - corner[6]) - (corner[5] - corner[4]) - pair_12
    return corner[0], linear, pair_01, pair_02, pair_12, triple


def solve(corner, target):
    polys = []
    for component in range(3):
        start, linear, pair_01, pair_02, pair_12, triple = coefficients(
            [corner(q, component) for q in range(8)]
        )
        linear[component] = linear[component] + 1.0
        polys.append((start - target[component], linear, pair_01, pair_02, pair_12, triple))
    s0 = s1 = s2 = jnp.full(target[0].shape, 0.5, jnp.float32)
    for _ in range(4):
        s01, s02, s12 = s0 * s1, s0 * s2, s1 * s2
        misfit, jac = [], []
        for start, (l0, l1, l2), p01, p02, p12, triple in polys:
            d0 = l0 + s1 * p01 + s2 * p02 + s12 * triple
            d1 = l1 + s0 * p01 + s2 * p12 + s02 * triple
            d2 = l2 + s0 * p02 + s1 * p12 + s01 * triple
            misfit.append(start + s0 * d0 + s1 * (l1 + s2 * p12) + s2 * l2)
            jac.append((d0, d1, d2))
        (a0, a1, a2), (b0, b1, b2), (c0, c1, c2) = jac
        m0, m1, m2 = misfit
        bc12 = b1 * c2 - b2 * c1
        bc02 = b0 * c2 - b2 * c0
        bc01 = b0 * c1 - b1 * c0
        det = a0 * bc12 - a1 * bc02 + a2 * bc01
        bm2 = m1 * c2 - b2 * m2
        bm1 = m1 * c1 - b1 * m2
        bm0 = b0 * m2 - m1 * c0
        inverse = 1.0 / det
        u0 = m0 * bc12 - a1 * bm2 + a2 * bm1
        u1 = a0 * bm2 - m0 * bc02 + a2 * bm0
        u2 = a0 * (b1 * m2 - m1 * c1) - a1 * bm0 + m0 * bc01
        s0 = s0 - u0 * inverse
        s1 = s1 - u1 * inverse
        s2 = s2 - u2 * inverse
    values = []
    for variable in range(5):
        u = [corner(q, 3 + variable) for q in range(8)]
        e = [u[q] + s2 * (u[q + 1] - u[q]) for q in (0, 2, 4, 6)]
        f = [e[q] + s1 * (e[q + 1] - e[q]) for q in (0, 2)]
        values.append(f[0] + s0 * (f[1] - f[0]))
    return values


def lay_out(table, field_ref, jitter_ref, next_ref):
    planes, columns = field_ref.shape[1], field_ref.shape[3]

    def read(plane, variable):
        if plane == planes:
            return next_ref[variable, 0]
        return jitter_ref[variable, plane] if variable < 3 else field_ref[variable - 3, plane]

    for plane in range(planes + 1):
        for half in range(2):
            tile = jnp.concatenate([read(plane, 4 * half + w) for w in range(4)], 0).T
            first = plane * (2 * columns) + half
            table[pl.ds(first, columns, stride=2), :] = tile


def separated(tiles, lane):
    even = (lane & 1) == 0
    result = [None] * 8
    for a1 in range(2):
        block = ((lane - a1) & 127) >> 5
        held = [jnp.where(even, tiles[2 * h + a1], tiles[2 * h + 1 - a1]) for h in range(4)]
        masks = [block == h for h in range(4)]
        for w in range(4):
            tile = held[3]
            for h in range(3):
                tile = jnp.where(masks[(h + w) & 3], held[h], tile)
            distance = (LANES - 32 * w - a1) % LANES
            result[2 * w + a1] = pltpu.roll(tile, distance, 1) if distance else tile
    return result


def tile_rows(tile):
    first = tile * ROWS
    return pl.ds(first if isinstance(first, int) else pl.multiple_of(first, ROWS), ROWS)


def after(me, body):
    def once(step, carry):
        body()
        return carry

    lax.fori_loop(0, jnp.minimum(me + 1, 1), once, 0)


def each_source(owners, body):
    if owners <= 8:
        for distance in range(owners + 1):
            body(distance, 1 if distance == 2 else LANES)
    else:

        def one(distance, carry):
            body(distance, LANES)
            return carry

        lax.fori_loop(0, owners + 1, one, 0)


def gather_kernel(
    owners, field_ref, jitter_ref, next_ref, below_ref, message_ref, out_ref,
    table, message, decoded, codes, picked, parts, answers, sem,
):
    rows_count = 32
    me = lax.axis_index("grid")
    lane = lax.broadcasted_iota(jnp.int32, (ROWS, LANES), 1)
    sublane = lax.broadcasted_iota(jnp.int32, (ROWS, LANES), 0)

    def decode(cells, place):
        cells = cells.astype(jnp.int32)
        row = (cells >> 12) * (2 * LANES) + (cells & 127) * 2
        shift = (lane - ((cells >> 7) & (rows_count - 1))) & 127
        decoded[place, :] = row * LANES + shift

    def of_source(distance):
        return lax.rem(me + owners - distance, owners)

    for distance in range(owners):
        message[tile_rows(distance), :] = message_ref[tile_rows(of_source(distance)), :]
    for block in range(owners // ROWS):
        cells = message[pl.ds(block * ROWS * 8, ROWS, stride=8), :]
        decode(cells, pl.ds(block * ROWS, ROWS))
    more = jnp.broadcast_to(message[12:13, :], (ROWS, LANES))
    decode(more, pl.ds(owners, ROWS))
    needed = pl.ds(0, owners + 1)
    copy = pltpu.make_async_copy(decoded.at[needed], codes.at[needed], sem)
    copy.start()
    after(me, lambda: lay_out(table, field_ref, jitter_ref, next_ref))
    copy.wait()

    low = sublane < 4
    pairs = [((lane - k) & 31) >> 1 for k in range(2)]

    def one_source(source, points, blocks=range(4)):
        for block in blocks:
            if block * 32 >= points:
                continue
            held = [None, None]
            for k in range(min(32, points)):
                code = codes[source, block * 32 + k]
                row = code >> 7
                tile = jnp.where(
                    low,
                    table[pl.ds(row, ROWS), :],
                    table[pl.ds(row + (2 * LANES - 4), ROWS), :],
                )
                tile = pltpu.roll(tile, code & 127, 1)
                k2 = k & 1
                held[k2] = tile if held[k2] is None else jnp.where(pairs[k2] == k >> 1, tile, held[k2])
            for k in range(min(2, points)):
                picked[tile_rows((2 * block + k) * (owners + 1) + source), :] = held[k]

    if owners <= 8:
        for block in range(4):
            each_source(owners, lambda source, points: one_source(source, points, [block]))
    else:
        each_source(owners, one_source)

    def one_block(block, last):
        for s in range(8):
            tiles = [
                picked[pl.ds((g * (owners + 1) + block * ROWS) * 8 + s, ROWS, stride=8), :]
                for g in range(8)
            ]
            for x, tile in enumerate(separated(tiles, lane)):
                parts[s, x] = tile
        if last:
            tiles = [picked[pl.ds((g * (owners + 1) + owners) * 8, 8), :] for g in range(8)]
            for x, tile in enumerate(separated(tiles, lane)):
                parts[8, x] = tile

        def corner(q, variable):
            a0, a1, a2 = q >> 2, (q >> 1) & 1, q & 1
            s, x = 4 * a0 + 2 * a2 + (variable >> 2), 2 * (variable & 3) + a1
            tile = parts[s, x]
            if last:
                more = jnp.broadcast_to(parts[8, x, s : s + 1, :], (ROWS, LANES))
                tile = jnp.concatenate([tile, more], 0)
            return tile

        target = []
        for c in range(3):
            tile = message[pl.ds(block * (ROWS * 8) + 1 + c, ROWS, stride=8), :]
            if last:
                more = message[13 + c : 14 + c, :]
                tile = jnp.concatenate([tile, jnp.broadcast_to(more, (ROWS, LANES))], 0)
            target.append(tile)
        values = solve(corner, target)
        for variable in range(5):
            answers[pl.ds(variable, ROWS, stride=8), :] = values[variable][:ROWS]
            if last:
                place = pl.ds(of_source(1) * 16 + 8 + variable, 1)
                out_ref[place, :] = values[variable][ROWS : ROWS + 1]
        for distance in range(ROWS):
            source = of_source(block * ROWS + distance)
            out_ref[tile_rows(2 * source), :] = answers[tile_rows(distance), :]

    for block in range(owners // ROWS):
        one_block(block, block == owners // ROWS - 1)


def relax_kernel(
    owners, code_ref, field_ref, next_ref, below_ref, ratio_ref, values_ref, out_ref,
    table, codes, rolled, plain, inverse, out_vmem, sem, out_sem,
):
    variables, planes, rows_count, _ = out_ref.shape
    width = 8
    blocks = rows_count // ROWS
    plane_rows = rows_count * width
    needed = pl.ds(0, 2 * owners + 2)
    copy = pltpu.make_async_copy(code_ref.at[needed], codes.at[needed], sem)
    copy.start()
    lane = lax.broadcasted_iota(jnp.int32, (ROWS, LANES), 1)
    sublane = lax.broadcasted_iota(jnp.int32, (ROWS, LANES), 0)
    me = lax.axis_index("grid")

    def lay_out_rows():
        for plane in range(planes):
            for variable in range(variables + 1):
                tile = jnp.zeros((rows_count, LANES), jnp.float32)
                if variable < variables:
                    tile = field_ref[variable, plane]
                first = plane * plane_rows + variable
                table[pl.ds(first, rows_count, stride=width), :] = tile
            inverse[plane] = 1.0 / (1.0 + 6.0 * ratio_ref[plane])

    lane_id = lane.astype(jnp.float32)

    def values_of(distance):
        if isinstance(distance, int):
            owner = lax.rem(me + distance % owners + distance // owners, owners)
            first = owner * 16 + 8 * (distance // owners)
        else:
            more = distance == owners
            owner = lax.rem(jnp.where(more, me + 1, me + distance), owners)
            first = owner * 16 + jnp.where(more, 8, 0)
        tile = values_ref[pl.ds(pl.multiple_of(first, 8), 8), :]
        return jnp.where(sublane == variables, 1.0, tile)

    def spread(distances):
        tiles = []
        for distance in distances:
            column = (code_ref[pl.ds(owners + 1 + distance, 1), :] + lane[:1]) & (LANES - 1)
            column = column.astype(jnp.float32)
            tiles.append(jnp.where(sublane == variables + 1, column, values_of(distance)))
        for point in range(LANES):
            for distance, tile in zip(distances, tiles):
                rolled[tile_rows(distance * LANES + point), :] = jnp.broadcast_to(
                    tile[:, point : point + 1], (ROWS, LANES)
                )

    def rotate(distance, points, buffer):
        tile = values_of(distance)
        tile = jnp.where(sublane == variables + 1, lane.astype(jnp.float32), tile)
        for point in range(points):
            place = tile_rows(buffer * LANES + point)
            rolled[place, :] = pltpu.roll(tile, codes[owners + 1 + distance, point], 1)

    def store(distance, points, buffer):
        for point in range(points):
            place = (buffer * LANES + point) * ROWS
            tag = rolled[place + variables + 1 : place + variables + 2, :]
            row = pl.multiple_of(codes[distance, point], width)
            tag = jnp.broadcast_to(tag, (ROWS, LANES))
            early = isinstance(distance, int) and distance in EARLY
            pltpu.store(
                table.at[pl.ds(row, width), :],
                rolled[place : place + ROWS, :],
                mask=tag == (lane_id if early else float(point)),
            )

    if owners <= 8:
        todo = []
        each_source(owners, lambda distance, points: todo.append((distance, points, distance)))

        def meanwhile():
            lay_out_rows()
            spread(EARLY)

        after(me, meanwhile)
        copy.wait()
        late = [item for item in todo if item[0] not in EARLY]
        rotate(*late[0])
        for distance in EARLY:
            store(distance, LANES, distance)
        for now, later in zip(late, late[1:] + [None]):
            if later is not None:
                rotate(*later)
            store(*now)
    else:

        after(me, lay_out_rows)
        copy.wait()

        def one_source(distance, points):
            rotate(distance, points, 0)
            store(distance, points, 0)

        each_source(owners, one_source)

    def out_copy(plane):
        return pltpu.make_async_copy(
            out_vmem.at[:, pl.ds(plane, 1)], out_ref.at[:, pl.ds(plane, 1)], out_sem.at[plane]
        )

    def place(plane, block, variable, step=0):
        return pl.ds(ROWS + (variable * planes + plane) * rows_count + block * ROWS + step, ROWS)

    def flat(plane):
        for block in range(blocks):
            for variable in range(variables):
                first = plane * plane_rows + block * ROWS * width + variable
                plain[place(plane, block, variable), :] = table[pl.ds(first, ROWS, stride=width), :]

    def one_plane(plane):
        for block in range(blocks):
            rows = pl.ds(block * ROWS, ROWS)
            ratio, divisor = ratio_ref[plane, rows, :], inverse[plane, rows, :]
            first = plane * plane_rows + block * ROWS * width + variables
            fringe = table[pl.ds(first, ROWS, stride=width), :] > 0.5
            for variable in range(variables):
                here = plain[place(plane, block, variable), :]
                up = plain[place(plane, block, variable, 1), :]
                down = plain[place(plane, block, variable, -1), :]
                if block == 0:
                    down = jnp.where(sublane == 0, 0.0, down)
                if block == blocks - 1:
                    up = jnp.where(sublane == ROWS - 1, 0.0, up)
                right = jnp.where(lane == LANES - 1, 0.0, pltpu.roll(here, LANES - 1, 1))
                left = jnp.where(lane == 0, 0.0, pltpu.roll(here, 1, 1))
                if plane == 0:
                    below = below_ref[variable, 0, rows, :]
                else:
                    below = plain[place(plane - 1, block, variable), :]
                if plane == planes - 1:
                    above = next_ref[3 + variable, 0, rows, :]
                else:
                    above = plain[place(plane + 1, block, variable), :]
                total = (above + below) + (up + down) + (right + left)
                smooth = (here + ratio * total) * divisor
                out_vmem[variable, plane, rows, :] = jnp.where(fringe, here, smooth)
        out_copy(plane).start()

    flat(0)
    for plane in range(planes):
        if plane < planes - 1:
            flat(plane + 1)
        one_plane(plane)
    for plane in range(planes):
        out_copy(plane).wait()


def on_device(
    field, node_jitter, time_ratio, donor_cell, receptor_offset, receptor_node, point_count
):
    variables, planes, rows_count, cols_count = field.shape
    owners, points = donor_cell.shape[1], donor_cell.shape[3]
    params = pltpu.CompilerParams(vmem_limit_bytes=LIMIT)
    offsets = jnp.swapaxes(receptor_offset, 2, 3)
    f32, i32 = jnp.float32, jnp.int32
    message, codes, first, last = pl.pallas_call(
        first_kernel,
        out_shape=[
            jax.ShapeDtypeStruct((owners, 8, LANES), f32),
            jax.ShapeDtypeStruct((2 * owners + 8, LANES), i32),
            jax.ShapeDtypeStruct((3 + variables, 1, rows_count, cols_count), f32),
            jax.ShapeDtypeStruct((variables, 1, rows_count, cols_count), f32),
        ],
        in_specs=[HBM] * 6,
        out_specs=[VMEM] * 4,
        scratch_shapes=[
            pltpu.SMEM(point_count.shape, i32),
            pltpu.VMEM(donor_cell.shape, i32),
            pltpu.VMEM(offsets.shape, f32),
            pltpu.VMEM(receptor_node.shape, i32),
            pltpu.SemaphoreType.DMA((7,)),
        ],
        compiler_params=params,
        name="first",
    )(*[
        pltpu.with_memory_space_constraint(x, pltpu.HBM)
        for x in (point_count, donor_cell, offsets, receptor_node, field, node_jitter)
    ])
    following = passed_along(first, "sub", -1)
    below = passed_along(last, "sub", 1)
    message = lax.all_to_all(message, "grid", split_axis=0, concat_axis=0, tiled=True)
    values = pl.pallas_call(
        functools.partial(gather_kernel, owners),
        out_shape=jax.ShapeDtypeStruct((owners * 16, LANES), f32),
        in_specs=[VMEM] * 5,
        out_specs=VMEM,
        scratch_shapes=[
            pltpu.VMEM(((planes + 1) * cols_count * 2, LANES), f32),
            pltpu.VMEM((owners * 8, LANES), f32),
            pltpu.VMEM((owners + 8, LANES), i32),
            pltpu.SMEM((owners + 8, LANES), i32),
            pltpu.VMEM((8 * (owners + 1) * 8, LANES), f32),
            pltpu.VMEM((9, 8, ROWS, LANES), f32),
            pltpu.VMEM((ROWS * 8, LANES), f32),
            pltpu.SemaphoreType.DMA,
        ],
        compiler_params=params,
        name="gather",
    )(field, node_jitter, following, below, message.reshape(owners * 8, LANES))
    values = values.reshape(owners, 16, LANES)
    values = lax.all_to_all(values, "grid", split_axis=0, concat_axis=0, tiled=True)
    return pl.pallas_call(
        functools.partial(relax_kernel, owners),
        out_shape=jax.ShapeDtypeStruct(field.shape, f32),
        in_specs=[VMEM] * 6,
        out_specs=HBM,
        scratch_shapes=[
            pltpu.VMEM((planes * rows_count * 8 + 8, LANES), f32),
            pltpu.SMEM(codes.shape, i32),
            pltpu.VMEM(((owners + 1 if owners <= 8 else 1) * LANES * ROWS, LANES), f32),
            pltpu.VMEM((variables * planes * rows_count + 2 * ROWS, LANES), f32),
            pltpu.VMEM(time_ratio.shape, f32),
            pltpu.VMEM(field.shape, f32),
            pltpu.SemaphoreType.DMA,
            pltpu.SemaphoreType.DMA((planes,)),
        ],
        compiler_params=params,
        name="relax",
    )(codes, field, following, below, time_ratio, values.reshape(owners * 16, LANES))


def solution(mesh):
    placed = (
        P(None, ("grid", "sub"), None, None),
        P(None, ("grid", "sub"), None, None),
        P(("grid", "sub"), None, None),
        P(("grid", "sub"), None, None, None),
        P(("grid", "sub"), None, None, None, None),
        P(("grid", "sub"), None, None, None),
        P(("grid", "sub"), None),
    )
    return jax.shard_map(
        on_device,
        mesh=mesh,
        in_specs=placed,
        out_specs=P(None, ("grid", "sub"), None, None),
        check_vma=False,
    )
```

```python
import functools

import jax
import jax.numpy as jnp
from jax import lax
from jax.experimental import pallas as pl
from jax.experimental.pallas import tpu as pltpu
from jax.sharding import PartitionSpec as P

ROWS = 8
LANES = 128
VMEM = pl.BlockSpec(memory_space=pltpu.VMEM)
HBM = pl.BlockSpec(memory_space=pltpu.HBM)
LIMIT = 24 << 20
EARLY = (0, 1, 3,)


def passed_along(value, axis, steps):
    count = lax.axis_size(axis)
    pairs = [(source, (source + steps) % count) for source in range(count)]
    return lax.ppermute(value, axis, pairs)


def first_kernel(
    count_ref, cell_ref, offset_ref, node_ref, field_ref, jitter_ref,
    message_ref, code_ref, next_ref, last_ref,
    count_smem, cell_vmem, offset_vmem, node_vmem, sem,
):
    owners, points = cell_ref.shape[1], cell_ref.shape[3]
    variables, planes, rows_count, _ = field_ref.shape
    copies = [
        pltpu.make_async_copy(source, target, sem.at[k])
        for k, (source, target) in enumerate(
            (
                (jitter_ref.at[:, pl.ds(0, 1)], next_ref.at[pl.ds(0, 3)]),
                (field_ref.at[:, pl.ds(0, 1)], next_ref.at[pl.ds(3, variables)]),
                (field_ref.at[:, pl.ds(planes - 1, 1)], last_ref),
                (count_ref, count_smem),
                (cell_ref, cell_vmem),
                (offset_ref, offset_vmem),
                (node_ref, node_vmem),
            )
        )
    ]
    for copy in copies:
        copy.start()
    for copy in copies[3:]:
        copy.wait()

    spare = planes * rows_count * 8
    lane = lax.broadcasted_iota(jnp.int32, (1, points), 1)

    me = lax.axis_index("grid")

    def code(place, nodes, live):
        code_ref[pl.ds(place, 1), :] = jnp.where(live, (nodes >> 7) * 8, spare)
        code_ref[pl.ds(owners + 1 + place, 1), :] = ((nodes & 127) - lane) & 127

    def one(distance, carry):
        owner = lax.rem(me + distance, owners)
        count = count_smem[0, owner]
        cells = cell_vmem[0, owner].astype(jnp.float32)
        message_ref[owner, 0:1, :] = cells[0:1]
        counts = jnp.full((1, points), count, jnp.int32).astype(jnp.float32)
        message_ref[owner, 4:5, :] = jnp.where(distance == 1, cells[1:2], counts)
        for c in range(3):
            message_ref[owner, 1 + c : 2 + c, :] = offset_vmem[0, owner, c, 0:1, :]
            message_ref[owner, 5 + c : 6 + c, :] = offset_vmem[0, owner, c, 1:2, :]
        code(distance, node_vmem[0, owner, 0:1, :], lane < count)
        return carry

    lax.fori_loop(0, owners, one, 0, unroll=True)
    heavy = lax.rem(me + 1, owners)
    code(owners, node_vmem[0, heavy, 1:2, :], lane + points < count_smem[0, heavy])
    for copy in copies[:3]:
        copy.wait()


def coefficients(corner):
    linear = [corner[4] - corner[0], corner[2] - corner[0], corner[1] - corner[0]]
    pair_01 = corner[6] - corner[4] - linear[1]
    pair_02 = corner[5] - corner[4] - linear[2]
    pair_12 = corner[3] - corner[2] - linear[2]
    triple = (corner[7] - corner[6]) - (corner[5] - corner[4]) - pair_12
    return corner[0], linear, pair_01, pair_02, pair_12, triple


def solve(corner, target):
    polys = []
    for component in range(3):
        start, linear, pair_01, pair_02, pair_12, triple = coefficients(
            [corner(q, component) for q in range(8)]
        )
        linear[component] = linear[component] + 1.0
        polys.append((start - target[component], linear, pair_01, pair_02, pair_12, triple))
    s0 = s1 = s2 = jnp.full(target[0].shape, 0.5, jnp.float32)
    for _ in range(4):
        s01, s02, s12 = s0 * s1, s0 * s2, s1 * s2
        misfit, jac = [], []
        for start, (l0, l1, l2), p01, p02, p12, triple in polys:
            d0 = l0 + s1 * p01 + s2 * p02 + s12 * triple
            d1 = l1 + s0 * p01 + s2 * p12 + s02 * triple
            d2 = l2 + s0 * p02 + s1 * p12 + s01 * triple
            misfit.append(start + s0 * d0 + s1 * (l1 + s2 * p12) + s2 * l2)
            jac.append((d0, d1, d2))
        (a0, a1, a2), (b0, b1, b2), (c0, c1, c2) = jac
        m0, m1, m2 = misfit
        bc12 = b1 * c2 - b2 * c1
        bc02 = b0 * c2 - b2 * c0
        bc01 = b0 * c1 - b1 * c0
        det = a0 * bc12 - a1 * bc02 + a2 * bc01
        bm2 = m1 * c2 - b2 * m2
        bm1 = m1 * c1 - b1 * m2
        bm0 = b0 * m2 - m1 * c0
        inverse = 1.0 / det
        u0 = m0 * bc12 - a1 * bm2 + a2 * bm1
        u1 = a0 * bm2 - m0 * bc02 + a2 * bm0
        u2 = a0 * (b1 * m2 - m1 * c1) - a1 * bm0 + m0 * bc01
        s0 = s0 - u0 * inverse
        s1 = s1 - u1 * inverse
        s2 = s2 - u2 * inverse
    values = []
    for variable in range(5):
        u = [corner(q, 3 + variable) for q in range(8)]
        e = [u[q] + s2 * (u[q + 1] - u[q]) for q in (0, 2, 4, 6)]
        f = [e[q] + s1 * (e[q + 1] - e[q]) for q in (0, 2)]
        values.append(f[0] + s0 * (f[1] - f[0]))
    return values


def lay_out(table, field_ref, jitter_ref, next_ref):
    planes, columns = field_ref.shape[1], field_ref.shape[3]

    def read(plane, variable):
        if plane == planes:
            return next_ref[variable, 0]
        return jitter_ref[variable, plane] if variable < 3 else field_ref[variable - 3, plane]

    for plane in range(planes + 1):
        for half in range(2):
            tile = jnp.concatenate([read(plane, 4 * half + w) for w in range(4)], 0).T
            first = plane * (2 * columns) + half
            table[pl.ds(first, columns, stride=2), :] = tile


def separated(tiles, lane):
    even = (lane & 1) == 0
    result = [None] * 8
    for a1 in range(2):
        block = ((lane - a1) & 127) >> 5
        held = [jnp.where(even, tiles[2 * h + a1], tiles[2 * h + 1 - a1]) for h in range(4)]
        masks = [block == h for h in range(4)]
        for w in range(4):
            tile = held[3]
            for h in range(3):
                tile = jnp.where(masks[(h + w) & 3], held[h], tile)
            distance = (LANES - 32 * w - a1) % LANES
            result[2 * w + a1] = pltpu.roll(tile, distance, 1) if distance else tile
    return result


def tile_rows(tile):
    first = tile * ROWS
    return pl.ds(first if isinstance(first, int) else pl.multiple_of(first, ROWS), ROWS)


def after(me, body):
    def once(step, carry):
        body()
        return carry

    lax.fori_loop(0, jnp.minimum(me + 1, 1), once, 0)


def each_source(owners, body):
    if owners <= 8:
        for distance in range(owners + 1):
            body(distance, 1 if distance == 2 else LANES)
    else:

        def one(distance, carry):
            body(distance, LANES)
            return carry

        lax.fori_loop(0, owners + 1, one, 0)


def gather_kernel(
    owners, field_ref, jitter_ref, next_ref, below_ref, message_ref, out_ref,
    table, message, decoded, codes, picked, parts, answers, sem,
):
    rows_count = 32
    me = lax.axis_index("grid")
    lane = lax.broadcasted_iota(jnp.int32, (ROWS, LANES), 1)
    sublane = lax.broadcasted_iota(jnp.int32, (ROWS, LANES), 0)

    def decode(cells, place):
        cells = cells.astype(jnp.int32)
        row = (cells >> 12) * (2 * LANES) + (cells & 127) * 2
        shift = (lane - ((cells >> 7) & (rows_count - 1))) & 127
        decoded[place, :] = row * LANES + shift

    def of_source(distance):
        return lax.rem(me + owners - distance, owners)

    for distance in range(owners):
        message[tile_rows(distance), :] = message_ref[tile_rows(of_source(distance)), :]
    for block in range(owners // ROWS):
        cells = message[pl.ds(block * ROWS * 8, ROWS, stride=8), :]
        decode(cells, pl.ds(block * ROWS, ROWS))
    more = jnp.broadcast_to(message[12:13, :], (ROWS, LANES))
    decode(more, pl.ds(owners, ROWS))
    most = jnp.where(sublane == 1, 0.0, message[pl.ds(4, ROWS, stride=8), :])
    most = jnp.max(most, axis=0, keepdims=True).astype(jnp.int32)
    decoded[owners + 1 : owners + 2, :] = most
    needed = pl.ds(0, owners + 2)
    copy = pltpu.make_async_copy(decoded.at[needed], codes.at[needed], sem)
    copy.start()
    after(me, lambda: lay_out(table, field_ref, jitter_ref, next_ref))
    copy.wait()

    low = sublane < 4
    pairs = [((lane - k) & 31) >> 1 for k in range(2)]

    def one_source(source, points, blocks=range(4)):
        for block in blocks:
            if block * 32 >= points:
                continue
            held = [None, None]
            for k in range(min(32, points)):
                code = codes[source, block * 32 + k]
                row = code >> 7
                tile = jnp.where(
                    low,
                    table[pl.ds(row, ROWS), :],
                    table[pl.ds(row + (2 * LANES - 4), ROWS), :],
                )
                tile = pltpu.roll(tile, code & 127, 1)
                k2 = k & 1
                held[k2] = tile if held[k2] is None else jnp.where(pairs[k2] == k >> 1, tile, held[k2])
            for k in range(min(2, points)):
                picked[tile_rows((2 * block + k) * (owners + 1) + source), :] = held[k]

    if owners <= 8:
        def blocks_of(sources, blocks):
            for block in blocks:
                for source in sources:
                    one_source(source, 1 if source == 2 else LANES, [block])

        full = [1, owners]
        others = [source for source in range(owners) if source not in full]

        @pl.when(codes[owners + 1, 0] > LANES // 2)
        def _():
            blocks_of(others, (2, 3))

        blocks_of(others + full, (0, 1))
        blocks_of(full, (2, 3))
    else:
        each_source(owners, one_source)

    def one_block(block, last):
        for s in range(8):
            tiles = [
                picked[pl.ds((g * (owners + 1) + block * ROWS) * 8 + s, ROWS, stride=8), :]
                for g in range(8)
            ]
            for x, tile in enumerate(separated(tiles, lane)):
                parts[s, x] = tile
        if last:
            tiles = [picked[pl.ds((g * (owners + 1) + owners) * 8, 8), :] for g in range(8)]
            for x, tile in enumerate(separated(tiles, lane)):
                parts[8, x] = tile

        def corner(q, variable):
            a0, a1, a2 = q >> 2, (q >> 1) & 1, q & 1
            s, x = 4 * a0 + 2 * a2 + (variable >> 2), 2 * (variable & 3) + a1
            tile = parts[s, x]
            if last:
                more = jnp.broadcast_to(parts[8, x, s : s + 1, :], (ROWS, LANES))
                tile = jnp.concatenate([tile, more], 0)
            return tile

        target = []
        for c in range(3):
            tile = message[pl.ds(block * (ROWS * 8) + 1 + c, ROWS, stride=8), :]
            if last:
                more = message[13 + c : 14 + c, :]
                tile = jnp.concatenate([tile, jnp.broadcast_to(more, (ROWS, LANES))], 0)
            target.append(tile)
        values = solve(corner, target)
        for variable in range(5):
            answers[pl.ds(variable, ROWS, stride=8), :] = values[variable][:ROWS]
            if last:
                place = pl.ds(of_source(1) * 16 + 8 + variable, 1)
                out_ref[place, :] = values[variable][ROWS : ROWS + 1]
        for distance in range(ROWS):
            source = of_source(block * ROWS + distance)
            out_ref[tile_rows(2 * source), :] = answers[tile_rows(distance), :]

    for block in range(owners // ROWS):
        one_block(block, block == owners // ROWS - 1)


def relax_kernel(
    owners, code_ref, field_ref, next_ref, below_ref, ratio_ref, values_ref, out_ref,
    table, codes, rolled, plain, inverse, out_vmem, sem, out_sem,
):
    variables, planes, rows_count, _ = out_ref.shape
    width = 8
    blocks = rows_count // ROWS
    plane_rows = rows_count * width
    needed = pl.ds(0, 2 * owners + 2)
    copy = pltpu.make_async_copy(code_ref.at[needed], codes.at[needed], sem)
    copy.start()
    lane = lax.broadcasted_iota(jnp.int32, (ROWS, LANES), 1)
    sublane = lax.broadcasted_iota(jnp.int32, (ROWS, LANES), 0)
    me = lax.axis_index("grid")

    def lay_out_rows():
        for plane in range(planes):
            for variable in range(variables + 1):
                tile = jnp.zeros((rows_count, LANES), jnp.float32)
                if variable < variables:
                    tile = field_ref[variable, plane]
                first = plane * plane_rows + variable
                table[pl.ds(first, rows_count, stride=width), :] = tile
            inverse[plane] = 1.0 / (1.0 + 6.0 * ratio_ref[plane])

    lane_id = lane.astype(jnp.float32)

    def values_of(distance):
        if isinstance(distance, int):
            owner = lax.rem(me + distance % owners + distance // owners, owners)
            first = owner * 16 + 8 * (distance // owners)
        else:
            more = distance == owners
            owner = lax.rem(jnp.where(more, me + 1, me + distance), owners)
            first = owner * 16 + jnp.where(more, 8, 0)
        tile = values_ref[pl.ds(pl.multiple_of(first, 8), 8), :]
        return jnp.where(sublane == variables, 1.0, tile)

    def spread(distances):
        tiles = []
        for distance in distances:
            column = (code_ref[pl.ds(owners + 1 + distance, 1), :] + lane[:1]) & (LANES - 1)
            column = column.astype(jnp.float32)
            tiles.append(jnp.where(sublane == variables + 1, column, values_of(distance)))
        for point in range(LANES):
            for distance, tile in zip(distances, tiles):
                rolled[tile_rows(distance * LANES + point), :] = jnp.broadcast_to(
                    tile[:, point : point + 1], (ROWS, LANES)
                )

    def rotate(distance, points, buffer):
        tile = values_of(distance)
        tile = jnp.where(sublane == variables + 1, lane.astype(jnp.float32), tile)
        for point in range(points):
            place = tile_rows(buffer * LANES + point)
            rolled[place, :] = pltpu.roll(tile, codes[owners + 1 + distance, point], 1)

    def store(distance, points, buffer):
        for point in range(points):
            place = (buffer * LANES + point) * ROWS
            tag = rolled[place + variables + 1 : place + variables + 2, :]
            row = pl.multiple_of(codes[distance, point], width)
            tag = jnp.broadcast_to(tag, (ROWS, LANES))
            early = isinstance(distance, int) and distance in EARLY
            pltpu.store(
                table.at[pl.ds(row, width), :],
                rolled[place : place + ROWS, :],
                mask=tag == (lane_id if early else float(point)),
            )

    if owners <= 8:
        todo = []
        each_source(owners, lambda distance, points: todo.append((distance, points, distance)))

        def meanwhile():
            lay_out_rows()
            spread(EARLY)

        after(me, meanwhile)
        copy.wait()
        late = [item for item in todo if item[0] not in EARLY]
        rotate(*late[0])
        for distance in EARLY:
            store(distance, LANES, distance)
        for now, later in zip(late, late[1:] + [None]):
            if later is not None:
                rotate(*later)
            store(*now)
    else:

        after(me, lay_out_rows)
        copy.wait()

        def one_source(distance, points):
            rotate(distance, points, 0)
            store(distance, points, 0)

        each_source(owners, one_source)

    def out_copy(plane):
        return pltpu.make_async_copy(
            out_vmem.at[:, pl.ds(plane, 1)], out_ref.at[:, pl.ds(plane, 1)], out_sem.at[plane]
        )

    def place(plane, block, variable, step=0):
        return pl.ds(ROWS + (variable * planes + plane) * rows_count + block * ROWS + step, ROWS)

    def flat(plane):
        for block in range(blocks):
            for variable in range(variables):
                first = plane * plane_rows + block * ROWS * width + variable
                plain[place(plane, block, variable), :] = table[pl.ds(first, ROWS, stride=width), :]

    def one_plane(plane):
        for block in range(blocks):
            rows = pl.ds(block * ROWS, ROWS)
            ratio, divisor = ratio_ref[plane, rows, :], inverse[plane, rows, :]
            first = plane * plane_rows + block * ROWS * width + variables
            fringe = table[pl.ds(first, ROWS, stride=width), :] > 0.5
            for variable in range(variables):
                here = plain[place(plane, block, variable), :]
                up = plain[place(plane, block, variable, 1), :]
                down = plain[place(plane, block, variable, -1), :]
                if block == 0:
                    down = jnp.where(sublane == 0, 0.0, down)
                if block == blocks - 1:
                    up = jnp.where(sublane == ROWS - 1, 0.0, up)
                right = jnp.where(lane == LANES - 1, 0.0, pltpu.roll(here, LANES - 1, 1))
                left = jnp.where(lane == 0, 0.0, pltpu.roll(here, 1, 1))
                if plane == 0:
                    below = below_ref[variable, 0, rows, :]
                else:
                    below = plain[place(plane - 1, block, variable), :]
                if plane == planes - 1:
                    above = next_ref[3 + variable, 0, rows, :]
                else:
                    above = plain[place(plane + 1, block, variable), :]
                total = (above + below) + (up + down) + (right + left)
                smooth = (here + ratio * total) * divisor
                out_vmem[variable, plane, rows, :] = jnp.where(fringe, here, smooth)
        out_copy(plane).start()

    flat(0)
    for plane in range(planes):
        if plane < planes - 1:
            flat(plane + 1)
        one_plane(plane)
    for plane in range(planes):
        out_copy(plane).wait()


def on_device(
    field, node_jitter, time_ratio, donor_cell, receptor_offset, receptor_node, point_count
):
    variables, planes, rows_count, cols_count = field.shape
    owners, points = donor_cell.shape[1], donor_cell.shape[3]
    params = pltpu.CompilerParams(vmem_limit_bytes=LIMIT)
    offsets = jnp.swapaxes(receptor_offset, 2, 3)
    f32, i32 = jnp.float32, jnp.int32
    message, codes, first, last = pl.pallas_call(
        first_kernel,
        out_shape=[
            jax.ShapeDtypeStruct((owners, 8, LANES), f32),
            jax.ShapeDtypeStruct((2 * owners + 8, LANES), i32),
            jax.ShapeDtypeStruct((3 + variables, 1, rows_count, cols_count), f32),
            jax.ShapeDtypeStruct((variables, 1, rows_count, cols_count), f32),
        ],
        in_specs=[HBM] * 6,
        out_specs=[VMEM] * 4,
        scratch_shapes=[
            pltpu.SMEM(point_count.shape, i32),
            pltpu.VMEM(donor_cell.shape, i32),
            pltpu.VMEM(offsets.shape, f32),
            pltpu.VMEM(receptor_node.shape, i32),
            pltpu.SemaphoreType.DMA((7,)),
        ],
        compiler_params=params,
        name="first",
    )(*[
        pltpu.with_memory_space_constraint(x, pltpu.HBM)
        for x in (point_count, donor_cell, offsets, receptor_node, field, node_jitter)
    ])
    following = passed_along(first, "sub", -1)
    below = passed_along(last, "sub", 1)
    message = lax.all_to_all(message, "grid", split_axis=0, concat_axis=0, tiled=True)
    values = pl.pallas_call(
        functools.partial(gather_kernel, owners),
        out_shape=jax.ShapeDtypeStruct((owners * 16, LANES), f32),
        in_specs=[VMEM] * 5,
        out_specs=VMEM,
        scratch_shapes=[
            pltpu.VMEM(((planes + 1) * cols_count * 2, LANES), f32),
            pltpu.VMEM((owners * 8, LANES), f32),
            pltpu.VMEM((owners + 8, LANES), i32),
            pltpu.SMEM((owners + 8, LANES), i32),
            pltpu.VMEM((8 * (owners + 1) * 8, LANES), f32),
            pltpu.VMEM((9, 8, ROWS, LANES), f32),
            pltpu.VMEM((ROWS * 8, LANES), f32),
            pltpu.SemaphoreType.DMA,
        ],
        compiler_params=params,
        name="gather",
    )(field, node_jitter, following, below, message.reshape(owners * 8, LANES))
    values = values.reshape(owners, 16, LANES)
    values = lax.all_to_all(values, "grid", split_axis=0, concat_axis=0, tiled=True)
    return pl.pallas_call(
        functools.partial(relax_kernel, owners),
        out_shape=jax.ShapeDtypeStruct(field.shape, f32),
        in_specs=[VMEM] * 6,
        out_specs=HBM,
        scratch_shapes=[
            pltpu.VMEM((planes * rows_count * 8 + 8, LANES), f32),
            pltpu.SMEM(codes.shape, i32),
            pltpu.VMEM(((owners + 1 if owners <= 8 else 1) * LANES * ROWS, LANES), f32),
            pltpu.VMEM((variables * planes * rows_count + 2 * ROWS, LANES), f32),
            pltpu.VMEM(time_ratio.shape, f32),
            pltpu.VMEM(field.shape, f32),
            pltpu.SemaphoreType.DMA,
            pltpu.SemaphoreType.DMA((planes,)),
        ],
        compiler_params=params,
        name="relax",
    )(codes, field, following, below, time_ratio, values.reshape(owners * 16, LANES))


def solution(mesh):
    placed = (
        P(None, ("grid", "sub"), None, None),
        P(None, ("grid", "sub"), None, None),
        P(("grid", "sub"), None, None),
        P(("grid", "sub"), None, None, None),
        P(("grid", "sub"), None, None, None, None),
        P(("grid", "sub"), None, None, None),
        P(("grid", "sub"), None),
    )
    return jax.shard_map(
        on_device,
        mesh=mesh,
        in_specs=placed,
        out_specs=P(None, ("grid", "sub"), None, None),
        check_vma=False,
    )
```
